32 devices in a mesh: batch: 16 (over z, x, core), head: 2 (over y).
Axes of the slice: x: 2, y: 2, z: 4, core: 2. Of those that a mesh axis runs over, the one named last changes fastest.
Arguments:
- clip_in: bfloat16 [16, 6272, 192], P('batch', 'head'), may hold values from -6 to 6
- frame_count: int32 [16], P('batch'), may hold values from 2 to 8, as said below
- frame_mask: int32 [16, 8], P('batch'), may hold values from 0 to 1, as said below
- pool_index: int32 [16, 1568], P('batch'), may hold values from 0 to 3
- first_norm_gain: float32 [192], replicated, may hold values from 0.25 to 1.75
- first_norm_bias: float32 [192], replicated, may hold values from -1.75 to 1.75
- first_widen_weight: bfloat16 [192, 384], replicated, may hold values from -0.4375 to 0.4375
- first_widen_bias: float32 [384], replicated, may hold values from -1.75 to 1.75
- first_qkv_weight: bfloat16 [192, 3, 384], P(None, None, 'head'), may hold values from -0.4375 to 0.4375
- first_qv_bias: float32 [2, 384], P(None, 'head'), may hold values from -1.75 to 1.75
- first_out_weight: bfloat16 [384, 384], P('head'), may hold values from -6 to 6
- first_out_bias: float32 [384], replicated, may hold values from -1.75 to 1.75
- first_mlp_gain: float32 [384], replicated, may hold values from 0.25 to 1.75
- first_mlp_bias: float32 [384], replicated, may hold values from -1.75 to 1.75
- first_up_weight: bfloat16 [384, 1536], P(None, 'head'), may hold values from -0.3125 to 0.3125
- first_up_bias: float32 [1536], P('head'), may hold values from -1.75 to 1.75
- first_down_weight: bfloat16 [1536, 384], P('head'), may hold values from -0.15625 to 0.15625
- first_down_bias: float32 [384], replicated, may hold values from -1.75 to 1.75
- second_norm_gain: float32 [384], replicated, may hold values from 0.25 to 1.75
- second_norm_bias: float32 [384], replicated, may hold values from -1.75 to 1.75
- second_qkv_weight: bfloat16 [384, 3, 384], P(None, None, 'head'), may hold values from -0.3125 to 0.3125
- second_qv_bias: float32 [2, 384], P(None, 'head'), may hold values from -1.75 to 1.75
- second_out_weight: bfloat16 [384, 384], P('head'), may hold values from -6 to 6
- second_out_bias: float32 [384], replicated, may hold values from -1.75 to 1.75
- second_mlp_gain: float32 [384], replicated, may hold values from 0.25 to 1.75
- second_mlp_bias: float32 [384], replicated, may hold values from -1.75 to 1.75
- second_up_weight: bfloat16 [384, 1536], P(None, 'head'), may hold values from -0.3125 to 0.3125
- second_up_bias: float32 [1536], P('head'), may hold values from -1.75 to 1.75
- second_down_weight: bfloat16 [1536, 384], P('head'), may hold values from -0.15625 to 0.15625
- second_down_bias: float32 [384], replicated, may hold values from -1.75 to 1.75
- cotangent: bfloat16 [16, 1568, 384], P('batch', 'head'), may hold values from -6 to 6
Outputs:
- layer_output: bfloat16 [16, 1568, 384], P('batch', 'head')
- input_gradient: float32 [16, 6272, 192], P('batch', 'head')
- grad_first_norm_gain: float32 [192], replicated
- grad_first_norm_bias: float32 [192], replicated
- grad_first_widen_weight: float32 [192, 384], replicated
- grad_first_widen_bias: float32 [384], replicated
- grad_first_qkv_weight: float32 [192, 3, 384], P(None, None, 'head')
- grad_first_qv_bias: float32 [2, 384], P(None, 'head')
- grad_first_out_weight: float32 [384, 384], P('head')
- grad_first_out_bias: float32 [384], replicated
- grad_first_mlp_gain: float32 [384], replicated
- grad_first_mlp_bias: float32 [384], replicated
- grad_first_up_weight: float32 [384, 1536], P(None, 'head')
- grad_first_up_bias: float32 [1536], P('head')
- grad_first_down_weight: float32 [1536, 384], P('head')
- grad_first_down_bias: float32 [384], replicated
- grad_second_norm_gain: float32 [384], replicated
- grad_second_norm_bias: float32 [384], replicated
- grad_second_qkv_weight: float32 [384, 3, 384], P(None, None, 'head')
- grad_second_qv_bias: float32 [2, 384], P(None, 'head')
- grad_second_out_weight: float32 [384, 384], P('head')
- grad_second_out_bias: float32 [384], replicated
- grad_second_mlp_gain: float32 [384], replicated
- grad_second_mlp_bias: float32 [384], replicated
- grad_second_up_weight: float32 [384, 1536], P(None, 'head')
- grad_second_up_bias: float32 [1536], P('head')
- grad_second_down_weight: float32 [1536, 384], P('head')
- grad_second_down_bias: float32 [384], replicated
The draws below stay inside these ranges and needn't reach their ends.
Inputs may be any that keep to these rules, and one draw needn't show every extreme that they name: `frame_count`: at least one clip has all 8 frames. `frame_mask`: frame 0 of every clip is marked 1, and so is every frame of some clip that has all 8 frames.
All inputs are finite; a program needn't handle non-finite values.
Results may differ from the reference program's by a relative error of at most 0.013.
Values may be sent and summed in bfloat16 or wider, within the bound.
No kernel may reach another device: no remote copies, remote signals or barrier semaphores. Data moves between devices by JAX's collectives and lax.ppermute only.
A program may use at most 256 MiB of HBM per device.

```python
import jax
import jax.numpy as jnp
from jax import lax

C_IN = 192
DIM = 384
HEADS = 4
HIDDEN_SIZE = 1536
HEAD_DIM = 96
FRAMES = 8
SIDE = 14
QBLOCK = 784
CLIPS = 16
TOK = 1568
TOK_IN = 6272


def full_clip(key):
    return jax.random.randint(jax.random.fold_in(key, 5), (), 0, CLIPS)


def draw_frame_count(key, part):
    chosen = full_clip(key)
    key = jax.random.fold_in(key, 11)
    counts = jax.random.randint(key, (CLIPS,), 2, FRAMES + 1)
    return jnp.where(jnp.arange(CLIPS) == chosen, FRAMES, counts).astype(jnp.int32)


def draw_frame_mask(key, part):
    chosen = full_clip(key)
    key = jax.random.fold_in(key, 12)
    marks = jax.random.randint(key, (CLIPS, FRAMES), 0, 4) > 0
    marks = marks | (jnp.arange(FRAMES)[None, :] == 0) | (jnp.arange(CLIPS)[:, None] == chosen)
    return marks.astype(jnp.int32)


def plant(values, stream_key, smallest, high):
    longest = values.shape.index(max(values.shape))
    spots = []
    for shift in (0, 1):
        where = [jax.random.randint(jax.random.fold_in(stream_key, axis), (), 0, length) for axis, length in enumerate(values.shape)]
        where[longest] = (where[longest] + shift) % values.shape[longest]
        spots.append(tuple(where))
    return values.at[spots[0]].set(smallest).at[spots[1]].set(high)


def block_levels(rng, dims, cuts, low, largest):
    def one(dim, shards_of):
        heights = jax.random.uniform(jax.random.fold_in(jax.random.fold_in(rng, 6), dim), (shards_of,), jnp.float32, low / len(cuts), largest / len(cuts))
        return jnp.repeat(jnp.exp(heights), dims[dim] // shards_of).reshape((-1,) + (1,) * (len(dims) - dim - 1))

    loudness = one(*cuts[0])
    for cut in cuts[1:]:
        loudness = loudness * one(*cut)
    return loudness


def noise(stream_key, extent, scale, limit, shards=(), kind=jnp.bfloat16):
    entries = jax.random.normal(stream_key, extent, jnp.float32) * scale
    if len(shards) > 0:
        entries = block_levels(stream_key, extent, shards, -0.22, 0.18) * entries
    return jnp.clip(entries, min=-limit, max=limit).astype(kind)


def setup_inputs(seed: int = 0) -> dict:
    key_list = jax.random.split(jax.random.key(seed), 32)
    return {
        "clip_in": noise(key_list[0], (CLIPS, TOK_IN, C_IN), 1.0, 6.0, ((0, 16), (1, 2))),
        "frame_count": draw_frame_count(jax.random.fold_in(key_list[31], 71), 0),
        "frame_mask": draw_frame_mask(jax.random.fold_in(key_list[31], 71), 0),
        "pool_index": plant(jax.random.randint(key_list[3], (CLIPS, TOK), 0, 4), jax.random.fold_in(key_list[3], 1), 0, 3).astype(jnp.int32),
        "first_norm_gain": jnp.clip(1.0 + 0.15 * jax.random.normal(key_list[4], (C_IN,), jnp.float32), 0.25, 1.75),
        "first_norm_bias": noise(key_list[5], (C_IN,), 0.3, 1.75, (), jnp.float32),
        "first_widen_weight": noise(key_list[6], (C_IN, DIM), C_IN ** -0.5, 0.4375),
        "first_widen_bias": noise(key_list[7], (DIM,), 0.3, 1.75, (), jnp.float32),
        "first_qkv_weight": noise(key_list[8], (C_IN, 3, DIM), C_IN ** -0.5, 0.4375, ((2, 2),)),
        "first_qv_bias": noise(key_list[9], (2, DIM), 0.3, 1.75, ((1, 2),), jnp.float32),
        "first_out_weight": noise(key_list[10], (DIM, DIM), 1.5, 6.0, ((0, 2),)),
        "first_out_bias": noise(key_list[11], (DIM,), 0.3, 1.75, (), jnp.float32),
        "first_mlp_gain": jnp.clip(1.0 + 0.15 * jax.random.normal(key_list[12], (DIM,), jnp.float32), 0.25, 1.75),
        "first_mlp_bias": noise(key_list[13], (DIM,), 0.3, 1.75, (), jnp.float32),
        "first_up_weight": noise(key_list[14], (DIM, HIDDEN_SIZE), DIM ** -0.5, 0.3125, ((1, 2),)),
        "first_up_bias": noise(key_list[15], (HIDDEN_SIZE,), 0.3, 1.75, ((0, 2),), jnp.float32),
        "first_down_weight": noise(key_list[16], (HIDDEN_SIZE, DIM), HIDDEN_SIZE ** -0.5, 0.15625, ((0, 2),)),
        "first_down_bias": noise(key_list[17], (DIM,), 0.3, 1.75, (), jnp.float32),
        "second_norm_gain": jnp.clip(1.0 + 0.15 * jax.random.normal(key_list[18], (DIM,), jnp.float32), 0.25, 1.75),
        "second_norm_bias": noise(key_list[19], (DIM,), 0.3, 1.75, (), jnp.float32),
        "second_qkv_weight": noise(key_list[20], (DIM, 3, DIM), DIM ** -0.5, 0.3125, ((2, 2),)),
        "second_qv_bias": noise(key_list[21], (2, DIM), 0.3, 1.75, ((1, 2),), jnp.float32),
        "second_out_weight": noise(key_list[22], (DIM, DIM), 0.8, 6.0, ((0, 2),)),
        "second_out_bias": noise(key_list[23], (DIM,), 0.3, 1.75, (), jnp.float32),
        "second_mlp_gain": jnp.clip(1.0 + 0.15 * jax.random.normal(key_list[24], (DIM,), jnp.float32), 0.25, 1.75),
        "second_mlp_bias": noise(key_list[25], (DIM,), 0.3, 1.75, (), jnp.float32),
        "second_up_weight": noise(key_list[26], (DIM, HIDDEN_SIZE), DIM ** -0.5, 0.3125, ((1, 2),)),
        "second_up_bias": noise(key_list[27], (HIDDEN_SIZE,), 0.3, 1.75, ((0, 2),), jnp.float32),
        "second_down_weight": noise(key_list[28], (HIDDEN_SIZE, DIM), HIDDEN_SIZE ** -0.5, 0.15625, ((0, 2),)),
        "second_down_bias": noise(key_list[29], (DIM,), 0.3, 1.75, (), jnp.float32),
        "cotangent": noise(key_list[30], (CLIPS, TOK, DIM), 1.0, 6.0, ((0, 16), (1, 2))),
    }


eps_norm = 1e-06
highest = lax.Precision.HIGHEST

@jax.custom_vjp
def low(v):
    return lax.optimization_barrier(v.astype(jnp.bfloat16)).astype(jnp.float32)

@jax.custom_vjp
def low_back(v):
    return v

def low_keep(v):
    return (low(v), None)

def low_pass(kept, grad):
    return (grad,)

def back_keep(v):
    return (v, None)

def back_low(kept, grad):
    return (low(grad),)
low.defvjp(low_keep, low_pass)
low_back.defvjp(back_keep, back_low)

def rounded_both(tensor):
    return low_back(low(tensor))

def layer_norm(residual, norm_gain, norm_shift):
    centered = residual - lax.optimization_barrier(jnp.mean(residual, axis=-1, keepdims=True))
    spread = lax.optimization_barrier(jnp.mean(centered * centered, axis=-1, keepdims=True))
    return centered * lax.rsqrt(spread + eps_norm) * norm_gain + norm_shift

def window_weights(pool_picks):
    leading = pool_picks.shape[:-1]
    frames = pool_picks.shape[-1] // (SIDE * SIDE)
    onehot = (pool_picks[..., None] == jnp.arange(4, dtype=jnp.int32)).astype(jnp.float32)
    onehot = onehot.reshape(leading + (frames, SIDE, SIDE, 2, 2))
    return jnp.swapaxes(onehot, -3, -2)[..., None]

def pool_rows(tensor, onehot):
    leading = onehot.shape[:-6]
    frames = onehot.shape[-6]
    features = tensor.shape[-1]
    blocks = tensor.reshape(leading + (frames, SIDE, 2, SIDE, 2, features))
    return lax.optimization_barrier(jnp.sum(blocks * onehot, axis=(-4, -2))).reshape(leading + (frames * SIDE * SIDE, features))

def attention(query_rows, key_rows, value_rows, live_keys):
    queries = query_rows.shape[0]
    query_blocks = query_rows.reshape(queries // QBLOCK, QBLOCK, HEADS, HEAD_DIM)
    key_heads = key_rows.reshape(-1, HEADS, HEAD_DIM)
    value_heads = value_rows.reshape(-1, HEADS, HEAD_DIM)

    def one_block(query_block):
        scores = jnp.einsum('qhd,khd->hqk', query_block, key_heads, precision=highest) * HEAD_DIM ** (-0.5)
        scores = low_back(scores)
        scores = jnp.where(live_keys[None, None, :], scores, -1e+30)
        softmaxed = low(jax.nn.softmax(scores, axis=-1))
        return jnp.einsum('hqk,khd->qhd', softmaxed, value_heads, precision=highest)
    attended = lax.map(jax.checkpoint(one_block), query_blocks)
    return attended.reshape(queries, HEADS * HEAD_DIM)

def layer(residual, params, frame_live, onehot, widening):
    if widening:
        norm_gain, norm_shift, widen_weight, widen_bias, qkv_weight, qv_bias, out_weight, out_bias, mlp_gain, mlp_shift, up_weight, up_bias, down_weight, down_bias = params
    else:
        norm_gain, norm_shift, qkv_weight, qv_bias, out_weight, out_bias, mlp_gain, mlp_shift, up_weight, up_bias, down_weight, down_bias = params
    normed = low(layer_norm(residual, norm_gain, norm_shift))
    projected = jnp.einsum('tc,cjd->tjd', normed, qkv_weight, precision=highest)
    query_rows = projected[:, 0] + qv_bias[0]
    if widening:
        query_rows = pool_rows(query_rows, onehot)
    query_rows = rounded_both(query_rows)
    key_rows = rounded_both(projected[:, 1])
    value_rows = rounded_both(projected[:, 2] + qv_bias[1])
    live_keys = jnp.repeat(frame_live, key_rows.shape[0] // FRAMES)
    attended = rounded_both(attention(query_rows, key_rows, value_rows, live_keys))
    branch = low_back(jnp.dot(attended, out_weight, precision=highest)) + out_bias
    if widening:
        widened = low_back(jnp.dot(normed, widen_weight, precision=highest)) + widen_bias
        middle = pool_rows(widened, onehot) + branch
    else:
        middle = residual + branch
    normed_mid = low(layer_norm(middle, mlp_gain, mlp_shift))
    hidden = low_back(jnp.dot(normed_mid, up_weight, precision=highest) + up_bias)
    active = low(jax.nn.gelu(hidden, approximate=False))
    return middle + low_back(jnp.dot(active, down_weight, precision=highest)) + down_bias

def clip_forward(first, second, residual, clip_count, clip_mask, pool_picks):
    frame_live = (jnp.arange(FRAMES, dtype=jnp.int32) < clip_count) & (clip_mask == 1)
    onehot = window_weights(pool_picks)
    middle = layer(residual, first, frame_live, onehot, True)
    return layer(middle, second, frame_live, None, False)

def reference(clip_in, frame_count, frame_mask, pool_index, first_norm_gain, first_norm_bias, first_widen_weight, first_widen_bias, first_qkv_weight, first_qv_bias, first_out_weight, first_out_bias, first_mlp_gain, first_mlp_bias, first_up_weight, first_up_bias, first_down_weight, first_down_bias, second_norm_gain, second_norm_bias, second_qkv_weight, second_qv_bias, second_out_weight, second_out_bias, second_mlp_gain, second_mlp_bias, second_up_weight, second_up_bias, second_down_weight, second_down_bias, cotangent):
    first = tuple((tensor.astype(jnp.float32) for tensor in (first_norm_gain, first_norm_bias, first_widen_weight, first_widen_bias, first_qkv_weight, first_qv_bias, first_out_weight, first_out_bias, first_mlp_gain, first_mlp_bias, first_up_weight, first_up_bias, first_down_weight, first_down_bias)))
    second = tuple((tensor.astype(jnp.float32) for tensor in (second_norm_gain, second_norm_bias, second_qkv_weight, second_qv_bias, second_out_weight, second_out_bias, second_mlp_gain, second_mlp_bias, second_up_weight, second_up_bias, second_down_weight, second_down_bias)))
    clips_float = clip_in.astype(jnp.float32)
    checked = jax.checkpoint(clip_forward)

    def forward(first_params, second_params, clips):

        def clip_step(carried, pieces):
            residual, clip_count, clip_mask, pool_picks = pieces
            return (carried, checked(first_params, second_params, residual, clip_count, clip_mask, pool_picks))
        return lax.scan(clip_step, None, (clips, frame_count, frame_mask, pool_index))[1]
    output, pull = jax.vjp(forward, first, second, clips_float)
    grad_first, grad_second, grad_clips = pull(cotangent.astype(jnp.float32))
    return (output.astype(jnp.bfloat16), grad_clips, grad_first[0], grad_first[1], grad_first[2], grad_first[3], grad_first[4], grad_first[5], grad_first[6], grad_first[7], grad_first[8], grad_first[9], grad_first[10], grad_first[11], grad_first[12], grad_first[13], grad_second[0], grad_second[1], grad_second[2], grad_second[3], grad_second[4], grad_second[5], grad_second[6], grad_second[7], grad_second[8], grad_second[9], grad_second[10], grad_second[11])
```

```python
import functools

import jax
import jax.numpy as jnp
from jax import lax
from jax.experimental import pallas as pl
from jax.experimental.pallas import tpu as pltpu
from jax.sharding import Mesh, PartitionSpec as P

HEAD_DIM = 96
WIDE = 128
SIDE = 14
DEAD = -1e30
LOG2E = 1.4426950408889634
LN2 = 0.6931471805599453
SCALE = HEAD_DIM ** (-0.5)
EPS = 1e-06
CHUNK = 512
SAFE = 60.0
BATCH = ("outer", "core")

bf16 = jnp.bfloat16
f32 = jnp.float32


def dot(a, b):
    return jnp.dot(a, b, preferred_element_type=f32)


def dot_nt(a, b):
    return lax.dot_general(a, b, (((1,), (1,)), ((), ())), preferred_element_type=f32)


def flip(a):
    return a.astype(f32).T


def chunks(total):
    return [(start, min(CHUNK, total - start)) for start in range(0, total, CHUNK)]


def norm_stats(v):
    centered = v - jnp.mean(v, axis=-1, keepdims=True)
    rstd = lax.rsqrt(jnp.mean(centered * centered, axis=-1, keepdims=True) + EPS)
    return centered * rstd, rstd


def norm_back(xhat, rstd, gain, grad):
    scaled = grad * gain
    back = rstd * (
        scaled
        - jnp.mean(scaled, axis=-1, keepdims=True)
        - xhat * jnp.mean(scaled * xhat, axis=-1, keepdims=True)
    )
    return (
        back,
        jnp.sum(grad * xhat, axis=0, keepdims=True),
        jnp.sum(grad, axis=0, keepdims=True),
    )


def three_parts(v):
    high = v.astype(bf16).astype(f32)
    rest = v - high
    middle = rest.astype(bf16).astype(f32)
    return high, middle, rest - middle


def with_columns(block, first, column):
    lane = lax.broadcasted_iota(jnp.int32, block.shape, 1)
    for offset, part in enumerate(three_parts(column)):
        block = jnp.where(lane == first + offset, part, block)
    return block


def gelu_both(u):
    cdf = 0.5 + 0.5 * lax.erf(u * 0.7071067811865476)
    return u * cdf, cdf + u * (jnp.exp(-0.5 * u * u) * 0.3989422804014327)


NORM1, WIDEN_B, OUT_B1, MLP1, DOWN_B1, NORM2, OUT_B2, MLP2, DOWN_B2 = 0, 2, 3, 4, 6, 7, 9, 10, 12
SMEM = "smem"


def call(body, grid, ins, outs, scratch, micros, offset=0, megabytes=56):
    def spec(shape, block):
        if block == SMEM:
            return pl.BlockSpec(memory_space=pltpu.SMEM)
        if block is None:
            zeros = (0,) * len(shape)
            return pl.BlockSpec(tuple(shape), lambda *_: zeros)
        if block[0] == "own":
            rest = (0,) * (len(shape) - 1)
            return pl.BlockSpec(tuple(block[1:]), lambda i, *_: (i,) + rest)
        if block[0] == "half":
            rest = (0,) * (len(shape) - 1)
            return pl.BlockSpec(tuple(block[1:]), lambda i, *_: ((i + offset) // 2,) + rest)
        rest = (0,) * (len(shape) - 1)
        return pl.BlockSpec(tuple(block), lambda i, *_: (i + offset,) + rest)

    def out_spec(shape, block):
        if block is None or block[0] == "half":
            return spec(shape, block)
        rest = (0,) * (len(shape) - 1)
        return pl.BlockSpec(tuple(block), lambda i, *_: (i,) + rest)

    return pl.pallas_call(
        body,
        grid=grid,
        in_specs=[spec(a.shape, b) for a, b in ins],
        out_specs=[out_spec(s, b) for s, _, b in outs],
        out_shape=[jax.ShapeDtypeStruct(s, d) for s, d, _ in outs],
        scratch_shapes=scratch,
        cost_estimate=pl.CostEstimate(
            flops=int(micros * 1.15e9), transcendentals=0, bytes_accessed=int(micros * 3.69e6)
        ),
        compiler_params=pltpu.CompilerParams(
            dimension_semantics=("arbitrary",) * len(grid),
            vmem_limit_bytes=megabytes << 20,
        ),
    )(*[a for a, _ in ins])


def full(*arrays):
    return [(a, None) for a in arrays]


def dead_keys(spot, count, marks, keys, far):
    half = marks.shape[1] // 2
    each = keys // half
    first = (1 - spot[0] if far else spot[0]) * half
    lane = lax.broadcasted_iota(jnp.int32, (1, keys), 1)
    row = jnp.zeros((1, keys), f32)
    for f in range(half):
        dead = (first + f >= count[0]) | (marks[0, first + f] != 1)
        row = jnp.where((lane >= f * each) & (lane < (f + 1) * each), jnp.where(dead, DEAD, 0.0), row)
    return row


def head_forms(spot, w_own, w_far, pack_own, pack_far, layer, w_out, b_out):
    first = spot[1] == 0
    w_out[...] = jnp.zeros_like(w_out)
    b_out[...] = jnp.zeros_like(b_out)
    for side, (w, pack) in enumerate(((w_own, pack_own), (w_far, pack_far))):
        for j in range(3):
            low = w[j, :, :HEAD_DIM].astype(f32)
            high = w[j, :, HEAD_DIM:].astype(f32)
            lanes = slice(j * WIDE, j * WIDE + HEAD_DIM)
            w_out[2 * side, :, lanes] = jnp.where(first, low, high).astype(bf16)
            w_out[2 * side + 1, :, lanes] = jnp.where(first, high, low).astype(bf16)
        for j in range(2):
            start = (2 * layer + j) * 2 * HEAD_DIM
            low = pack[2:3, start : start + HEAD_DIM]
            high = pack[2:3, start + HEAD_DIM : start + 2 * HEAD_DIM]
            b_out[2 * side, j : j + 1, :HEAD_DIM] = jnp.where(first, low, high)
            b_out[2 * side + 1, j : j + 1, :HEAD_DIM] = jnp.where(first, high, low)


def project_keys(x_t, w, b, mask, kt_out, vt_out):
    both = dot(flip(w[:, WIDE:]).astype(bf16), x_t)
    k_t, v_t = both[:WIDE], both[WIDE:]
    key_bound = jnp.max(jnp.sum(k_t * k_t, axis=0, keepdims=True))
    row = lax.broadcasted_iota(jnp.int32, k_t.shape, 0)
    k_t = jnp.where(row == HEAD_DIM, mask, k_t)
    k_t = jnp.where((row > HEAD_DIM) & (row < HEAD_DIM + 4), 1.0, k_t)
    kt_out[0] = k_t.astype(bf16)
    column = jnp.broadcast_to(b[1:2], (WIDE, WIDE)).T[:, :1]
    row = lax.broadcasted_iota(jnp.int32, column.shape, 0)
    column = jnp.where((row >= HEAD_DIM) & (row < HEAD_DIM + 3), 1.0, column)
    vt_out[0] = (v_t + column).astype(bf16)
    return key_bound


def soft_part(q, key_bound, kt_ref, vt_ref, s_ref, o_ref, m_ref):
    total = kt_ref.shape[2]
    q_wide = q.astype(f32)
    bound = jnp.max(jnp.sum(q_wide * q_wide, axis=1, keepdims=True)) * key_bound
    safe = bound < SAFE * SAFE

    @pl.when(safe)
    def _():
        out = None
        for start, size in chunks(total):
            part = slice(start, start + size)
            p = jnp.exp2(dot(q, kt_ref[0, :, part])).astype(bf16)
            o = dot_nt(p, vt_ref[0, :, part])
            out = o if out is None else out + o
        o_ref[0] = out
        m_ref[0] = jnp.zeros_like(m_ref[0])

    @pl.when(jnp.logical_not(safe))
    def _():
        peak = None
        for start, size in chunks(total):
            s = dot(q, kt_ref[0, :, start : start + size])
            s_ref[:, start : start + size] = s
            top = jnp.max(s, axis=1, keepdims=True)
            peak = top if peak is None else jnp.maximum(peak, top)
        out = None
        for start, size in chunks(total):
            part = slice(start, start + size)
            p = jnp.exp2(s_ref[:, part] - peak).astype(bf16)
            o = dot_nt(p, vt_ref[0, :, part])
            out = o if out is None else out + o
        o_ref[0] = out
        m_ref[0] = peak


def queries(rows, w, b):
    q = (dot(rows, w[:, :WIDE]) + b[0:1]) * (SCALE * LOG2E)
    lane = lax.broadcasted_iota(jnp.int32, q.shape, 1)
    return jnp.where(lane == HEAD_DIM, 1.0, q).astype(bf16)


def fwd_own_first(
    spot, count, marks, clip, vec, target, w_own, w_far, pack_own, pack_far,
    x_out, xp_out, xpt_out, w_out, b_out, kt_out, vt_out, q_out, o_out, m_out,
    xt_s, s_s,
):
    head = pl.program_id(0)

    @pl.when(head == 0)
    def _():
        head_forms(spot, w_own, w_far, pack_own, pack_far, 0, w_out, b_out)
        width = clip.shape[1]
        xhat, _ = norm_stats(clip[...].astype(f32))
        x = xhat * vec[NORM1 : NORM1 + 1, :width] + vec[NORM1 + 1 : NORM1 + 2, :width]
        x = x.astype(bf16)
        x_out[...] = x
        xt_s[...] = flip(x).astype(bf16)
        picked = None
        for start, size in chunks(clip.shape[0]):
            lane = lax.broadcasted_iota(jnp.int32, (target.shape[0], size), 1) + start
            hot = jnp.where(lane == target[...], 1.0, 0.0).astype(bf16)
            part = dot(hot, x_out[start : start + size, :])
            picked = part if picked is None else picked + part
        xp_out[...] = picked.astype(bf16)
        xpt_out[...] = picked.T.astype(bf16)

    mask = dead_keys(spot, count, marks, clip.shape[0], False)
    w, b = w_out[head], b_out[head]
    bound = project_keys(xt_s[...], w, b, mask, kt_out, vt_out)
    q = queries(xp_out[...], w, b)
    q_out[0] = q
    soft_part(q, bound, kt_out, vt_out, s_s, o_out, m_out)


def fwd_own_second(
    spot, count, marks, x, w_own, w_far, pack_own, pack_far,
    w_out, b_out, kt_out, vt_out, q_out, o_out, m_out,
    xt_s, s_s,
):
    head = pl.program_id(0)

    @pl.when(head == 0)
    def _():
        head_forms(spot, w_own, w_far, pack_own, pack_far, 1, w_out, b_out)
        xt_s[...] = flip(x[...]).astype(bf16)

    mask = dead_keys(spot, count, marks, x.shape[0], False)
    w, b = w_out[head], b_out[head]
    bound = project_keys(xt_s[...], w, b, mask, kt_out, vt_out)
    q = queries(x[...], w, b)
    q_out[0] = q
    soft_part(q, bound, kt_out, vt_out, s_s, o_out, m_out)


def finish_head(q, o1, m1, o2, m2, att_out, attt_out, qb_out, qt_out):
    peak = jnp.maximum(m1, m2)
    o = o1 * jnp.exp2(m1 - peak) + o2 * jnp.exp2(m2 - peak)
    total = o[:, HEAD_DIM : HEAD_DIM + 1]
    att = (o / total).astype(bf16)
    att_out[0] = att
    attt_out[0] = flip(att).astype(bf16)
    lse = peak + jnp.log(total) * LOG2E
    q_wide = q.astype(f32)
    qb_out[0] = with_columns(q_wide, HEAD_DIM + 1, -lse).astype(bf16)
    qt_out[0] = q_wide.T.astype(bf16)


def fwd_far_first(
    spot, count, marks, clip, vec, w, b, q, o1, m1,
    x_out, kt_out, vt_out, att_out, attt_out, qb_out, qt_out,
    xt_s, s_s, o_s, m_s,
):
    @pl.when(pl.program_id(0) == 0)
    def _():
        width = clip.shape[1]
        xhat, _ = norm_stats(clip[...].astype(f32))
        x = xhat * vec[NORM1 : NORM1 + 1, :width] + vec[NORM1 + 1 : NORM1 + 2, :width]
        x = x.astype(bf16)
        x_out[...] = x
        xt_s[...] = flip(x).astype(bf16)

    mask = dead_keys(spot, count, marks, clip.shape[0], True)
    bound = project_keys(xt_s[...], w[0], b[0], mask, kt_out, vt_out)
    soft_part(q[0], bound, kt_out, vt_out, s_s, o_s, m_s)
    finish_head(q[0], o1[0], m1[0], o_s[0], m_s[0], att_out, attt_out, qb_out, qt_out)


def fwd_far_second(
    spot, count, marks, x, w, b, q, o1, m1,
    kt_out, vt_out, att_out, attt_out, qb_out, qt_out,
    xt_s, s_s, o_s, m_s,
):
    @pl.when(pl.program_id(0) == 0)
    def _():
        xt_s[...] = flip(x[...]).astype(bf16)

    mask = dead_keys(spot, count, marks, x.shape[0], True)
    bound = project_keys(xt_s[...], w[0], b[0], mask, kt_out, vt_out)
    soft_part(q[0], bound, kt_out, vt_out, s_s, o_s, m_s)
    finish_head(q[0], o1[0], m1[0], o_s[0], m_s[0], att_out, attt_out, qb_out, qt_out)


def attend_own(scalars, x, weights, packs, vec=None, target=None):
    heads = 4
    keys, width = x.shape
    rows = keys if target is None else target.shape[0]
    flat = (1, WIDE, keys)
    head_outs = [
        ((heads, width, 3 * WIDE), bf16, None),
        ((heads, 8, WIDE), f32, None),
        ((heads,) + flat[1:], bf16, flat),
        ((heads,) + flat[1:], bf16, flat),
        ((heads, rows, WIDE), bf16, (1, rows, WIDE)),
        ((heads, rows, WIDE), f32, (1, rows, WIDE)),
        ((heads, rows, 1), f32, (1, rows, 1)),
    ]
    scratch = [pltpu.VMEM((width, keys), bf16), pltpu.VMEM((rows, keys), f32)]
    micros = 5 + keys / 210
    if target is not None:
        ins = scalars + full(x, vec, target, *weights, *packs)
        outs = [
            ((keys, width), bf16, None),
            ((rows, width), bf16, None),
            ((width, rows), bf16, None),
        ] + head_outs
        return call(fwd_own_first, (heads,), ins, outs, scratch, micros)
    ins = scalars + full(x, *weights, *packs)
    return call(fwd_own_second, (heads,), ins, head_outs, scratch, micros)


def attend_far(scalars, x, w, b, q, o1, m1, vec=None):
    heads = w.shape[0]
    keys, width = x.shape
    rows = q.shape[1]
    flat = (1, WIDE, keys)
    head_ins = [
        (w, (1,) + w.shape[1:]),
        (b, (1,) + b.shape[1:]),
        (q, (1, rows, WIDE)),
        (o1, (1, rows, WIDE)),
        (m1, (1, rows, 1)),
    ]
    head_outs = [
        ((heads,) + flat[1:], bf16, flat),
        ((heads,) + flat[1:], bf16, flat),
        ((heads, rows, WIDE), bf16, (1, rows, WIDE)),
        ((heads, WIDE, rows), bf16, (1, WIDE, rows)),
        ((heads, rows, WIDE), bf16, (1, rows, WIDE)),
        ((heads, WIDE, rows), bf16, (1, WIDE, rows)),
    ]
    scratch = [
        pltpu.VMEM((width, keys), bf16),
        pltpu.VMEM((rows, keys), f32),
        pltpu.VMEM((1, rows, WIDE), f32),
        pltpu.VMEM((1, rows, 1), f32),
    ]
    micros = 6 + keys / 210
    if vec is not None:
        ins = scalars + full(x, vec) + head_ins
        outs = [((keys, width), bf16, None)] + head_outs
        return call(fwd_far_first, (heads,), ins, outs, scratch, micros)
    return call(fwd_far_second, (heads,), scalars + full(x) + head_ins, head_outs, scratch, micros)


def score_grads(qb, qt, do, dot_, kt, vt, dkv_s):
    q_all, qt_all, do_all, dot_all = qb[0], qt[0], do[0], dot_[0]
    dq = None
    for start, size in chunks(kt.shape[2]):
        part = slice(start, start + size)
        p = jnp.exp2(dot(q_all, kt[0, :, part]))
        ds = (p * dot(do_all, vt[0, :, part])).astype(bf16)
        dkv_s[WIDE:, part] = dot(dot_all, p.astype(bf16)).astype(bf16)
        dkv_s[:WIDE, part] = (dot(qt_all, ds) * LN2).astype(bf16)
        dq_part = dot_nt(ds, kt[0, :, part])
        dq = dq_part if dq is None else dq + dq_part
    return dq


def add_up(head, total, value):
    @pl.when(head == 0)
    def _():
        total[...] = value

    @pl.when(head > 0)
    def _():
        total[...] += value


def row_sums(columns):
    ones = jnp.ones((8, columns.shape[1]), bf16)
    return dot_nt(ones, columns)[0:1]


def bwd_far(first, last, qb, qt, do, dot_, kt, vt, w, x, *refs):
    if first:
        dxt_in = None
    else:
        dxt_in, refs = refs[0], refs[1:]
    dq_out, dw_out, dvs_out, dx_out, dxt_s, dkv_s = refs
    head = pl.program_id(0)
    dq_out[0] = score_grads(qb, qt, do, dot_, kt, vt, dkv_s)
    dxt = dot(w[0, :, WIDE:], dkv_s[...])
    dw_out[0, 0] = dot(dkv_s[:HEAD_DIM, :], x[...])
    dw_out[0, 1] = dot(dkv_s[WIDE : WIDE + HEAD_DIM, :], x[...])
    dvs_out[0] = jnp.broadcast_to(row_sums(dkv_s[WIDE:, :]), (8, WIDE))
    add_up(head, dxt_s, dxt if first else dxt + jnp.where(head == 0, 1.0, 0.0) * dxt_in[...])

    @pl.when(head == pl.num_programs(0) - 1)
    def _():
        if first and last:
            dx_out[...] = dxt_s[...].T.astype(bf16)
        else:
            dx_out[...] = dxt_s[...].astype(dx_out.dtype)


def near_head(
    spot, head, step, qb, qt, do, dot_, kt, vt, w, x, xq, dq_far, dw_far, dvs_far,
    gmy_out, goth_out, sums_out, dkv_s,
):
    dq = score_grads(qb, qt, do, dot_, kt, vt, dkv_s) + dq_far[0]
    dqt = (dq * SCALE).T.astype(bf16)
    grads = (
        dot(dqt[:HEAD_DIM, :], xq[...]),
        dot(dkv_s[:HEAD_DIM, :], x[...]) + dw_far[0, 0],
        dot(dkv_s[WIDE : WIDE + HEAD_DIM, :], x[...]) + dw_far[0, 1],
    )

    @pl.when(head % 2 == 0)
    def _():
        for j in range(3):
            gmy_out[0, j] = grads[j].astype(bf16)

    @pl.when(head % 2 == 1)
    def _():
        for j in range(3):
            goth_out[0, j] = grads[j].astype(bf16)

    @pl.when(step == 0)
    def _():
        sums_out[...] = jnp.zeros_like(sums_out)

    side = jnp.where(head < 2, spot[0], 1 - spot[0])
    piece = jnp.where(head % 2 == 0, spot[1], 1 - spot[1])
    quarter = 2 * side + piece
    put_row(sums_out, quarter, row_sums(dqt), WIDE)
    put_row(sums_out, 4 + quarter, row_sums(dkv_s[WIDE:, :]) + dvs_far[0, 0:1], WIDE)
    return dot(w[0, :, :WIDE], dqt), dot(w[0, :, WIDE:], dkv_s[...])


def bwd_own_second(
    spot, qb, qt, do, dot_, kt, vt, w, x, dq_far, dw_far, dvs_far,
    gmy_out, goth_out, sums_out, dx_out,
    dxt_s, dkv_s,
):
    head = pl.program_id(0)
    from_q, from_kv = near_head(
        spot, head, head, qb, qt, do, dot_, kt, vt, w, x, x, dq_far, dw_far, dvs_far,
        gmy_out, goth_out, sums_out, dkv_s,
    )
    add_up(head, dxt_s, from_q + from_kv)

    @pl.when(head == pl.num_programs(0) - 1)
    def _():
        dx_out[...] = dxt_s[...].T


def bwd_own_first(
    start, first, last, spot, qb, qt, do, dot_, kt, vt, w, x, xq, target, widen_grad,
    dq_far, dw_far, dvs_far, *refs,
):
    if not first:
        dxt_in, dxpt_in, sums_in, dxt_far, clip, vec = refs[:6]
        refs = refs[6:]
    gmy_out, goth_out, sums_out, refs = refs[0], refs[1], refs[2], refs[3:]
    if last:
        dx_out, dxt_s, dxpt_s, dkv_s = refs
    else:
        dxt_s, dxpt_s, dkv_s = refs
    step = pl.program_id(0)

    @pl.when(step == 0)
    def _():
        sums_out[...] = jnp.zeros_like(sums_out)
        if not first:
            sums_out[0:8] = sums_in[...]

    from_q, from_kv = near_head(
        spot, start + step, 1, qb, qt, do, dot_, kt, vt, w, x, xq, dq_far, dw_far, dvs_far,
        gmy_out, goth_out, sums_out, dkv_s,
    )

    @pl.when(step == 0)
    def _():
        dxt_s[...] = from_kv if first else from_kv + dxt_in[...]
        dxpt_s[...] = from_q + (widen_grad[...].T if first else dxpt_in[...])

    @pl.when(step > 0)
    def _():
        dxt_s[...] += from_kv
        dxpt_s[...] += from_q

    if not last:
        return

    @pl.when(step == pl.num_programs(0) - 1)
    def _():
        width = clip.shape[1]
        dxpt = dxpt_s[...].astype(bf16)
        for at, size in chunks(x.shape[0]):
            lane = lax.broadcasted_iota(jnp.int32, (target.shape[0], size), 1) + at
            hot = jnp.where(lane == target[...], 1.0, 0.0).astype(bf16)
            part = slice(at, at + size)
            grad = (dxt_s[:, part] + dxt_far[:, part].astype(f32) + dot(dxpt, hot)).T
            xhat, rstd = norm_stats(clip[part, :].astype(f32))
            dx_out[part, :], dgain, dbeta = norm_back(
                xhat, rstd, vec[NORM1 : NORM1 + 1, :width], grad
            )
            sums_out[8:9, :width] += dgain
            sums_out[9:10, :width] += dbeta


def back_ins(saved, parts, w, x):
    qb, qt, do, dot_ = saved
    kt, vt = parts
    rows, keys = qb.shape[1], x.shape[0]
    flat = (1, WIDE, keys)
    rtall, rflat = (1, rows, WIDE), (1, WIDE, rows)
    return [
        (qb, rtall), (qt, rflat), (do, rtall), (dot_, rflat),
        (kt, flat), (vt, flat), (w, (1,) + w.shape[1:]), (x, None),
    ]


def attend_back_far(saved, parts, w, x, start, count, before=None):
    heads = w.shape[0]
    last = start + count == heads
    rows = saved[0].shape[1]
    keys, width = x.shape
    ins = back_ins(saved, parts, w, x)
    if before is not None:
        ins += full(before)
    outs = [
        ((count, rows, WIDE), f32, (1, rows, WIDE)),
        ((count, 2, HEAD_DIM, width), f32, (1, 2, HEAD_DIM, width)),
        ((count, 8, WIDE), f32, (1, 8, WIDE)),
        ((keys, width), bf16, None)
        if count == heads
        else ((width, keys), bf16 if last else f32, None),
    ]
    scratch = [pltpu.VMEM((width, keys), f32), pltpu.VMEM((2 * WIDE, keys), bf16)]
    body = functools.partial(bwd_far, before is None, last)
    return call(body, (count,), ins, outs, scratch, 14 if count == heads else 1, start)


def attend_back_own(spot, saved, parts, w, x, far):
    dq_far, dw_far, dvs_far = far
    heads = w.shape[0]
    rows = saved[0].shape[1]
    keys, width = x.shape
    ins = [(spot, SMEM)] + back_ins(saved, parts, w, x)
    ins += [
        (dq_far, (1, rows, WIDE)),
        (dw_far, (1,) + dw_far.shape[1:]),
        (dvs_far, (1,) + dvs_far.shape[1:]),
    ]
    outs = [
        ((2, 3, HEAD_DIM, width), bf16, ("half", 1, 3, HEAD_DIM, width)),
        ((2, 3, HEAD_DIM, width), bf16, ("half", 1, 3, HEAD_DIM, width)),
        ((8, 3 * WIDE), f32, None),
        ((keys, width), f32, None),
    ]
    scratch = [pltpu.VMEM((width, keys), f32), pltpu.VMEM((2 * WIDE, keys), bf16)]
    return call(bwd_own_second, (heads,), ins, outs, scratch, 9 + keys / 105)


def attend_back_side(spot, saved, parts, w, x, far, pooled, start, before):
    dq_far, dw_far, dvs_far = far
    rows = saved[0].shape[1]
    keys, width = x.shape
    whole = lambda a: (a, ("own", 1) + a.shape[1:])
    ins = [(spot, SMEM)] + back_ins(saved, parts, w, x) + full(*pooled)
    ins += [whole(dq_far), whole(dw_far), whole(dvs_far)]
    first = before is None
    if not first:
        ins += full(*before)
    outs = [
        ((1, 3, HEAD_DIM, width), bf16, None),
        ((1, 3, HEAD_DIM, width), bf16, None),
        ((8 if first else 16, 3 * WIDE), f32, None),
    ]
    scratch = [pltpu.VMEM((2 * WIDE, keys), bf16)]
    totals = [(width, keys), (width, rows)]
    if first:
        outs += [(shape, f32, None) for shape in totals]
    else:
        outs.append(((keys, width), f32, None))
        scratch = [pltpu.VMEM(shape, f32) for shape in totals] + scratch
    body = functools.partial(bwd_own_first, start, first, not first)
    return call(body, (2,), ins, outs, scratch, 20 if first else 0.3, start)


def pieces(spot):
    order = (spot[1], 1 - spot[1])
    return [(2 * side + p, side, p, order[p]) for side in (0, 1) for p in (0, 1)]


def put_row(ref, row, value, width):
    at = lax.broadcasted_iota(jnp.int32, (ref.shape[0], width), 0)
    ref[:, :width] = jnp.where(at == row, value, ref[:, :width])


def get_row(ref, row):
    at = lax.broadcasted_iota(jnp.int32, ref.shape, 0)
    return jnp.sum(jnp.where(at == row, ref[...], 0.0), axis=0, keepdims=True)


def absolute(spot, side, index):
    return 2 * (spot[0] if side == 0 else 1 - spot[0]) + index


def lanes_of(index, size):
    return pl.ds(pl.multiple_of(index * size, size), size)


def pad_heads(spot, wo_own, wo_far, wo_s):
    wo_s[...] = jnp.zeros_like(wo_s)
    for place, side, _, index in pieces(spot):
        wo_s[place, :HEAD_DIM, :] = (wo_own, wo_far)[side][lanes_of(index, HEAD_DIM), :]


def out_branch(att, wo_s):
    total = None
    for head in range(att.shape[0]):
        part = dot(att[head], wo_s[head])
        total = part if total is None else total + part
    return total


def sort_far(spot, mine, other, far_s):
    far_s[spot[1]] = mine[...]
    far_s[1 - spot[1]] = other[...]


def mid_first(
    spot, att, wo_own, wo_far, xp, widen, vec, up_own, down_own, up_far, down_far, pack_own, pack_far,
    mid_out, yt_out, act_out, slope_out, layer_out, x2_out, wo_s,
):
    pad_heads(spot, wo_own, wo_far, wo_s)
    size = up_own.shape[1] // 2
    branch = out_branch(att, wo_s) + vec[OUT_B1 : OUT_B1 + 1]
    mid = (dot(xp[...], widen[...]) + vec[WIDEN_B : WIDEN_B + 1]) + branch
    mid_out[...] = mid
    xhat, _ = norm_stats(mid)
    y = (xhat * vec[MLP1 : MLP1 + 1] + vec[MLP1 + 1 : MLP1 + 2]).astype(bf16)
    yt_out[...] = flip(y).astype(bf16)
    feed = None
    for place, side, _, index in pieces(spot):
        lanes = lanes_of(index, size)
        up = (up_own, up_far)[side][:, lanes]
        down = (down_own, down_far)[side][:, lanes]
        hidden = dot(y, up) + (pack_own, pack_far)[side][0:1, lanes]
        act, slope = gelu_both(hidden)
        act = act.astype(bf16)
        act_out[:, place * size : (place + 1) * size] = act
        slope_out[:, place * size : (place + 1) * size] = slope.astype(bf16)
        part = dot_nt(act, down)
        feed = part if feed is None else feed + part
    layer = mid + feed + vec[DOWN_B1 : DOWN_B1 + 1]
    layer_out[...] = layer
    xhat, _ = norm_stats(layer)
    x2_out[...] = (xhat * vec[NORM2 : NORM2 + 1] + vec[NORM2 + 1 : NORM2 + 2]).astype(bf16)


def branch_back(gatt, att, attt, wo_s, do_out, dot_out, g_outs, at):
    for head in range(att.shape[0]):
        do = dot_nt(gatt, wo_s[head]).astype(bf16).astype(f32)
        inner = jnp.sum(do * att[head].astype(f32), axis=1, keepdims=True)
        do_out[head] = with_columns(do, HEAD_DIM, -inner).astype(bf16)
        dot_out[head] = do.T.astype(bf16)
        grad = dot(attt[head, :HEAD_DIM, :], gatt).astype(bf16)
        g_outs[head % 2][head // 2, at : at + HEAD_DIM, :] = grad


def mid_second(
    spot, att, attt, wo_own, wo_far, layer1, vec, up_own, down_own, mine, other,
    pack_own, pack_far, cot,
    y_out, dmid_out, do_out, dot_out, gmy_out, goth_out, small_out, wo_s, far_s,
):
    pad_heads(spot, wo_own, wo_far, wo_s)
    sort_far(spot, mine, other, far_s)
    size = up_own.shape[1] // 2
    width = cot.shape[1]
    g_outs = (gmy_out, goth_out)
    small_out[...] = jnp.zeros_like(small_out)
    mid = layer1[...] + (out_branch(att, wo_s) + vec[OUT_B2 : OUT_B2 + 1])
    xhat, rstd = norm_stats(mid)
    gain = vec[MLP2 : MLP2 + 1]
    y = (xhat * gain + vec[MLP2 + 1 : MLP2 + 2]).astype(bf16)
    yt = flip(y).astype(bf16)
    g_low = cot[...]
    g = g_low.astype(f32)
    gt = g.T.astype(bf16)
    feed = None
    dy = None
    for place, side, p, index in pieces(spot):
        lanes = lanes_of(index, size)
        up = (up_own, far_s.at[0])[side][:, lanes]
        down = (down_own, far_s.at[1])[side][:, lanes]
        hidden = dot(y, up) + (pack_own, pack_far)[side][1:2, lanes]
        act, slope = gelu_both(hidden)
        act = act.astype(bf16)
        dhid = (dot(g_low, down) * slope).astype(bf16)
        part = dot_nt(act, down)
        feed = part if feed is None else feed + part
        part = dot_nt(dhid, up)
        dy = part if dy is None else dy + part
        g_outs[p][side, :width, :] = dot(yt, dhid).astype(bf16)
        g_outs[p][side, width : 2 * width, :] = dot(gt, act).astype(bf16)
        row = 4 + absolute(spot, side, index)
        put_row(small_out, row, jnp.sum(dhid.astype(f32), axis=0, keepdims=True), size)
    y_out[...] = (mid + feed + vec[DOWN_B2 : DOWN_B2 + 1]).astype(bf16)
    back, dgain, dbeta = norm_back(xhat, rstd, gain, dy)
    dmid = g + back
    dmid_out[...] = dmid
    small_out[0:1] = jnp.sum(g, axis=0, keepdims=True)
    small_out[1:2] = dgain
    small_out[2:3] = dbeta
    small_out[3:4] = jnp.sum(dmid, axis=0, keepdims=True)
    branch_back(dmid.astype(bf16), att, attt, wo_s, do_out, dot_out, g_outs, 2 * width)


def mid_back(
    spot, dx_own, dx_far, layer1, vec, dmid2, act, slope, yt, mid,
    up_own, down_own, up_far, down_far, wo_own, wo_far, att, attt, xpt, widen,
    do_out, dot_out, gmy_out, goth_out, wgrad_out, small_out, wo_s, widen_s,
):
    pad_heads(spot, wo_own, wo_far, wo_s)
    size = up_own.shape[1] // 2
    width = layer1.shape[1]
    g_outs = (gmy_out, goth_out)
    small_out[...] = jnp.zeros_like(small_out)
    xhat, rstd = norm_stats(layer1[...])
    back, dgain2, dbeta2 = norm_back(
        xhat, rstd, vec[NORM2 : NORM2 + 1], dx_own[...] + dx_far[...].astype(f32)
    )
    g = dmid2[...] + back
    g_low = g.astype(bf16)
    gt = flip(g_low).astype(bf16)
    dy = None
    for place, side, p, index in pieces(spot):
        lanes = lanes_of(index, size)
        here = slice(place * size, (place + 1) * size)
        up = (up_own, up_far)[side][:, lanes]
        down = (down_own, down_far)[side][:, lanes]
        dhid = (dot(g_low, down) * slope[:, here].astype(f32)).astype(bf16)
        part = dot_nt(dhid, up)
        dy = part if dy is None else dy + part
        g_outs[p][side, :width, :] = dot(yt[...], dhid).astype(bf16)
        g_outs[p][side, width : 2 * width, :] = dot(gt, act[:, here]).astype(bf16)
        row = 4 + absolute(spot, side, index)
        put_row(small_out, row, jnp.sum(dhid.astype(f32), axis=0, keepdims=True), size)
    xhat, rstd = norm_stats(mid[...])
    back, dgain, dbeta = norm_back(xhat, rstd, vec[MLP1 : MLP1 + 1], dy)
    dmid = g + back
    small_out[0:1] = jnp.sum(g, axis=0, keepdims=True)
    small_out[1:2] = dgain
    small_out[2:3] = dbeta
    small_out[3:4] = jnp.sum(dmid, axis=0, keepdims=True)
    small_out[8:9] = dgain2
    small_out[9:10] = dbeta2
    gatt = dmid.astype(bf16)
    branch_back(gatt, att, attt, wo_s, do_out, dot_out, g_outs, 2 * width)
    widen_s[...] = dot(xpt[...], gatt)
    rows = widen_s.shape[0] // 4
    at = 2 * width + HEAD_DIM
    for place, side, p, index in pieces(spot):
        quarter = widen_s[lanes_of(absolute(spot, side, index), rows), :]
        g_outs[p][side, at : at + rows, :] = quarter.astype(bf16)
    wgrad_out[...] = dot_nt(gatt, widen[...])


def finish_mlp(spot, mine, other, *refs):
    if len(refs) == 3:
        widen_far, widen_out = None, None
        up_out, down_out, out_out = refs
    else:
        widen_far, up_out, down_out, out_out, widen_out = refs
    width = up_out.shape[0]
    size = up_out.shape[1] // 2
    for part, index in ((mine, spot[1]), (other, 1 - spot[1])):
        lanes = lanes_of(index, size)
        up_out[:, lanes] = part[:width, :].astype(f32)
        down_out[lanes, :] = part[width : 2 * width, :].astype(f32).T
        out_out[lanes_of(index, HEAD_DIM), :] = part[2 * width : 2 * width + HEAD_DIM, :].astype(f32)
    if widen_out is not None:
        rows = widen_out.shape[0] // 4
        at = 2 * width + HEAD_DIM
        for side in (0, 1):
            for p, index in ((0, spot[1]), (1, 1 - spot[1])):
                if side == 0:
                    value = (mine, other)[p][at : at + rows, :]
                else:
                    value = widen_far[p]
                widen_out[lanes_of(absolute(spot, side, index), rows), :] = value.astype(f32)


def finish_qkv(spot, mine, other, out, both_s):
    for j in range(3):
        for part, index in ((mine, spot[1]), (other, 1 - spot[1])):
            both_s[lanes_of(index, HEAD_DIM), :] = part[j].astype(f32)
        out[:, j, :] = both_s[...].T


def finish_small(spot, small, *outs):
    (n1g, n1b, wb, qvb1, ob1, m1g, m1b, ub1, db1, n2g, n2b, qvb2, ob2, m2g, m2b, ub2, db2) = outs
    first = 2 * spot[0]

    def put(out, row):
        out[...] = small[row, : out.shape[0]]

    def put_layer(base, sums, ub, qvb):
        size = ub.shape[0] // 2
        for p in (0, 1):
            ub[p * size : (p + 1) * size] = get_row(small, base + 4 + first + p)[0]
            for j in (0, 1):
                row = get_row(small, sums + 4 * j + first + p)
                qvb[j : j + 1, p * HEAD_DIM : (p + 1) * HEAD_DIM] = row[:, :HEAD_DIM]

    put(db2, 0)
    put(m2g, 1)
    put(m2b, 2)
    put(ob2, 3)
    put(db1, 16)
    put(m1g, 17)
    put(m1b, 18)
    put(ob1, 19)
    put(wb, 19)
    put(n2g, 24)
    put(n2b, 25)
    put(n1g, 48)
    put(n1b, 49)
    put_layer(0, 32, ub2, qvb2)
    put_layer(16, 40, ub1, qvb1)


def swap(x):
    return lax.ppermute(x, "head", [(0, 1), (1, 0)])


def core_swap(x):
    return lax.ppermute(x, "core", [(0, 1), (1, 0)])


def add_low(a, b):
    return (a.astype(f32) + b.astype(f32)).astype(bf16)


def tie(later, dep):
    return lax.optimization_barrier((later, dep))


def exchange(x, axis, bit):
    other = lax.ppermute(x, axis, [(i, i ^ bit) for i in range(lax.axis_size(axis))])
    return (x.astype(f32) + other.astype(f32)).astype(x.dtype)


def exchange_bits(axis):
    bits = [1 << k for k in range((lax.axis_size(axis) - 1).bit_length())]
    return bits[1:] + bits[:1]


def tree_sum(x, axis):
    for bit in exchange_bits(axis):
        x = exchange(x, axis, bit)
    return x


def shards(
    clip_in,
    frame_count,
    frame_mask,
    pool_index,
    first_norm_gain,
    first_norm_bias,
    first_widen_weight,
    first_widen_bias,
    first_qkv_weight,
    first_qv_bias,
    first_out_weight,
    first_out_bias,
    first_mlp_gain,
    first_mlp_bias,
    first_up_weight,
    first_up_bias,
    first_down_weight,
    first_down_bias,
    second_norm_gain,
    second_norm_bias,
    second_qkv_weight,
    second_qv_bias,
    second_out_weight,
    second_out_bias,
    second_mlp_gain,
    second_mlp_bias,
    second_up_weight,
    second_up_bias,
    second_down_weight,
    second_down_bias,
    cotangent,
):
    clip = clip_in[0]
    cot = cotangent[0]
    side = lax.axis_index("head")
    spot = jnp.stack([side, lax.axis_index("core")]).astype(jnp.int32)
    scalars = [(spot, SMEM), (frame_count, SMEM), (frame_mask, SMEM)]
    place = (spot, SMEM)
    keys1, width1 = clip.shape
    rows, dim = cot.shape
    n_up = first_up_bias.shape[0]
    hidden = 2 * n_up
    heads = 4
    out_rows = 2 * dim + HEAD_DIM
    half_up = n_up // 2

    qkv1 = jnp.swapaxes(first_qkv_weight, 0, 1)
    qkv2 = jnp.swapaxes(second_qkv_weight, 0, 1)
    qv_row = jnp.concatenate([first_qv_bias.reshape(-1), second_qv_bias.reshape(-1)])
    pack = jnp.stack([first_up_bias, second_up_bias, qv_row])
    far_qkv1 = swap(qkv1)
    far_pack = swap(pack)
    clip_send, (far_qkv1, far_pack) = tie(clip, (far_qkv1, far_pack))
    far_clip = swap(clip_send)
    down1, down2 = first_down_weight.T, second_down_weight.T
    first_core = lax.axis_index("core") == 0
    send2 = jnp.where(first_core, second_up_weight, down2)

    def wide(v):
        return jnp.pad(v, (0, dim - v.shape[0]))

    vec = jnp.stack(
        [
            wide(first_norm_gain), wide(first_norm_bias), first_widen_bias, first_out_bias,
            first_mlp_gain, first_mlp_bias, first_down_bias, second_norm_gain, second_norm_bias,
            second_out_bias, second_mlp_gain, second_mlp_bias, second_down_bias,
        ]
    )

    picks = lax.dynamic_slice_in_dim(pool_index[0], side * rows, rows, 0)
    token = jnp.arange(rows, dtype=jnp.int32)
    frame, cell = token // (SIDE * SIDE), token % (SIDE * SIDE)
    line = 2 * (cell // SIDE) + picks // 2
    column = 2 * (cell % SIDE) + picks % 2
    target = (frame * (4 * SIDE * SIDE) + line * (2 * SIDE) + column)[:, None]

    x1, x1p, x1pt, w1, b1, kt1, vt1, q1, o1, m1 = attend_own(
        scalars, clip, (qkv1, far_qkv1), (pack, far_pack), vec, target
    )
    mlp1, m1 = tie((first_out_weight, first_up_weight, down1), m1)
    far_out1, far_up1, far_down1 = [swap(w) for w in mlp1]
    x1f, kt1f, vt1f, att1, attt1, qb1, qt1 = attend_far(
        scalars, far_clip, w1, b1, q1, o1, m1, vec
    )
    late, att1 = tie((qkv2, second_out_weight), att1)
    far_qkv2, far_out2 = [swap(w) for w in late]
    send2, far_qkv2 = tie(send2, far_qkv2)
    mine2 = swap(send2)
    mid1, yt1, act1, slope1, layer1, x2 = call(
        mid_first,
        (),
        [place]
        + full(
            att1, first_out_weight, far_out1, x1p, first_widen_weight, vec,
            first_up_weight, down1, far_up1, far_down1, pack, far_pack,
        ),
        [
            ((rows, dim), f32, None),
            ((dim, rows), bf16, None),
            ((rows, hidden), bf16, None),
            ((rows, hidden), bf16, None),
            ((rows, dim), f32, None),
            ((rows, dim), bf16, None),
        ],
        [pltpu.VMEM((heads, WIDE, dim), bf16)],
        11,
    )

    x2f = swap(x2)
    w2, b2, kt2, vt2, q2, o2, m2 = attend_own(scalars, x2, (qkv2, far_qkv2), (pack, far_pack))
    far_out2, m2 = tie(far_out2, m2)
    kt2f, vt2f, att2, attt2, qb2, qt2 = attend_far(scalars, x2f, w2, b2, q2, o2, m2)
    mine2, att2 = tie(mine2, att2)
    other2 = core_swap(mine2)
    out, dmid2, do2, dot2, gmy2, goth2, small2 = call(
        mid_second,
        (),
        [place]
        + full(
            att2, attt2, second_out_weight, far_out2, layer1, vec, second_up_weight, down2,
            mine2, other2, pack, far_pack, cot,
        ),
        [
            ((rows, dim), bf16, None),
            ((rows, dim), f32, None),
            ((heads, rows, WIDE), bf16, None),
            ((heads, WIDE, rows), bf16, None),
            ((2, out_rows, half_up), bf16, None),
            ((2, out_rows, half_up), bf16, None),
            ((16, dim), f32, None),
        ],
        [pltpu.VMEM((heads, WIDE, dim), bf16), pltpu.VMEM((2, dim, n_up), bf16)],
        18,
    )

    got_a = core_swap(goth2)
    saved2 = (qb2, qt2, do2, dot2)
    dq2f, dw2f, dvs2f, dx2_send = attend_back_far(saved2, (kt2f, vt2f), w2, x2f, 0, heads)
    dx2_far = swap(dx2_send)
    near_a, away_a = add_low(gmy2[0], got_a[0]), add_low(gmy2[1], got_a[1])
    (near_a, away_a), dq2f = tie((near_a, away_a), dq2f)
    hmy2, hoth2, sums2, dx2 = attend_back_own(
        spot, saved2, (kt2, vt2), w2, x2, (dq2f, dw2f, dvs2f)
    )
    (away_a, hoth2), dx2 = tie((away_a, hoth2), dx2)
    got_a2 = swap(away_a)
    got_h2 = core_swap(hoth2)

    widen_rows = width1 // 4
    do1, dot1, gmy1, goth1, wgrad, small1 = call(
        mid_back,
        (),
        [place]
        + full(
            dx2, dx2_far, layer1, vec, dmid2, act1, slope1, yt1, mid1,
            first_up_weight, down1, far_up1, far_down1,
            first_out_weight, far_out1, att1, attt1, x1pt, first_widen_weight,
        ),
        [
            ((heads, rows, WIDE), bf16, None),
            ((heads, WIDE, rows), bf16, None),
            ((2, out_rows + widen_rows, half_up), bf16, None),
            ((2, out_rows + widen_rows, half_up), bf16, None),
            ((rows, width1), f32, None),
            ((16, dim), f32, None),
        ],
        [
            pltpu.VMEM((heads, WIDE, dim), bf16),
            pltpu.VMEM((width1, dim), f32),
        ],
        17,
    )
    near_h, away_h = add_low(hmy2[0], got_h2[0]), add_low(hmy2[1], got_h2[1])
    total_a = add_low(near_a, got_a2)
    (total_a, near_h, away_h, goth1), do1 = tie((total_a, near_h, away_h, goth1), do1)
    bits = exchange_bits("outer")
    next_a = exchange(total_a, "outer", bits[0])
    got_b = core_swap(goth1)
    got_h = swap(away_h)

    saved1 = (qb1, qt1, do1, dot1)
    two = heads // 2
    *own_far, dx1_part = attend_back_far(saved1, (kt1f, vt1f), w1, x1f, 0, two)
    near_b, away_b = add_low(gmy1[0], got_b[0]), add_low(gmy1[1], got_b[1])
    total_h = add_low(near_h, got_h)
    (near_b, away_b, total_h, next_a), dx1_part = tie((near_b, away_b, total_h, next_a), dx1_part)
    got_b2 = swap(away_b)
    next_a = exchange(next_a, "outer", bits[1])
    *far_far, dx1_send = attend_back_far(saved1, (kt1f, vt1f), w1, x1f, two, two, dx1_part)
    dx1_far = swap(dx1_send)
    total_b = add_low(near_b, got_b2)
    (next_a, total_b, total_h), far_far = tie((next_a, total_b, total_h), far_far)
    total_b, total_h = lax.psum((total_b, total_h), "outer")
    for bit in bits[2:]:
        next_a = exchange(next_a, "outer", bit)
    pooled = (x1p, target, wgrad)
    gmy_f, goth_f, sums1f, *totals = attend_back_side(
        spot, saved1, (kt1, vt1), w1, x1, far_far, pooled, two, None
    )
    (dx1_far, goth_f, total_a), own_far = tie((dx1_far, goth_f, next_a), own_far)
    other_a = core_swap(total_a)
    got_cf = core_swap(goth_f)
    gmy_o, goth_o, sums1, grad_in = attend_back_side(
        spot, saved1, (kt1, vt1), w1, x1, own_far, pooled, 0, (*totals, sums1f, dx1_far, clip, vec)
    )

    got_co = core_swap(goth_o)
    got_c2 = swap(add_low(gmy_f[0], got_cf[0]))
    total_c = (gmy_o[0].astype(f32) + got_co[0].astype(f32)).astype(bf16)
    total_c = add_low(total_c, got_c2)
    (total_b, total_h), total_c = tie((total_b, total_h), total_c)
    total_c = tree_sum(total_c, "outer")
    small = jnp.concatenate([small2, small1, sums2, sums1])
    small = tree_sum(small, "core")
    small = tree_sum(small, "head")
    small = tree_sum(small, "outer")

    def qkv_form(mine):
        width = mine.shape[2]
        (grad,) = call(
            finish_qkv,
            (),
            [place] + full(mine, core_swap(mine)),
            [((width, 3, 2 * HEAD_DIM), f32, None)],
            [pltpu.VMEM((2 * HEAD_DIM, width), f32)],
            2,
        )
        return grad

    mlp_outs = [
        ((dim, n_up), f32, None),
        ((n_up, dim), f32, None),
        ((2 * HEAD_DIM, dim), f32, None),
    ]
    gup2, gdn2, gout2 = call(
        finish_mlp, (), [place] + full(total_a, other_a), mlp_outs, [], 3
    )
    other_b = core_swap(total_b)
    widen_far = swap(jnp.stack([total_b[out_rows:], other_b[out_rows:]]))
    gup1, gdn1, gout1, gwiden = call(
        finish_mlp,
        (),
        [place] + full(total_b, other_b, widen_far),
        mlp_outs + [((width1, dim), f32, None)],
        [],
        3,
    )
    gqkv2 = qkv_form(total_h)
    gqkv1 = qkv_form(total_c)
    vector = ((dim,), f32, None)
    thin = ((width1,), f32, None)
    layer_vectors = [((2, 2 * HEAD_DIM), f32, None)] + [vector] * 3 + [((n_up,), f32, None), vector]
    (n1g, n1b, wb, qvb1, ob1, m1g, m1b, ub1, db1, n2g, n2b, qvb2, ob2, m2g, m2b, ub2, db2) = call(
        finish_small,
        (),
        [place] + full(small),
        [thin, thin, vector] + layer_vectors + [vector, vector] + layer_vectors,
        [],
        2,
    )
    return (
        out[None], grad_in[None],
        n1g, n1b, gwiden, wb, gqkv1, qvb1, gout1, ob1, m1g, m1b, gup1, ub1, gdn1, db1,
        n2g, n2b, gqkv2, qvb2, gout2, ob2, m2g, m2b, gup2, ub2, gdn2, db2,
    )


def solution(mesh):
    in_specs = (
        P(BATCH, "head", None),
        P(BATCH),
        P(BATCH, None),
        P(BATCH, None),
        P(),
        P(),
        P(),
        P(),
        P(None, None, "head"),
        P(None, "head"),
        P("head", None),
        P(),
        P(),
        P(),
        P(None, "head"),
        P("head"),
        P("head", None),
        P(),
        P(),
        P(),
        P(None, None, "head"),
        P(None, "head"),
        P("head", None),
        P(),
        P(),
        P(),
        P(None, "head"),
        P("head"),
        P("head", None),
        P(),
        P(BATCH, "head", None),
    )
    out_specs = (
        P(BATCH, "head", None),
        P(BATCH, "head", None),
        P(),
        P(),
        P(),
        P(),
        P(None, None, "head"),
        P(None, "head"),
        P("head", None),
        P(),
        P(),
        P(),
        P(None, "head"),
        P("head"),
        P("head", None),
        P(),
        P(),
        P(),
        P(None, None, "head"),
        P(None, "head"),
        P("head", None),
        P(),
        P(),
        P(),
        P(None, "head"),
        P("head"),
        P("head", None),
        P(),
    )
    outer = mesh.shape["batch"] // 2
    split = Mesh(
        mesh.devices.reshape(outer, 2, mesh.shape["head"]), ("outer", "core", "head")
    )
    return jax.shard_map(shards, mesh=split, in_specs=in_specs, out_specs=out_specs, check_vma=False)
```

```python
import functools

import jax
import jax.numpy as jnp
from jax import lax
from jax.experimental import pallas as pl
from jax.experimental.pallas import tpu as pltpu
from jax.sharding import Mesh, PartitionSpec as P

HEAD_DIM = 96
WIDE = 128
SIDE = 14
DEAD = -1e30
LOG2E = 1.4426950408889634
LN2 = 0.6931471805599453
SCALE = HEAD_DIM ** (-0.5)
EPS = 1e-06
CHUNK = 512
SAFE = 60.0
BATCH = ("outer", "core")

bf16 = jnp.bfloat16
f32 = jnp.float32


def dot(a, b):
    return jnp.dot(a, b, preferred_element_type=f32)


def dot_nt(a, b):
    return lax.dot_general(a, b, (((1,), (1,)), ((), ())), preferred_element_type=f32)


def eye(size):
    row = lax.broadcasted_iota(jnp.int32, (size, size), 0)
    return jnp.where(row == lax.broadcasted_iota(jnp.int32, (size, size), 1), 1.0, 0.0).astype(bf16)


def flip(a):
    return dot_nt(eye(a.shape[1]), a).astype(bf16)


def dot_tn(a, b):
    return lax.dot_general(a, b, (((0,), (0,)), ((), ())), preferred_element_type=f32)


def chunks(total):
    return [(start, min(CHUNK, total - start)) for start in range(0, total, CHUNK)]


def norm_stats(v):
    centered = v - jnp.mean(v, axis=-1, keepdims=True)
    rstd = lax.rsqrt(jnp.mean(centered * centered, axis=-1, keepdims=True) + EPS)
    return centered * rstd, rstd


def norm_back(xhat, rstd, gain, grad):
    scaled = grad * gain
    back = rstd * (
        scaled
        - jnp.mean(scaled, axis=-1, keepdims=True)
        - xhat * jnp.mean(scaled * xhat, axis=-1, keepdims=True)
    )
    return (
        back,
        jnp.sum(grad * xhat, axis=0, keepdims=True),
        jnp.sum(grad, axis=0, keepdims=True),
    )


def norm_flat(v):
    centered = v - jnp.mean(v, axis=0, keepdims=True)
    rstd = lax.rsqrt(jnp.mean(centered * centered, axis=0, keepdims=True) + EPS)
    return centered * rstd, rstd


def as_column(row):
    return jnp.broadcast_to(row, (WIDE, row.shape[1])).T[:, :1]


def as_row(column):
    return jnp.broadcast_to(column, (column.shape[0], WIDE)).T[:1]


def three_parts(v):
    high = v.astype(bf16).astype(f32)
    rest = v - high
    middle = rest.astype(bf16).astype(f32)
    return high, middle, rest - middle


def with_columns(block, first, column):
    lane = lax.broadcasted_iota(jnp.int32, block.shape, 1)
    for offset, part in enumerate(three_parts(column)):
        block = jnp.where(lane == first + offset, part, block)
    return block


def gelu_both(u):
    cdf = 0.5 + 0.5 * lax.erf(u * 0.7071067811865476)
    return u * cdf, cdf + u * (jnp.exp(-0.5 * u * u) * 0.3989422804014327)


NORM1, WIDEN_B, OUT_B1, MLP1, DOWN_B1, NORM2, OUT_B2, MLP2, DOWN_B2 = 0, 2, 3, 4, 6, 7, 9, 10, 12
SMEM = "smem"


def call(body, grid, ins, outs, scratch, micros, offset=0, megabytes=56):
    def spec(shape, block):
        if block == SMEM:
            return pl.BlockSpec(memory_space=pltpu.SMEM)
        if block is None:
            zeros = (0,) * len(shape)
            return pl.BlockSpec(tuple(shape), lambda *_: zeros)
        if block[0] == "own":
            rest = (0,) * (len(shape) - 1)
            return pl.BlockSpec(tuple(block[1:]), lambda i, *_: (i,) + rest)
        if block[0] == "half":
            rest = (0,) * (len(shape) - 1)
            return pl.BlockSpec(tuple(block[1:]), lambda i, *_: ((i + offset) // 2,) + rest)
        rest = (0,) * (len(shape) - 1)
        return pl.BlockSpec(tuple(block), lambda i, *_: (i + offset,) + rest)

    def out_spec(shape, block):
        if block is None or block[0] == "half":
            return spec(shape, block)
        rest = (0,) * (len(shape) - 1)
        return pl.BlockSpec(tuple(block), lambda i, *_: (i,) + rest)

    return pl.pallas_call(
        body,
        grid=grid,
        in_specs=[spec(a.shape, b) for a, b in ins],
        out_specs=[out_spec(s, b) for s, _, b in outs],
        out_shape=[jax.ShapeDtypeStruct(s, d) for s, d, _ in outs],
        scratch_shapes=scratch,
        cost_estimate=pl.CostEstimate(
            flops=int(micros * 1.15e9), transcendentals=0, bytes_accessed=int(micros * 3.69e6)
        ),
        compiler_params=pltpu.CompilerParams(
            dimension_semantics=("arbitrary",) * len(grid),
            vmem_limit_bytes=megabytes << 20,
        ),
    )(*[a for a, _ in ins])


def full(*arrays):
    return [(a, None) for a in arrays]


def dead_keys(spot, count, marks, keys, far):
    half = marks.shape[1] // 2
    each = keys // half
    first = (1 - spot[0] if far else spot[0]) * half
    lane = lax.broadcasted_iota(jnp.int32, (1, keys), 1)
    row = jnp.zeros((1, keys), f32)
    for f in range(half):
        dead = (first + f >= count[0]) | (marks[0, first + f] != 1)
        row = jnp.where((lane >= f * each) & (lane < (f + 1) * each), jnp.where(dead, DEAD, 0.0), row)
    return row


def head_forms(spot, w_own, w_far, pack_own, pack_far, layer, w_out, wt_out, b_out):
    first = spot[1] == 0
    filled = wt_out if layer else w_out
    filled[...] = jnp.zeros_like(filled)
    b_out[...] = jnp.zeros_like(b_out)
    for side, (w, pack) in enumerate(((w_own, pack_own), (w_far, pack_far))):
        for j in range(3):
            place = slice(j * WIDE, j * WIDE + HEAD_DIM)
            if layer:
                low, high = w[j, :HEAD_DIM].astype(f32), w[j, HEAD_DIM:].astype(f32)
                wt_out[2 * side, place] = jnp.where(first, low, high).astype(bf16)
                wt_out[2 * side + 1, place] = jnp.where(first, high, low).astype(bf16)
            else:
                low, high = w[j, :, :HEAD_DIM].astype(f32), w[j, :, HEAD_DIM:].astype(f32)
                w_out[2 * side, :, place] = jnp.where(first, low, high).astype(bf16)
                w_out[2 * side + 1, :, place] = jnp.where(first, high, low).astype(bf16)
        for j in range(2):
            start = (2 * layer + j) * 2 * HEAD_DIM
            low = pack[2:3, start : start + HEAD_DIM]
            high = pack[2:3, start + HEAD_DIM : start + 2 * HEAD_DIM]
            b_out[2 * side, j : j + 1, :HEAD_DIM] = jnp.where(first, low, high)
            b_out[2 * side + 1, j : j + 1, :HEAD_DIM] = jnp.where(first, high, low)
    for head in range(w_out.shape[0]):
        if layer:
            w_out[head] = flip(wt_out[head])
        else:
            wt_out[head] = flip(w_out[head])


def project_keys(x_t, w_t, b, mask, kt_out, vt_out):
    both = dot(w_t[WIDE:], x_t)
    k_t, v_t = both[:WIDE], both[WIDE:]
    key_bound = jnp.max(jnp.sum(k_t * k_t, axis=0, keepdims=True))
    row = lax.broadcasted_iota(jnp.int32, k_t.shape, 0)
    k_t = jnp.where(row == HEAD_DIM, mask, k_t)
    k_t = jnp.where((row > HEAD_DIM) & (row < HEAD_DIM + 4), 1.0, k_t)
    kt_out[0] = k_t.astype(bf16)
    column = as_column(b[1:2])
    row = lax.broadcasted_iota(jnp.int32, column.shape, 0)
    column = jnp.where((row >= HEAD_DIM) & (row < HEAD_DIM + 3), 1.0, column)
    vt_out[0] = (v_t + column).astype(bf16)
    return key_bound


def soft_part(q_t_ref, q, key_bound, kt_ref, vt_ref, s_ref, o_ref, m_ref):
    total = kt_ref.shape[2]
    q_wide = q_t_ref[0, :HEAD_DIM, :].astype(f32)
    bound = jnp.max(jnp.sum(q_wide * q_wide, axis=0, keepdims=True)) * key_bound
    safe = bound < SAFE * SAFE

    @pl.when(safe)
    def _():
        out = None
        for start, size in chunks(total):
            part = slice(start, start + size)
            p = jnp.exp2(dot(q, kt_ref[0, :, part])).astype(bf16)
            o = dot_nt(vt_ref[0, :, part], p)
            out = o if out is None else out + o
        o_ref[0] = out
        m_ref[0] = jnp.zeros_like(m_ref[0])

    @pl.when(jnp.logical_not(safe))
    def _():
        peak = None
        for start, size in chunks(total):
            s = dot(q, kt_ref[0, :, start : start + size])
            s_ref[:, start : start + size] = s
            top = jnp.max(s, axis=1, keepdims=True)
            peak = top if peak is None else jnp.maximum(peak, top)
        out = None
        for start, size in chunks(total):
            part = slice(start, start + size)
            p = jnp.exp2(s_ref[:, part] - peak).astype(bf16)
            o = dot_nt(vt_ref[0, :, part], p)
            out = o if out is None else out + o
        o_ref[0] = out
        m_ref[0] = as_row(peak)


def queries(q, rows_t, w_t, b, q_out, qt_out):
    q = (q + b[0:1]) * (SCALE * LOG2E)
    lane = lax.broadcasted_iota(jnp.int32, q.shape, 1)
    q = jnp.where(lane == HEAD_DIM, 1.0, q).astype(bf16)
    q_out[0] = q
    qt_out[0] = ((dot(w_t[:WIDE], rows_t) + as_column(b[0:1])) * (SCALE * LOG2E)).astype(bf16)
    return q


def input_norm(clip_t, vec):
    width = clip_t.shape[0]
    xhat, _ = norm_flat(clip_t[...].astype(f32))
    gain, beta = vec[NORM1 : NORM1 + 1, :width], vec[NORM1 + 1 : NORM1 + 2, :width]
    return (xhat * as_column(gain) + as_column(beta)).astype(bf16)


def fwd_own_first(
    spot, count, marks, clip_t, vec, target, w_own, w_far, pack_own, pack_far,
    xt_out, xpt_out, w_out, wt_out, b_out, kt_out, vt_out, q_out, qt_out, o_out, m_out,
    s_s,
):
    head = pl.program_id(0)

    @pl.when(head == 0)
    def _():
        head_forms(spot, w_own, w_far, pack_own, pack_far, 0, w_out, wt_out, b_out)
        xt_out[...] = input_norm(clip_t, vec)
        picked = None
        for start, size in chunks(clip_t.shape[1]):
            lane = lax.broadcasted_iota(jnp.int32, (target.shape[0], size), 1) + start
            hot = jnp.where(lane == target[...], 1.0, 0.0).astype(bf16)
            part = dot_nt(xt_out[:, start : start + size], hot)
            picked = part if picked is None else picked + part
        xpt_out[...] = picked.astype(bf16)

    mask = dead_keys(spot, count, marks, clip_t.shape[1], False)
    w_t, b = wt_out[head], b_out[head]
    bound = project_keys(xt_out[...], w_t, b, mask, kt_out, vt_out)
    q = dot_tn(xpt_out[...], w_out[head, :, :WIDE])
    q = queries(q, xpt_out[...], w_t, b, q_out, qt_out)
    soft_part(qt_out, q, bound, kt_out, vt_out, s_s, o_out, m_out)


def fwd_own_second(
    spot, count, marks, x, w_own, w_far, pack_own, pack_far,
    w_out, wt_out, b_out, kt_out, vt_out, q_out, qt_out, o_out, m_out,
    xt_s, s_s,
):
    head = pl.program_id(0)

    @pl.when(head == 0)
    def _():
        head_forms(spot, w_own, w_far, pack_own, pack_far, 1, w_out, wt_out, b_out)
        xt_s[...] = flip(x[...])

    mask = dead_keys(spot, count, marks, x.shape[0], False)
    w_t, b = wt_out[head], b_out[head]
    bound = project_keys(xt_s[...], w_t, b, mask, kt_out, vt_out)
    q = queries(dot(x[...], w_out[head, :, :WIDE]), xt_s[...], w_t, b, q_out, qt_out)
    soft_part(qt_out, q, bound, kt_out, vt_out, s_s, o_out, m_out)


def finish_head(q, o1, m1, o2, m2, attt_out, inv_out, qb_out):
    peak = jnp.maximum(m1, m2)
    o = o1 * jnp.exp2(m1 - peak) + o2 * jnp.exp2(m2 - peak)
    inv = 1.0 / o[HEAD_DIM : HEAD_DIM + 1]
    attt_out[0] = (o * inv).astype(bf16)
    inv_out[0] = inv
    qb_out[0] = q

    @pl.when(jnp.max(jnp.abs(peak)) > 0.0)
    def _():
        qb_out[0] = with_columns(q.astype(f32), HEAD_DIM + 1, -as_column(peak)).astype(bf16)


def fwd_far_first(
    spot, count, marks, clip_t, vec, w_t, b, q, qt, o1, m1,
    xt_out, kt_out, vt_out, attt_out, inv_out, qb_out,
    s_s, o_s, m_s,
):
    @pl.when(pl.program_id(0) == 0)
    def _():
        xt_out[...] = input_norm(clip_t, vec)

    mask = dead_keys(spot, count, marks, clip_t.shape[1], True)
    bound = project_keys(xt_out[...], w_t[0], b[0], mask, kt_out, vt_out)
    soft_part(qt, q[0], bound, kt_out, vt_out, s_s, o_s, m_s)
    finish_head(q[0], o1[0], m1[0], o_s[0], m_s[0], attt_out, inv_out, qb_out)


def fwd_far_second(
    spot, count, marks, x, w_t, b, q, qt, o1, m1,
    kt_out, vt_out, attt_out, inv_out, qb_out,
    s_s, o_s, m_s, xt_s,
):
    @pl.when(pl.program_id(0) == 0)
    def _():
        xt_s[...] = flip(x[...])

    mask = dead_keys(spot, count, marks, x.shape[0], True)
    bound = project_keys(xt_s[...], w_t[0], b[0], mask, kt_out, vt_out)
    soft_part(qt, q[0], bound, kt_out, vt_out, s_s, o_s, m_s)
    finish_head(q[0], o1[0], m1[0], o_s[0], m_s[0], attt_out, inv_out, qb_out)


def attend_own(scalars, x, weights, packs, vec=None, target=None):
    heads = 4
    width, keys = x.shape if target is not None else x.shape[::-1]
    rows = keys if target is None else target.shape[0]
    flat = (1, WIDE, keys)
    head_outs = [
        ((heads, width, 3 * WIDE), bf16, None),
        ((heads, 3 * WIDE, width), bf16, None),
        ((heads, 8, WIDE), f32, None),
        ((heads,) + flat[1:], bf16, flat),
        ((heads,) + flat[1:], bf16, flat),
        ((heads, rows, WIDE), bf16, (1, rows, WIDE)),
        ((heads, WIDE, rows), bf16, (1, WIDE, rows)),
        ((heads, WIDE, rows), f32, (1, WIDE, rows)),
        ((heads, 1, rows), f32, (1, 1, rows)),
    ]
    scratch = [pltpu.VMEM((rows, keys), f32)]
    micros = 5 + keys / 210
    if target is not None:
        ins = scalars + full(x, vec, target, *weights, *packs)
        outs = [((width, keys), bf16, None), ((width, rows), bf16, None)] + head_outs
        return call(fwd_own_first, (heads,), ins, outs, scratch, micros)
    ins = scalars + full(x, *weights, *packs)
    scratch = [pltpu.VMEM((width, keys), bf16)] + scratch
    return call(fwd_own_second, (heads,), ins, head_outs, scratch, micros)


def attend_far(scalars, x, w_t, b, q, qt, o1, m1, vec=None):
    heads = w_t.shape[0]
    width, keys = x.shape if vec is not None else x.shape[::-1]
    rows = q.shape[1]
    flat = (1, WIDE, keys)
    head_ins = [
        (w_t, (1,) + w_t.shape[1:]),
        (b, (1,) + b.shape[1:]),
        (q, (1, rows, WIDE)),
        (qt, (1, WIDE, rows)),
        (o1, (1, WIDE, rows)),
        (m1, (1, 1, rows)),
    ]
    head_outs = [
        ((heads,) + flat[1:], bf16, flat),
        ((heads,) + flat[1:], bf16, flat),
        ((heads, WIDE, rows), bf16, (1, WIDE, rows)),
        ((heads, 1, rows), f32, (1, 1, rows)),
        ((heads, rows, WIDE), bf16, (1, rows, WIDE)),
    ]
    scratch = [
        pltpu.VMEM((rows, keys), f32),
        pltpu.VMEM((1, WIDE, rows), f32),
        pltpu.VMEM((1, 1, rows), f32),
    ]
    micros = 6 + keys / 210
    if vec is not None:
        ins = scalars + full(x, vec) + head_ins
        outs = [((width, keys), bf16, None)] + head_outs
        return call(fwd_far_first, (heads,), ins, outs, scratch, micros)
    scratch.append(pltpu.VMEM((width, keys), bf16))
    return call(fwd_far_second, (heads,), scalars + full(x) + head_ins, head_outs, scratch, micros)


def score_grads(qb, qt, do, dot_, kt, vt, dkv_s):
    q_all, qt_all, do_all, dot_all = qb[0], qt[0], do[0], dot_[0]
    dq = None
    for start, size in chunks(kt.shape[2]):
        part = slice(start, start + size)
        p = jnp.exp2(dot(q_all, kt[0, :, part]))
        ds = (p * dot(do_all, vt[0, :, part])).astype(bf16)
        dkv_s[WIDE:, part] = dot(dot_all, p.astype(bf16)).astype(bf16)
        dkv_s[:WIDE, part] = (dot(qt_all, ds) * LN2).astype(bf16)
        dq_part = dot_nt(kt[0, :, part], ds)
        dq = dq_part if dq is None else dq + dq_part
    return dq


def add_up(head, total, value):
    @pl.when(head == 0)
    def _():
        total[...] = value

    @pl.when(head > 0)
    def _():
        total[...] += value


def row_sums(columns):
    ones = jnp.ones((8, columns.shape[1]), bf16)
    return dot_nt(ones, columns)[0:1]


def times(a, x, flat):
    return dot_nt(a, x) if flat else dot(a, x)


def bwd_far(first, last, flat, qb, qt, do, dot_, kt, vt, w, x, *refs):
    if first:
        dxt_in = None
    else:
        dxt_in, refs = refs[0], refs[1:]
    dq_out, dw_out, dvs_out, dx_out, dxt_s, dkv_s = refs
    head = pl.program_id(0)
    dq_out[0] = score_grads(qb, qt, do, dot_, kt, vt, dkv_s)
    dxt = dot(w[0, :, WIDE:], dkv_s[...])
    dw_out[0, 0] = times(dkv_s[:HEAD_DIM, :], x[...], flat)
    dw_out[0, 1] = times(dkv_s[WIDE : WIDE + HEAD_DIM, :], x[...], flat)
    dvs_out[0] = jnp.broadcast_to(row_sums(dkv_s[WIDE:, :]), (8, WIDE))
    add_up(head, dxt_s, dxt if first else dxt + jnp.where(head == 0, 1.0, 0.0) * dxt_in[...])

    @pl.when(head == pl.num_programs(0) - 1)
    def _():
        if first and last:
            dx_out[...] = dxt_s[...].T.astype(bf16)
        else:
            dx_out[...] = dxt_s[...].astype(dx_out.dtype)


def near_head(
    flat, spot, head, step, qb, qt, do, dot_, kt, vt, w, x, xq, dq_far, dw_far, dvs_far,
    gmy_out, goth_out, sums_out, dkv_s,
):
    dqt = score_grads(qb, qt, do, dot_, kt, vt, dkv_s) + dq_far[0]
    dqt = (dqt * SCALE).astype(bf16)
    grads = (
        times(dqt[:HEAD_DIM, :], xq[...], flat),
        times(dkv_s[:HEAD_DIM, :], x[...], flat) + dw_far[0, 0],
        times(dkv_s[WIDE : WIDE + HEAD_DIM, :], x[...], flat) + dw_far[0, 1],
    )

    @pl.when(head % 2 == 0)
    def _():
        for j in range(3):
            gmy_out[0, j] = grads[j].astype(bf16)

    @pl.when(head % 2 == 1)
    def _():
        for j in range(3):
            goth_out[0, j] = grads[j].astype(bf16)

    @pl.when(step == 0)
    def _():
        sums_out[...] = jnp.zeros_like(sums_out)

    side = jnp.where(head < 2, spot[0], 1 - spot[0])
    piece = jnp.where(head % 2 == 0, spot[1], 1 - spot[1])
    quarter = 2 * side + piece
    put_row(sums_out, quarter, row_sums(dqt), WIDE)
    put_row(sums_out, 4 + quarter, row_sums(dkv_s[WIDE:, :]) + dvs_far[0, 0:1], WIDE)
    return dot(w[0, :, :WIDE], dqt), dot(w[0, :, WIDE:], dkv_s[...])


def bwd_own_second(
    spot, qb, qt, do, dot_, kt, vt, w, x, dq_far, dw_far, dvs_far,
    gmy_out, goth_out, sums_out, dx_out,
    dxt_s, dkv_s,
):
    head = pl.program_id(0)
    from_q, from_kv = near_head(
        False, spot, head, head, qb, qt, do, dot_, kt, vt, w, x, x, dq_far, dw_far, dvs_far,
        gmy_out, goth_out, sums_out, dkv_s,
    )
    add_up(head, dxt_s, from_q + from_kv)

    @pl.when(head == pl.num_programs(0) - 1)
    def _():
        dx_out[...] = dxt_s[...].T


def bwd_own_first(
    start, first, last, spot, qb, qt, do, dot_, kt, vt, w, x, xq, target, widen_grad,
    dq_far, dw_far, dvs_far, *refs,
):
    if not first:
        dxt_in, dxpt_in, sums_in, dxt_far, clip_t, vec = refs[:6]
        refs = refs[6:]
    gmy_out, goth_out, sums_out, refs = refs[0], refs[1], refs[2], refs[3:]
    if last:
        dx_out, dxt_s, dxpt_s, dkv_s = refs
    else:
        dxt_s, dxpt_s, dkv_s = refs
    step = pl.program_id(0)

    @pl.when(step == 0)
    def _():
        sums_out[...] = jnp.zeros_like(sums_out)
        if not first:
            sums_out[0:8] = sums_in[...]

    from_q, from_kv = near_head(
        True, spot, start + step, 1, qb, qt, do, dot_, kt, vt, w, x, xq, dq_far, dw_far, dvs_far,
        gmy_out, goth_out, sums_out, dkv_s,
    )

    @pl.when(step == 0)
    def _():
        dxt_s[...] = from_kv if first else from_kv + dxt_in[...]
        dxpt_s[...] = from_q + (widen_grad[...].T if first else dxpt_in[...])

    @pl.when(step > 0)
    def _():
        dxt_s[...] += from_kv
        dxpt_s[...] += from_q

    if not last:
        return

    @pl.when(step == pl.num_programs(0) - 1)
    def _():
        width = clip_t.shape[0]
        dxpt = dxpt_s[...].astype(bf16)
        gain = as_column(vec[NORM1 : NORM1 + 1, :width])
        dgain = jnp.zeros((width, 1), f32)
        dbeta = jnp.zeros((width, 1), f32)
        for at, size in chunks(clip_t.shape[1]):
            lane = lax.broadcasted_iota(jnp.int32, (target.shape[0], size), 1) + at
            hot = jnp.where(lane == target[...], 1.0, 0.0).astype(bf16)
            part = slice(at, at + size)
            grad = dxt_s[:, part] + dxt_far[:, part].astype(f32) + dot(dxpt, hot)
            xhat, rstd = norm_flat(clip_t[:, part].astype(f32))
            scaled = grad * gain
            dx_out[:, part] = rstd * (
                scaled
                - jnp.mean(scaled, axis=0, keepdims=True)
                - xhat * jnp.mean(scaled * xhat, axis=0, keepdims=True)
            )
            dgain = dgain + jnp.sum(grad * xhat, axis=1, keepdims=True)
            dbeta = dbeta + jnp.sum(grad, axis=1, keepdims=True)
        sums_out[8:9, :width] = as_row(dgain)
        sums_out[9:10, :width] = as_row(dbeta)


def back_ins(saved, parts, w, x):
    qb, qt, do, dot_ = saved
    kt, vt = parts
    rows, keys = qb.shape[1], kt.shape[2]
    flat = (1, WIDE, keys)
    rtall, rflat = (1, rows, WIDE), (1, WIDE, rows)
    return [
        (qb, rtall), (qt, rflat), (do, rtall), (dot_, rflat),
        (kt, flat), (vt, flat), (w, (1,) + w.shape[1:]), (x, None),
    ]


def attend_back_far(saved, parts, w, x, start, count, before=None):
    heads = w.shape[0]
    last = start + count == heads
    rows = saved[0].shape[1]
    keys, width = parts[0].shape[2], w.shape[1]
    ins = back_ins(saved, parts, w, x)
    if before is not None:
        ins += full(before)
    outs = [
        ((count, WIDE, rows), f32, (1, WIDE, rows)),
        ((count, 2, HEAD_DIM, width), f32, (1, 2, HEAD_DIM, width)),
        ((count, 8, WIDE), f32, (1, 8, WIDE)),
        ((keys, width), bf16, None)
        if count == heads
        else ((width, keys), bf16 if last else f32, None),
    ]
    scratch = [pltpu.VMEM((width, keys), f32), pltpu.VMEM((2 * WIDE, keys), bf16)]
    body = functools.partial(bwd_far, before is None, last, count != heads)
    return call(body, (count,), ins, outs, scratch, 14 if count == heads else 1, start)


def attend_back_own(spot, saved, parts, w, x, far):
    dq_far, dw_far, dvs_far = far
    heads = w.shape[0]
    rows = saved[0].shape[1]
    keys, width = parts[0].shape[2], w.shape[1]
    ins = [(spot, SMEM)] + back_ins(saved, parts, w, x)
    ins += [
        (dq_far, (1, WIDE, rows)),
        (dw_far, (1,) + dw_far.shape[1:]),
        (dvs_far, (1,) + dvs_far.shape[1:]),
    ]
    outs = [
        ((2, 3, HEAD_DIM, width), bf16, ("half", 1, 3, HEAD_DIM, width)),
        ((2, 3, HEAD_DIM, width), bf16, ("half", 1, 3, HEAD_DIM, width)),
        ((8, 3 * WIDE), f32, None),
        ((keys, width), f32, None),
    ]
    scratch = [pltpu.VMEM((width, keys), f32), pltpu.VMEM((2 * WIDE, keys), bf16)]
    return call(bwd_own_second, (heads,), ins, outs, scratch, 9 + keys / 105)


def attend_back_side(spot, saved, parts, w, x, far, pooled, start, before):
    dq_far, dw_far, dvs_far = far
    rows = saved[0].shape[1]
    keys, width = parts[0].shape[2], w.shape[1]
    whole = lambda a: (a, ("own", 1) + a.shape[1:])
    ins = [(spot, SMEM)] + back_ins(saved, parts, w, x) + full(*pooled)
    ins += [whole(dq_far), whole(dw_far), whole(dvs_far)]
    first = before is None
    if not first:
        ins += full(*before)
    outs = [
        ((1, 3, HEAD_DIM, width), bf16, None),
        ((1, 3, HEAD_DIM, width), bf16, None),
        ((8 if first else 16, 3 * WIDE), f32, None),
    ]
    scratch = [pltpu.VMEM((2 * WIDE, keys), bf16)]
    totals = [(width, keys), (width, rows)]
    if first:
        outs += [(shape, f32, None) for shape in totals]
    else:
        outs.append(((width, keys), f32, None))
        scratch = [pltpu.VMEM(shape, f32) for shape in totals] + scratch
    body = functools.partial(bwd_own_first, start, first, not first)
    return call(body, (2,), ins, outs, scratch, 20 if first else 0.3, start)


def pieces(spot):
    order = (spot[1], 1 - spot[1])
    return [(2 * side + p, side, p, order[p]) for side in (0, 1) for p in (0, 1)]


def put_row(ref, row, value, width):
    at = lax.broadcasted_iota(jnp.int32, (ref.shape[0], width), 0)
    ref[:, :width] = jnp.where(at == row, value, ref[:, :width])


def get_row(ref, row):
    at = lax.broadcasted_iota(jnp.int32, ref.shape, 0)
    return jnp.sum(jnp.where(at == row, ref[...], 0.0), axis=0, keepdims=True)


def absolute(spot, side, index):
    return 2 * (spot[0] if side == 0 else 1 - spot[0]) + index


def lanes_of(index, size):
    return pl.ds(pl.multiple_of(index * size, size), size)


def pad_heads(spot, wo_own, wo_far, wo_s):
    wo_s[...] = jnp.zeros_like(wo_s)
    for place, side, _, index in pieces(spot):
        wo_s[place, :HEAD_DIM, :] = (wo_own, wo_far)[side][lanes_of(index, HEAD_DIM), :]


def out_branch(attt, wo_s):
    total = None
    for head in range(attt.shape[0]):
        part = dot_tn(attt[head], wo_s[head])
        total = part if total is None else total + part
    return total


def sort_far(spot, mine, other, far_s):
    far_s[spot[1]] = mine[...]
    far_s[1 - spot[1]] = other[...]


def mid_first(
    spot, attt, wo_own, wo_far, xpt, widen, vec, up_own, down_own, up_far, down_far, pack_own, pack_far,
    mid_out, yt_out, act_out, slope_out, layer_out, x2_out, wo_s,
):
    pad_heads(spot, wo_own, wo_far, wo_s)
    size = up_own.shape[1] // 2
    branch = out_branch(attt, wo_s) + vec[OUT_B1 : OUT_B1 + 1]
    mid = (dot_tn(xpt[...], widen[...]) + vec[WIDEN_B : WIDEN_B + 1]) + branch
    mid_out[...] = mid
    xhat, _ = norm_stats(mid)
    y = (xhat * vec[MLP1 : MLP1 + 1] + vec[MLP1 + 1 : MLP1 + 2]).astype(bf16)
    yt_out[...] = flip(y)
    feed = None
    for place, side, _, index in pieces(spot):
        lanes = lanes_of(index, size)
        up = (up_own, up_far)[side][:, lanes]
        down = (down_own, down_far)[side][lanes, :]
        hidden = dot(y, up) + (pack_own, pack_far)[side][0:1, lanes]
        act, slope = gelu_both(hidden)
        act = act.astype(bf16)
        act_out[:, place * size : (place + 1) * size] = act
        slope_out[:, place * size : (place + 1) * size] = slope.astype(bf16)
        part = dot(act, down)
        feed = part if feed is None else feed + part
    layer = mid + feed + vec[DOWN_B1 : DOWN_B1 + 1]
    layer_out[...] = layer
    xhat, _ = norm_stats(layer)
    x2_out[...] = (xhat * vec[NORM2 : NORM2 + 1] + vec[NORM2 + 1 : NORM2 + 2]).astype(bf16)


def branch_back(gatt, attt, inv, wo_s, do_out, dot_out, g_outs, at):
    gatt_t = flip(gatt)
    for head in range(attt.shape[0]):
        do_t = dot(wo_s[head], gatt_t).astype(bf16).astype(f32)
        inner = jnp.sum(do_t * attt[head].astype(f32), axis=0, keepdims=True)
        scale = inv[head]
        do_t = do_t * scale
        row = lax.broadcasted_iota(jnp.int32, do_t.shape, 0)
        for offset, part in enumerate(three_parts(-inner * scale)):
            do_t = jnp.where(row == HEAD_DIM + offset, part, do_t)
        dot_out[head] = do_t.astype(bf16)
        do_out[head] = do_t.T.astype(bf16)
        grad = dot(attt[head, :HEAD_DIM, :], gatt).astype(bf16)
        g_outs[head % 2][head // 2, at : at + HEAD_DIM, :] = grad


def mid_second(
    spot, attt, inv, wo_own, wo_far, layer1, vec, up_own, down_own, mine, other,
    pack_own, pack_far, cot,
    y_out, dmid_out, do_out, dot_out, gmy_out, goth_out, small_out, wo_s, far_s,
):
    pad_heads(spot, wo_own, wo_far, wo_s)
    sort_far(spot, mine, other, far_s)
    size = up_own.shape[1] // 2
    width = cot.shape[1]
    g_outs = (gmy_out, goth_out)
    small_out[...] = jnp.zeros_like(small_out)
    mid = layer1[...] + (out_branch(attt, wo_s) + vec[OUT_B2 : OUT_B2 + 1])
    xhat, rstd = norm_stats(mid)
    gain = vec[MLP2 : MLP2 + 1]
    y = (xhat * gain + vec[MLP2 + 1 : MLP2 + 2]).astype(bf16)
    yt = flip(y)
    g_low = cot[...]
    g = g_low.astype(f32)
    gt = flip(g_low)
    feed = None
    dy = None
    for place, side, p, index in pieces(spot):
        lanes = lanes_of(index, size)
        up = (up_own, far_s.at[0])[side][:, lanes]
        down = (down_own, far_s.at[1])[side][:, lanes]
        hidden = dot(y, up) + (pack_own, pack_far)[side][1:2, lanes]
        act, slope = gelu_both(hidden)
        act = act.astype(bf16)
        dhid = (dot(g_low, down) * slope).astype(bf16)
        part = dot_nt(act, down)
        feed = part if feed is None else feed + part
        part = dot_nt(dhid, up)
        dy = part if dy is None else dy + part
        g_outs[p][side, :width, :] = dot(yt, dhid).astype(bf16)
        g_outs[p][side, width : 2 * width, :] = dot(gt, act).astype(bf16)
        row = 4 + absolute(spot, side, index)
        put_row(small_out, row, jnp.sum(dhid.astype(f32), axis=0, keepdims=True), size)
    y_out[...] = (mid + feed + vec[DOWN_B2 : DOWN_B2 + 1]).astype(bf16)
    back, dgain, dbeta = norm_back(xhat, rstd, gain, dy)
    dmid = g + back
    dmid_out[...] = dmid
    small_out[0:1] = jnp.sum(g, axis=0, keepdims=True)
    small_out[1:2] = dgain
    small_out[2:3] = dbeta
    small_out[3:4] = jnp.sum(dmid, axis=0, keepdims=True)
    branch_back(dmid.astype(bf16), attt, inv, wo_s, do_out, dot_out, g_outs, 2 * width)


def mid_back(
    spot, dx_own, dx_far, layer1, vec, dmid2, act, slope, yt, mid,
    up_own, down_own, up_far, down_far, wo_own, wo_far, attt, inv, xpt, widen,
    do_out, dot_out, gmy_out, goth_out, wgrad_out, small_out, wo_s, widen_s,
):
    pad_heads(spot, wo_own, wo_far, wo_s)
    size = up_own.shape[1] // 2
    width = layer1.shape[1]
    g_outs = (gmy_out, goth_out)
    small_out[...] = jnp.zeros_like(small_out)
    xhat, rstd = norm_stats(layer1[...])
    back, dgain2, dbeta2 = norm_back(
        xhat, rstd, vec[NORM2 : NORM2 + 1], dx_own[...] + dx_far[...].astype(f32)
    )
    g = dmid2[...] + back
    g_low = g.astype(bf16)
    gt = flip(g_low)
    dy = None
    for place, side, p, index in pieces(spot):
        lanes = lanes_of(index, size)
        here = slice(place * size, (place + 1) * size)
        up = (up_own, up_far)[side][:, lanes]
        down = (down_own, down_far)[side][lanes, :]
        dhid = (dot_nt(g_low, down) * slope[:, here].astype(f32)).astype(bf16)
        part = dot_nt(dhid, up)
        dy = part if dy is None else dy + part
        g_outs[p][side, :width, :] = dot(yt[...], dhid).astype(bf16)
        g_outs[p][side, width : 2 * width, :] = dot(gt, act[:, here]).astype(bf16)
        row = 4 + absolute(spot, side, index)
        put_row(small_out, row, jnp.sum(dhid.astype(f32), axis=0, keepdims=True), size)
    xhat, rstd = norm_stats(mid[...])
    back, dgain, dbeta = norm_back(xhat, rstd, vec[MLP1 : MLP1 + 1], dy)
    dmid = g + back
    small_out[0:1] = jnp.sum(g, axis=0, keepdims=True)
    small_out[1:2] = dgain
    small_out[2:3] = dbeta
    small_out[3:4] = jnp.sum(dmid, axis=0, keepdims=True)
    small_out[8:9] = dgain2
    small_out[9:10] = dbeta2
    gatt = dmid.astype(bf16)
    branch_back(gatt, attt, inv, wo_s, do_out, dot_out, g_outs, 2 * width)
    widen_s[...] = dot(xpt[...], gatt)
    rows = widen_s.shape[0] // 4
    at = 2 * width + HEAD_DIM
    for place, side, p, index in pieces(spot):
        quarter = widen_s[lanes_of(absolute(spot, side, index), rows), :]
        g_outs[p][side, at : at + rows, :] = quarter.astype(bf16)
    wgrad_out[...] = dot_nt(gatt, widen[...])


def finish_mlp(spot, mine, other, *refs):
    if len(refs) == 3:
        widen_far, widen_out = None, None
        up_out, down_out, out_out = refs
    else:
        widen_far, up_out, down_out, out_out, widen_out = refs
    width = up_out.shape[0]
    size = up_out.shape[1] // 2
    for part, index in ((mine, spot[1]), (other, 1 - spot[1])):
        lanes = lanes_of(index, size)
        up_out[:, lanes] = part[:width, :].astype(f32)
        down_out[lanes, :] = part[width : 2 * width, :].astype(f32).T
        out_out[lanes_of(index, HEAD_DIM), :] = part[2 * width : 2 * width + HEAD_DIM, :].astype(f32)
    if widen_out is not None:
        rows = widen_out.shape[0] // 4
        at = 2 * width + HEAD_DIM
        for side in (0, 1):
            for p, index in ((0, spot[1]), (1, 1 - spot[1])):
                if side == 0:
                    value = (mine, other)[p][at : at + rows, :]
                else:
                    value = widen_far[p]
                widen_out[lanes_of(absolute(spot, side, index), rows), :] = value.astype(f32)


def finish_qkv(turned, spot, mine, other, out, both_s):
    for j in range(3):
        for part, index in ((mine, spot[1]), (other, 1 - spot[1])):
            both_s[lanes_of(index, HEAD_DIM), :] = part[j].astype(f32)
        out[j] = both_s[...].T if turned else both_s[...]


def finish_small(spot, small, *outs):
    (n1g, n1b, wb, qvb1, ob1, m1g, m1b, ub1, db1, n2g, n2b, qvb2, ob2, m2g, m2b, ub2, db2) = outs
    first = 2 * spot[0]

    def put(out, row):
        out[...] = small[row, : out.shape[0]]

    def put_layer(base, sums, ub, qvb):
        size = ub.shape[0] // 2
        for p in (0, 1):
            ub[p * size : (p + 1) * size] = get_row(small, base + 4 + first + p)[0]
            for j in (0, 1):
                row = get_row(small, sums + 4 * j + first + p)
                qvb[j : j + 1, p * HEAD_DIM : (p + 1) * HEAD_DIM] = row[:, :HEAD_DIM]

    put(db2, 0)
    put(m2g, 1)
    put(m2b, 2)
    put(ob2, 3)
    put(db1, 16)
    put(m1g, 17)
    put(m1b, 18)
    put(ob1, 19)
    put(wb, 19)
    put(n2g, 24)
    put(n2b, 25)
    put(n1g, 48)
    put(n1b, 49)
    put_layer(0, 32, ub2, qvb2)
    put_layer(16, 40, ub1, qvb1)


def swap(x):
    return lax.ppermute(x, "head", [(0, 1), (1, 0)])


def core_swap(x):
    return lax.ppermute(x, "core", [(0, 1), (1, 0)])


def add_low(a, b):
    return (a.astype(f32) + b.astype(f32)).astype(bf16)


def tie(later, dep):
    return lax.optimization_barrier((later, dep))


def exchange(x, axis, bit):
    other = lax.ppermute(x, axis, [(i, i ^ bit) for i in range(lax.axis_size(axis))])
    return (x.astype(f32) + other.astype(f32)).astype(x.dtype)


def exchange_bits(axis):
    bits = [1 << k for k in range((lax.axis_size(axis) - 1).bit_length())]
    return bits[1:] + bits[:1]


def shards(
    clip_in,
    frame_count,
    frame_mask,
    pool_index,
    first_norm_gain,
    first_norm_bias,
    first_widen_weight,
    first_widen_bias,
    first_qkv_weight,
    first_qv_bias,
    first_out_weight,
    first_out_bias,
    first_mlp_gain,
    first_mlp_bias,
    first_up_weight,
    first_up_bias,
    first_down_weight,
    first_down_bias,
    second_norm_gain,
    second_norm_bias,
    second_qkv_weight,
    second_qv_bias,
    second_out_weight,
    second_out_bias,
    second_mlp_gain,
    second_mlp_bias,
    second_up_weight,
    second_up_bias,
    second_down_weight,
    second_down_bias,
    cotangent,
):
    clip_t = clip_in[0].T
    cot = cotangent[0]
    side = lax.axis_index("head")
    spot = jnp.stack([side, lax.axis_index("core")]).astype(jnp.int32)
    scalars = [(spot, SMEM), (frame_count, SMEM), (frame_mask, SMEM)]
    place = (spot, SMEM)
    width1, keys1 = clip_t.shape
    rows, dim = cot.shape
    n_up = first_up_bias.shape[0]
    hidden = 2 * n_up
    heads = 4
    out_rows = 2 * dim + HEAD_DIM
    half_up = n_up // 2

    qkv1 = jnp.swapaxes(first_qkv_weight, 0, 1)
    qkv2 = jnp.transpose(second_qkv_weight, (1, 2, 0))
    qv_row = jnp.concatenate([first_qv_bias.reshape(-1), second_qv_bias.reshape(-1)])
    pack = jnp.stack([first_up_bias, second_up_bias, qv_row])
    far_qkv1 = swap(qkv1)
    far_pack = swap(pack)
    clip_send, (far_qkv1, far_pack) = tie(clip_t, (far_qkv1, far_pack))
    far_clip = swap(clip_send)
    down2 = second_down_weight.T
    first_core = lax.axis_index("core") == 0
    send2 = jnp.where(first_core, second_up_weight, down2)

    def wide(v):
        return jnp.pad(v, (0, dim - v.shape[0]))

    vec = jnp.stack(
        [
            wide(first_norm_gain), wide(first_norm_bias), first_widen_bias, first_out_bias,
            first_mlp_gain, first_mlp_bias, first_down_bias, second_norm_gain, second_norm_bias,
            second_out_bias, second_mlp_gain, second_mlp_bias, second_down_bias,
        ]
    )

    picks = lax.dynamic_slice_in_dim(pool_index[0], side * rows, rows, 0)
    token = jnp.arange(rows, dtype=jnp.int32)
    frame, cell = token // (SIDE * SIDE), token % (SIDE * SIDE)
    line = 2 * (cell // SIDE) + picks // 2
    column = 2 * (cell % SIDE) + picks % 2
    target = (frame * (4 * SIDE * SIDE) + line * (2 * SIDE) + column)[:, None]

    x1t, x1pt, w1, w1t, b1, kt1, vt1, q1, qt1, o1, m1 = attend_own(
        scalars, clip_t, (qkv1, far_qkv1), (pack, far_pack), vec, target
    )
    mlp1, m1 = tie((first_out_weight, first_up_weight, first_down_weight), m1)
    far_out1, far_up1, far_down1 = [swap(w) for w in mlp1]
    x1ft, kt1f, vt1f, attt1, inv1, qb1 = attend_far(
        scalars, far_clip, w1t, b1, q1, qt1, o1, m1, vec
    )
    late, attt1 = tie((qkv2, second_out_weight), attt1)
    far_qkv2, far_out2 = [swap(w) for w in late]
    send2, far_qkv2 = tie(send2, far_qkv2)
    mine2 = swap(send2)
    mid1, yt1, act1, slope1, layer1, x2 = call(
        mid_first,
        (),
        [place]
        + full(
            attt1, first_out_weight, far_out1, x1pt, first_widen_weight, vec,
            first_up_weight, first_down_weight, far_up1, far_down1, pack, far_pack,
        ),
        [
            ((rows, dim), f32, None),
            ((dim, rows), bf16, None),
            ((rows, hidden), bf16, None),
            ((rows, hidden), bf16, None),
            ((rows, dim), f32, None),
            ((rows, dim), bf16, None),
        ],
        [pltpu.VMEM((heads, WIDE, dim), bf16)],
        11,
    )

    x2f = swap(x2)
    w2, w2t, b2, kt2, vt2, q2, qt2, o2, m2 = attend_own(scalars, x2, (qkv2, far_qkv2), (pack, far_pack))
    far_out2, m2 = tie(far_out2, m2)
    kt2f, vt2f, attt2, inv2, qb2 = attend_far(scalars, x2f, w2t, b2, q2, qt2, o2, m2)
    mine2, attt2 = tie(mine2, attt2)
    other2 = core_swap(mine2)
    out, dmid2, do2, dot2, gmy2, goth2, small2 = call(
        mid_second,
        (),
        [place]
        + full(
            attt2, inv2, second_out_weight, far_out2, layer1, vec, second_up_weight, down2,
            mine2, other2, pack, far_pack, cot,
        ),
        [
            ((rows, dim), bf16, None),
            ((rows, dim), f32, None),
            ((heads, rows, WIDE), bf16, None),
            ((heads, WIDE, rows), bf16, None),
            ((2, out_rows, half_up), bf16, None),
            ((2, out_rows, half_up), bf16, None),
            ((16, dim), f32, None),
        ],
        [pltpu.VMEM((heads, WIDE, dim), bf16), pltpu.VMEM((2, dim, n_up), bf16)],
        18,
    )

    got_a = core_swap(goth2)
    saved2 = (qb2, qt2, do2, dot2)
    dq2f, dw2f, dvs2f, dx2_send = attend_back_far(saved2, (kt2f, vt2f), w2, x2f, 0, heads)
    dx2_far = swap(dx2_send)
    near_a, away_a = add_low(gmy2[0], got_a[0]), add_low(gmy2[1], got_a[1])
    (near_a, away_a), dq2f = tie((near_a, away_a), dq2f)
    hmy2, hoth2, sums2, dx2 = attend_back_own(
        spot, saved2, (kt2, vt2), w2, x2, (dq2f, dw2f, dvs2f)
    )
    (away_a, hoth2), dx2 = tie((away_a, hoth2), dx2)
    got_a2 = swap(away_a)
    got_h2 = core_swap(hoth2)

    widen_rows = width1 // 4
    do1, dot1, gmy1, goth1, wgrad, small1 = call(
        mid_back,
        (),
        [place]
        + full(
            dx2, dx2_far, layer1, vec, dmid2, act1, slope1, yt1, mid1,
            first_up_weight, first_down_weight, far_up1, far_down1,
            first_out_weight, far_out1, attt1, inv1, x1pt, first_widen_weight,
        ),
        [
            ((heads, rows, WIDE), bf16, None),
            ((heads, WIDE, rows), bf16, None),
            ((2, out_rows + widen_rows, half_up), bf16, None),
            ((2, out_rows + widen_rows, half_up), bf16, None),
            ((rows, width1), f32, None),
            ((16, dim), f32, None),
        ],
        [
            pltpu.VMEM((heads, WIDE, dim), bf16),
            pltpu.VMEM((width1, dim), f32),
        ],
        17,
    )
    near_h, away_h = add_low(hmy2[0], got_h2[0]), add_low(hmy2[1], got_h2[1])
    total_a = add_low(near_a, got_a2)
    (total_a, near_h, away_h, goth1), do1 = tie((total_a, near_h, away_h, goth1), do1)
    bits = exchange_bits("outer")
    next_a = exchange(total_a, "outer", bits[0])
    got_b = core_swap(goth1)
    got_h = swap(away_h)

    saved1 = (qb1, qt1, do1, dot1)
    two = heads // 2
    *own_far, dx1_part = attend_back_far(saved1, (kt1f, vt1f), w1, x1ft, 0, two)
    near_b, away_b = add_low(gmy1[0], got_b[0]), add_low(gmy1[1], got_b[1])
    total_h = add_low(near_h, got_h)
    (near_b, away_b, total_h, next_a), dx1_part = tie((near_b, away_b, total_h, next_a), dx1_part)
    got_b2 = swap(away_b)
    next_a = exchange(next_a, "outer", bits[1])
    *far_far, dx1_send = attend_back_far(saved1, (kt1f, vt1f), w1, x1ft, two, two, dx1_part)
    dx1_far = swap(dx1_send)
    total_b = add_low(near_b, got_b2)
    (next_a, total_b, total_h), far_far = tie((next_a, total_b, total_h), far_far)
    next_b = exchange(total_b, "outer", bits[0])
    next_h = exchange(total_h, "outer", bits[0])
    for bit in bits[2:]:
        next_a = exchange(next_a, "outer", bit)
    pooled = (x1pt, target, wgrad)
    gmy_f, goth_f, sums1f, *totals = attend_back_side(
        spot, saved1, (kt1, vt1), w1, x1t, far_far, pooled, two, None
    )
    (dx1_far, goth_f, total_a, next_b, next_h), own_far = tie(
        (dx1_far, goth_f, next_a, next_b, next_h), own_far
    )
    next_b = exchange(next_b, "outer", bits[1])
    for bit in bits[2:]:
        next_h = exchange(next_h, "outer", bit)
    other_a = core_swap(total_a)
    got_cf = core_swap(goth_f)
    gmy_o, goth_o, sums1, grad_in = attend_back_side(
        spot, saved1, (kt1, vt1), w1, x1t, own_far, pooled, 0, (*totals, sums1f, dx1_far, clip_t, vec)
    )

    (next_b, next_h), goth_o = tie((next_b, next_h), goth_o)
    total_h = exchange(next_h, "outer", bits[1])
    total_b = next_b
    for bit in bits[2:]:
        total_b = exchange(total_b, "outer", bit)
    small = jnp.concatenate([small2, small1, sums2, sums1])
    got_co = core_swap(goth_o)
    got_c2 = swap(add_low(gmy_f[0], got_cf[0]))
    total_c = add_low(gmy_o[0], got_co[0])
    total_c, small = tie(add_low(total_c, got_c2), exchange(small, "core", 1))
    (total_c, small), total_h = tie((total_c, small), total_h)
    total_c, small = tie(exchange(total_c, "outer", bits[0]), exchange(small, "head", 1))
    (total_c, small), total_b = tie((total_c, small), total_b)
    other_b, other_h = core_swap(total_b), core_swap(total_h)
    total_c = exchange(total_c, "outer", bits[1])
    small = exchange(small, "outer", bits[0])
    (total_c, small), (other_b, other_h) = tie((total_c, small), (other_b, other_h))
    widen_far = swap(jnp.stack([total_b[out_rows:], other_b[out_rows:]]))
    for bit in bits[2:]:
        total_c = exchange(total_c, "outer", bit)
    small = exchange(small, "outer", bits[1])
    (total_c, small), widen_far = tie((total_c, small), widen_far)
    other_c = core_swap(total_c)
    for bit in bits[2:]:
        small = exchange(small, "outer", bit)

    def qkv_form(mine, other, turned):
        width = mine.shape[2]
        shape = (2 * HEAD_DIM, width)
        (grad,) = call(
            functools.partial(finish_qkv, turned),
            (),
            [place] + full(mine, other),
            [((3,) + (shape[::-1] if turned else shape), f32, None)],
            [pltpu.VMEM(shape, f32)],
            2,
        )
        return jnp.transpose(grad, (1, 0, 2) if turned else (2, 0, 1))

    mlp_outs = [
        ((dim, n_up), f32, None),
        ((n_up, dim), f32, None),
        ((2 * HEAD_DIM, dim), f32, None),
    ]
    gup2, gdn2, gout2 = call(
        finish_mlp, (), [place] + full(total_a, other_a), mlp_outs, [], 3
    )
    gup1, gdn1, gout1, gwiden = call(
        finish_mlp,
        (),
        [place] + full(total_b, other_b, widen_far),
        mlp_outs + [((width1, dim), f32, None)],
        [],
        3,
    )
    gqkv2 = qkv_form(total_h, other_h, False)
    gqkv1 = qkv_form(total_c, other_c, True)
    vector = ((dim,), f32, None)
    thin = ((width1,), f32, None)
    layer_vectors = [((2, 2 * HEAD_DIM), f32, None)] + [vector] * 3 + [((n_up,), f32, None), vector]
    (n1g, n1b, wb, qvb1, ob1, m1g, m1b, ub1, db1, n2g, n2b, qvb2, ob2, m2g, m2b, ub2, db2) = call(
        finish_small,
        (),
        [place] + full(small),
        [thin, thin, vector] + layer_vectors + [vector, vector] + layer_vectors,
        [],
        2,
    )
    return (
        out[None], grad_in.T[None],
        n1g, n1b, gwiden, wb, gqkv1, qvb1, gout1, ob1, m1g, m1b, gup1, ub1, gdn1, db1,
        n2g, n2b, gqkv2, qvb2, gout2, ob2, m2g, m2b, gup2, ub2, gdn2, db2,
    )


def solution(mesh):
    in_specs = (
        P(BATCH, "head", None),
        P(BATCH),
        P(BATCH, None),
        P(BATCH, None),
        P(),
        P(),
        P(),
        P(),
        P(None, None, "head"),
        P(None, "head"),
        P("head", None),
        P(),
        P(),
        P(),
        P(None, "head"),
        P("head"),
        P("head", None),
        P(),
        P(),
        P(),
        P(None, None, "head"),
        P(None, "head"),
        P("head", None),
        P(),
        P(),
        P(),
        P(None, "head"),
        P("head"),
        P("head", None),
        P(),
        P(BATCH, "head", None),
    )
    out_specs = (
        P(BATCH, "head", None),
        P(BATCH, "head", None),
        P(),
        P(),
        P(),
        P(),
        P(None, None, "head"),
        P(None, "head"),
        P("head", None),
        P(),
        P(),
        P(),
        P(None, "head"),
        P("head"),
        P("head", None),
        P(),
        P(),
        P(),
        P(None, None, "head"),
        P(None, "head"),
        P("head", None),
        P(),
        P(),
        P(),
        P(None, "head"),
        P("head"),
        P("head", None),
        P(),
    )
    outer = mesh.shape["batch"] // 2
    split = Mesh(
        mesh.devices.reshape(outer, 2, mesh.shape["head"]), ("outer", "core", "head")
    )
    return jax.shard_map(shards, mesh=split, in_specs=in_specs, out_specs=out_specs, check_vma=False)
```

```python
import functools

import jax
import jax.numpy as jnp
from jax import lax
from jax.experimental import pallas as pl
from jax.experimental.pallas import tpu as pltpu
from jax.sharding import Mesh, PartitionSpec as P

HEAD_DIM = 96
WIDE = 128
SIDE = 14
DEAD = -1e30
LOG2E = 1.4426950408889634
LN2 = 0.6931471805599453
SCALE = HEAD_DIM ** (-0.5)
EPS = 1e-06
CHUNK = 256
SAFE = 60.0
BATCH = ("outer", "core")

bf16 = jnp.bfloat16
f32 = jnp.float32


def dot(a, b):
    return jnp.dot(a, b, preferred_element_type=f32)


def dot_nt(a, b):
    return lax.dot_general(a, b, (((1,), (1,)), ((), ())), preferred_element_type=f32)


def eye(size):
    row = lax.broadcasted_iota(jnp.int32, (size, size), 0)
    return jnp.where(row == lax.broadcasted_iota(jnp.int32, (size, size), 1), 1.0, 0.0).astype(bf16)


def flip(a):
    return dot_nt(eye(a.shape[1]), a).astype(bf16)


def dot_tn(a, b):
    return lax.dot_general(a, b, (((0,), (0,)), ((), ())), preferred_element_type=f32)


def chunks(total):
    return [(start, min(CHUNK, total - start)) for start in range(0, total, CHUNK)]


def norm_stats(v):
    centered = v - jnp.mean(v, axis=-1, keepdims=True)
    rstd = lax.rsqrt(jnp.mean(centered * centered, axis=-1, keepdims=True) + EPS)
    return centered * rstd, rstd


def norm_back(xhat, rstd, gain, grad):
    scaled = grad * gain
    back = rstd * (
        scaled
        - jnp.mean(scaled, axis=-1, keepdims=True)
        - xhat * jnp.mean(scaled * xhat, axis=-1, keepdims=True)
    )
    return (
        back,
        jnp.sum(grad * xhat, axis=0, keepdims=True),
        jnp.sum(grad, axis=0, keepdims=True),
    )


def norm_flat(v):
    centered = v - jnp.mean(v, axis=0, keepdims=True)
    rstd = lax.rsqrt(jnp.mean(centered * centered, axis=0, keepdims=True) + EPS)
    return centered * rstd, rstd


def as_column(row):
    return jnp.broadcast_to(row, (WIDE, row.shape[1])).T[:, :1]


def as_row(column):
    return jnp.broadcast_to(column, (column.shape[0], WIDE)).T[:1]


def three_parts(v):
    high = v.astype(bf16).astype(f32)
    rest = v - high
    middle = rest.astype(bf16).astype(f32)
    return high, middle, rest - middle


def with_columns(block, first, column):
    lane = lax.broadcasted_iota(jnp.int32, block.shape, 1)
    for offset, part in enumerate(three_parts(column)):
        block = jnp.where(lane == first + offset, part, block)
    return block


def gelu_both(u):
    cdf = 0.5 + 0.5 * lax.erf(u * 0.7071067811865476)
    return u * cdf, cdf + u * (jnp.exp(-0.5 * u * u) * 0.3989422804014327)


NORM1, WIDEN_B, OUT_B1, MLP1, DOWN_B1, NORM2, OUT_B2, MLP2, DOWN_B2 = 0, 2, 3, 4, 6, 7, 9, 10, 12
SMEM = "smem"


def call(body, grid, ins, outs, scratch, micros, offset=0, megabytes=56):
    def spec(shape, block):
        if block == SMEM:
            return pl.BlockSpec(memory_space=pltpu.SMEM)
        if block is None:
            zeros = (0,) * len(shape)
            return pl.BlockSpec(tuple(shape), lambda *_: zeros)
        if block[0] == "own":
            rest = (0,) * (len(shape) - 1)
            return pl.BlockSpec(tuple(block[1:]), lambda i, *_: (i,) + rest)
        if block[0] == "half":
            rest = (0,) * (len(shape) - 1)
            return pl.BlockSpec(tuple(block[1:]), lambda i, *_: ((i + offset) // 2,) + rest)
        rest = (0,) * (len(shape) - 1)
        return pl.BlockSpec(tuple(block), lambda i, *_: (i + offset,) + rest)

    def out_spec(shape, block):
        if block is None or block[0] == "half":
            return spec(shape, block)
        rest = (0,) * (len(shape) - 1)
        return pl.BlockSpec(tuple(block), lambda i, *_: (i,) + rest)

    return pl.pallas_call(
        body,
        grid=grid,
        in_specs=[spec(a.shape, b) for a, b in ins],
        out_specs=[out_spec(s, b) for s, _, b in outs],
        out_shape=[jax.ShapeDtypeStruct(s, d) for s, d, _ in outs],
        scratch_shapes=scratch,
        cost_estimate=pl.CostEstimate(
            flops=int(micros * 1.15e9), transcendentals=0, bytes_accessed=int(micros * 3.69e6)
        ),
        compiler_params=pltpu.CompilerParams(
            dimension_semantics=("arbitrary",) * len(grid),
            vmem_limit_bytes=megabytes << 20,
        ),
    )(*[a for a, _ in ins])


def full(*arrays):
    return [(a, None) for a in arrays]


def dead_keys(spot, count, marks, keys, far):
    half = marks.shape[1] // 2
    each = keys // half
    first = (1 - spot[0] if far else spot[0]) * half
    lane = lax.broadcasted_iota(jnp.int32, (1, keys), 1)
    row = jnp.zeros((1, keys), f32)
    for f in range(half):
        dead = (first + f >= count[0]) | (marks[0, first + f] != 1)
        row = jnp.where((lane >= f * each) & (lane < (f + 1) * each), jnp.where(dead, DEAD, 0.0), row)
    return row


def head_forms(spot, w_own, w_far, pack_own, pack_far, layer, w_out, wt_out, b_out):
    first = spot[1] == 0
    filled = wt_out if layer else w_out
    filled[...] = jnp.zeros_like(filled)
    b_out[...] = jnp.zeros_like(b_out)
    for side, (w, pack) in enumerate(((w_own, pack_own), (w_far, pack_far))):
        for j in range(3):
            place = slice(j * WIDE, j * WIDE + HEAD_DIM)
            if layer:
                low, high = w[j, :HEAD_DIM].astype(f32), w[j, HEAD_DIM:].astype(f32)
                wt_out[2 * side, place] = jnp.where(first, low, high).astype(bf16)
                wt_out[2 * side + 1, place] = jnp.where(first, high, low).astype(bf16)
            else:
                low, high = w[j, :, :HEAD_DIM].astype(f32), w[j, :, HEAD_DIM:].astype(f32)
                w_out[2 * side, :, place] = jnp.where(first, low, high).astype(bf16)
                w_out[2 * side + 1, :, place] = jnp.where(first, high, low).astype(bf16)
        for j in range(2):
            start = (2 * layer + j) * 2 * HEAD_DIM
            low = pack[2:3, start : start + HEAD_DIM]
            high = pack[2:3, start + HEAD_DIM : start + 2 * HEAD_DIM]
            b_out[2 * side, j : j + 1, :HEAD_DIM] = jnp.where(first, low, high)
            b_out[2 * side + 1, j : j + 1, :HEAD_DIM] = jnp.where(first, high, low)
    for head in range(w_out.shape[0]):
        if layer:
            w_out[head] = flip(wt_out[head])
        else:
            wt_out[head] = flip(w_out[head])


def project_keys(x_t, w_t, b, mask, kt_out, vt_out):
    both = dot(w_t[WIDE:], x_t)
    k_t, v_t = both[:WIDE], both[WIDE:]
    key_bound = jnp.max(jnp.sum(k_t * k_t, axis=0, keepdims=True))
    row = lax.broadcasted_iota(jnp.int32, k_t.shape, 0)
    k_t = jnp.where(row == HEAD_DIM, mask, k_t)
    k_t = jnp.where((row > HEAD_DIM) & (row < HEAD_DIM + 4), 1.0, k_t)
    kt_out[0] = k_t.astype(bf16)
    column = as_column(b[1:2])
    row = lax.broadcasted_iota(jnp.int32, column.shape, 0)
    column = jnp.where((row >= HEAD_DIM) & (row < HEAD_DIM + 3), 1.0, column)
    vt_out[0] = (v_t + column).astype(bf16)
    return key_bound


def soft_part(q_t_ref, q, key_bound, kt_ref, vt_ref, s_ref, o_ref, m_ref):
    total = kt_ref.shape[2]
    q_wide = q_t_ref[0, :HEAD_DIM, :].astype(f32)
    bound = jnp.max(jnp.sum(q_wide * q_wide, axis=0, keepdims=True)) * key_bound
    safe = bound < SAFE * SAFE

    @pl.when(safe)
    def _():
        parts = [slice(start, start + size) for start, size in chunks(total)]
        out = s = p = None
        for i in range(len(parts) + 2):
            s_next = dot(q, kt_ref[0, :, parts[i]]) if i < len(parts) else None
            p_next = None if s is None else jnp.exp2(s).astype(bf16)
            if p is not None:
                o = dot_nt(vt_ref[0, :, parts[i - 2]], p)
                out = o if out is None else out + o
            s, p = s_next, p_next
        o_ref[0] = out
        m_ref[0] = jnp.zeros_like(m_ref[0])

    @pl.when(jnp.logical_not(safe))
    def _():
        peak = None
        for start, size in chunks(total):
            s = dot(q, kt_ref[0, :, start : start + size])
            s_ref[:, start : start + size] = s
            top = jnp.max(s, axis=1, keepdims=True)
            peak = top if peak is None else jnp.maximum(peak, top)
        out = None
        for start, size in chunks(total):
            part = slice(start, start + size)
            p = jnp.exp2(s_ref[:, part] - peak).astype(bf16)
            o = dot_nt(vt_ref[0, :, part], p)
            out = o if out is None else out + o
        o_ref[0] = out
        m_ref[0] = as_row(peak)


def queries(q, rows_t, w_t, b, q_out, qt_out):
    q = (q + b[0:1]) * (SCALE * LOG2E)
    lane = lax.broadcasted_iota(jnp.int32, q.shape, 1)
    q = jnp.where(lane == HEAD_DIM, 1.0, q).astype(bf16)
    q_out[0] = q
    qt_out[0] = ((dot(w_t[:WIDE], rows_t) + as_column(b[0:1])) * (SCALE * LOG2E)).astype(bf16)
    return q


def input_norm(clip_t, vec):
    width = clip_t.shape[0]
    xhat, _ = norm_flat(clip_t[...].astype(f32))
    gain, beta = vec[NORM1 : NORM1 + 1, :width], vec[NORM1 + 1 : NORM1 + 2, :width]
    return (xhat * as_column(gain) + as_column(beta)).astype(bf16)


def fwd_own_first(
    spot, count, marks, clip_t, vec, target, w_own, w_far, pack_own, pack_far,
    xt_out, xpt_out, w_out, wt_out, b_out, kt_out, vt_out, q_out, qt_out, o_out, m_out,
    s_s,
):
    head = pl.program_id(0)

    @pl.when(head == 0)
    def _():
        head_forms(spot, w_own, w_far, pack_own, pack_far, 0, w_out, wt_out, b_out)
        xt_out[...] = input_norm(clip_t, vec)
        picked = None
        for start, size in chunks(clip_t.shape[1]):
            lane = lax.broadcasted_iota(jnp.int32, (target.shape[0], size), 1) + start
            hot = jnp.where(lane == target[...], 1.0, 0.0).astype(bf16)
            part = dot_nt(xt_out[:, start : start + size], hot)
            picked = part if picked is None else picked + part
        xpt_out[...] = picked.astype(bf16)

    mask = dead_keys(spot, count, marks, clip_t.shape[1], False)
    w_t, b = wt_out[head], b_out[head]
    bound = project_keys(xt_out[...], w_t, b, mask, kt_out, vt_out)
    q = dot_tn(xpt_out[...], w_out[head, :, :WIDE])
    q = queries(q, xpt_out[...], w_t, b, q_out, qt_out)
    soft_part(qt_out, q, bound, kt_out, vt_out, s_s, o_out, m_out)


def fwd_own_second(
    spot, count, marks, x, w_own, w_far, pack_own, pack_far,
    w_out, wt_out, b_out, kt_out, vt_out, q_out, qt_out, o_out, m_out,
    xt_s, s_s,
):
    head = pl.program_id(0)

    @pl.when(head == 0)
    def _():
        head_forms(spot, w_own, w_far, pack_own, pack_far, 1, w_out, wt_out, b_out)
        xt_s[...] = flip(x[...])

    mask = dead_keys(spot, count, marks, x.shape[0], False)
    w_t, b = wt_out[head], b_out[head]
    bound = project_keys(xt_s[...], w_t, b, mask, kt_out, vt_out)
    q = queries(dot(x[...], w_out[head, :, :WIDE]), xt_s[...], w_t, b, q_out, qt_out)
    soft_part(qt_out, q, bound, kt_out, vt_out, s_s, o_out, m_out)


def finish_head(q, o1, m1, o2, m2, attt_out, inv_out, qb_out):
    peak = jnp.maximum(m1, m2)
    o = o1 * jnp.exp2(m1 - peak) + o2 * jnp.exp2(m2 - peak)
    inv = 1.0 / o[HEAD_DIM : HEAD_DIM + 1]
    attt_out[0] = (o * inv).astype(bf16)
    inv_out[0] = inv
    qb_out[0] = q

    @pl.when(jnp.max(jnp.abs(peak)) > 0.0)
    def _():
        qb_out[0] = with_columns(q.astype(f32), HEAD_DIM + 1, -as_column(peak)).astype(bf16)


def fwd_far_first(
    spot, count, marks, clip_t, vec, w_t, b, q, qt, o1, m1,
    xt_out, kt_out, vt_out, attt_out, inv_out, qb_out,
    s_s, o_s, m_s,
):
    @pl.when(pl.program_id(0) == 0)
    def _():
        xt_out[...] = input_norm(clip_t, vec)

    mask = dead_keys(spot, count, marks, clip_t.shape[1], True)
    bound = project_keys(xt_out[...], w_t[0], b[0], mask, kt_out, vt_out)
    soft_part(qt, q[0], bound, kt_out, vt_out, s_s, o_s, m_s)
    finish_head(q[0], o1[0], m1[0], o_s[0], m_s[0], attt_out, inv_out, qb_out)


def fwd_far_second(
    spot, count, marks, x, w_t, b, q, qt, o1, m1,
    kt_out, vt_out, attt_out, inv_out, qb_out,
    s_s, o_s, m_s, xt_s,
):
    @pl.when(pl.program_id(0) == 0)
    def _():
        xt_s[...] = flip(x[...])

    mask = dead_keys(spot, count, marks, x.shape[0], True)
    bound = project_keys(xt_s[...], w_t[0], b[0], mask, kt_out, vt_out)
    soft_part(qt, q[0], bound, kt_out, vt_out, s_s, o_s, m_s)
    finish_head(q[0], o1[0], m1[0], o_s[0], m_s[0], attt_out, inv_out, qb_out)


def attend_own(scalars, x, weights, packs, vec=None, target=None):
    heads = 4
    width, keys = x.shape if target is not None else x.shape[::-1]
    rows = keys if target is None else target.shape[0]
    flat = (1, WIDE, keys)
    head_outs = [
        ((heads, width, 3 * WIDE), bf16, None),
        ((heads, 3 * WIDE, width), bf16, None),
        ((heads, 8, WIDE), f32, None),
        ((heads,) + flat[1:], bf16, flat),
        ((heads,) + flat[1:], bf16, flat),
        ((heads, rows, WIDE), bf16, (1, rows, WIDE)),
        ((heads, WIDE, rows), bf16, (1, WIDE, rows)),
        ((heads, WIDE, rows), f32, (1, WIDE, rows)),
        ((heads, 1, rows), f32, (1, 1, rows)),
    ]
    scratch = [pltpu.VMEM((rows, keys), f32)]
    micros = 5 + keys / 210
    if target is not None:
        ins = scalars + full(x, vec, target, *weights, *packs)
        outs = [((width, keys), bf16, None), ((width, rows), bf16, None)] + head_outs
        return call(fwd_own_first, (heads,), ins, outs, scratch, micros)
    ins = scalars + full(x, *weights, *packs)
    scratch = [pltpu.VMEM((width, keys), bf16)] + scratch
    return call(fwd_own_second, (heads,), ins, head_outs, scratch, micros)


def attend_far(scalars, x, w_t, b, q, qt, o1, m1, vec=None):
    heads = w_t.shape[0]
    width, keys = x.shape if vec is not None else x.shape[::-1]
    rows = q.shape[1]
    flat = (1, WIDE, keys)
    head_ins = [
        (w_t, (1,) + w_t.shape[1:]),
        (b, (1,) + b.shape[1:]),
        (q, (1, rows, WIDE)),
        (qt, (1, WIDE, rows)),
        (o1, (1, WIDE, rows)),
        (m1, (1, 1, rows)),
    ]
    head_outs = [
        ((heads,) + flat[1:], bf16, flat),
        ((heads,) + flat[1:], bf16, flat),
        ((heads, WIDE, rows), bf16, (1, WIDE, rows)),
        ((heads, 1, rows), f32, (1, 1, rows)),
        ((heads, rows, WIDE), bf16, (1, rows, WIDE)),
    ]
    scratch = [
        pltpu.VMEM((rows, keys), f32),
        pltpu.VMEM((1, WIDE, rows), f32),
        pltpu.VMEM((1, 1, rows), f32),
    ]
    micros = 6 + keys / 210
    if vec is not None:
        ins = scalars + full(x, vec) + head_ins
        outs = [((width, keys), bf16, None)] + head_outs
        return call(fwd_far_first, (heads,), ins, outs, scratch, micros)
    scratch.append(pltpu.VMEM((width, keys), bf16))
    return call(fwd_far_second, (heads,), scalars + full(x) + head_ins, head_outs, scratch, micros)


def score_grads(qb, qt, do, dot_, kt, vt, dkv_s):
    q_all, qt_all, do_all, dot_all = qb[0], qt[0], do[0], dot_[0]
    parts = [slice(start, start + size) for start, size in chunks(kt.shape[2])]
    dq = scores = probs = None
    for i in range(len(parts) + 2):
        ahead = behind = None
        if i < len(parts):
            ahead = dot(q_all, kt[0, :, parts[i]]), dot(do_all, vt[0, :, parts[i]])
        if scores is not None:
            p = jnp.exp2(scores[0])
            behind = p.astype(bf16), (p * scores[1]).astype(bf16)
        if probs is not None:
            part = parts[i - 2]
            dkv_s[WIDE:, part] = dot(dot_all, probs[0]).astype(bf16)
            dkv_s[:WIDE, part] = (dot(qt_all, probs[1]) * LN2).astype(bf16)
            dq_part = dot_nt(kt[0, :, part], probs[1])
            dq = dq_part if dq is None else dq + dq_part
        scores, probs = ahead, behind
    return dq


def add_up(head, total, value):
    @pl.when(head == 0)
    def _():
        total[...] = value

    @pl.when(head > 0)
    def _():
        total[...] += value


def row_sums(columns):
    ones = jnp.ones((8, columns.shape[1]), bf16)
    return dot_nt(ones, columns)[0:1]


def times(a, x, flat):
    return dot_nt(a, x) if flat else dot(a, x)


def bwd_far(first, last, flat, qb, qt, do, dot_, kt, vt, w, x, *refs):
    if first:
        dxt_in = None
    else:
        dxt_in, refs = refs[0], refs[1:]
    dq_out, dw_out, dvs_out, dx_out, dxt_s, dkv_s = refs
    head = pl.program_id(0)
    dq_out[0] = score_grads(qb, qt, do, dot_, kt, vt, dkv_s)
    dxt = dot(w[0, :, WIDE:], dkv_s[...])
    dw_out[0, 0] = times(dkv_s[:HEAD_DIM, :], x[...], flat)
    dw_out[0, 1] = times(dkv_s[WIDE : WIDE + HEAD_DIM, :], x[...], flat)
    dvs_out[0] = jnp.broadcast_to(row_sums(dkv_s[WIDE:, :]), (8, WIDE))
    add_up(head, dxt_s, dxt if first else dxt + jnp.where(head == 0, 1.0, 0.0) * dxt_in[...])

    @pl.when(head == pl.num_programs(0) - 1)
    def _():
        if first and last:
            dx_out[...] = dxt_s[...].T.astype(bf16)
        else:
            dx_out[...] = dxt_s[...].astype(dx_out.dtype)


def near_head(
    flat, spot, head, step, qb, qt, do, dot_, kt, vt, w, x, xq, dq_far, dw_far, dvs_far,
    gmy_out, goth_out, sums_out, dkv_s,
):
    dqt = score_grads(qb, qt, do, dot_, kt, vt, dkv_s) + dq_far[0]
    dqt = (dqt * SCALE).astype(bf16)
    grads = (
        times(dqt[:HEAD_DIM, :], xq[...], flat),
        times(dkv_s[:HEAD_DIM, :], x[...], flat) + dw_far[0, 0],
        times(dkv_s[WIDE : WIDE + HEAD_DIM, :], x[...], flat) + dw_far[0, 1],
    )

    @pl.when(head % 2 == 0)
    def _():
        for j in range(3):
            gmy_out[0, j] = grads[j].astype(bf16)

    @pl.when(head % 2 == 1)
    def _():
        for j in range(3):
            goth_out[0, j] = grads[j].astype(bf16)

    @pl.when(step == 0)
    def _():
        sums_out[...] = jnp.zeros_like(sums_out)

    side = jnp.where(head < 2, spot[0], 1 - spot[0])
    piece = jnp.where(head % 2 == 0, spot[1], 1 - spot[1])
    quarter = 2 * side + piece
    put_row(sums_out, quarter, row_sums(dqt), WIDE)
    put_row(sums_out, 4 + quarter, row_sums(dkv_s[WIDE:, :]) + dvs_far[0, 0:1], WIDE)
    return dot(w[0, :, :WIDE], dqt), dot(w[0, :, WIDE:], dkv_s[...])


def bwd_own_second(
    spot, qb, qt, do, dot_, kt, vt, w, x, dq_far, dw_far, dvs_far,
    gmy_out, goth_out, sums_out, dx_out,
    dxt_s, dkv_s,
):
    head = pl.program_id(0)
    from_q, from_kv = near_head(
        False, spot, head, head, qb, qt, do, dot_, kt, vt, w, x, x, dq_far, dw_far, dvs_far,
        gmy_out, goth_out, sums_out, dkv_s,
    )
    add_up(head, dxt_s, from_q + from_kv)

    @pl.when(head == pl.num_programs(0) - 1)
    def _():
        dx_out[...] = dxt_s[...].T


def bwd_own_first(
    start, first, last, spot, qb, qt, do, dot_, kt, vt, w, x, xq, target, widen_grad,
    dq_far, dw_far, dvs_far, *refs,
):
    if not first:
        dxt_in, dxpt_in, sums_in, dxt_far, clip_t, vec = refs[:6]
        refs = refs[6:]
    gmy_out, goth_out, sums_out, refs = refs[0], refs[1], refs[2], refs[3:]
    if last:
        dx_out, dxt_s, dxpt_s, dkv_s = refs
    else:
        dxt_s, dxpt_s, dkv_s = refs
    step = pl.program_id(0)

    @pl.when(step == 0)
    def _():
        sums_out[...] = jnp.zeros_like(sums_out)
        if not first:
            sums_out[0:8] = sums_in[...]

    from_q, from_kv = near_head(
        True, spot, start + step, 1, qb, qt, do, dot_, kt, vt, w, x, xq, dq_far, dw_far, dvs_far,
        gmy_out, goth_out, sums_out, dkv_s,
    )

    @pl.when(step == 0)
    def _():
        dxt_s[...] = from_kv if first else from_kv + dxt_in[...]
        dxpt_s[...] = from_q + (widen_grad[...].T if first else dxpt_in[...])

    @pl.when(step > 0)
    def _():
        dxt_s[...] += from_kv
        dxpt_s[...] += from_q

    if not last:
        return

    @pl.when(step == pl.num_programs(0) - 1)
    def _():
        width = clip_t.shape[0]
        dxpt = dxpt_s[...].astype(bf16)
        gain = as_column(vec[NORM1 : NORM1 + 1, :width])
        dgain = jnp.zeros((width, 1), f32)
        dbeta = jnp.zeros((width, 1), f32)
        for at, size in chunks(clip_t.shape[1]):
            lane = lax.broadcasted_iota(jnp.int32, (target.shape[0], size), 1) + at
            hot = jnp.where(lane == target[...], 1.0, 0.0).astype(bf16)
            part = slice(at, at + size)
            grad = dxt_s[:, part] + dxt_far[:, part].astype(f32) + dot(dxpt, hot)
            xhat, rstd = norm_flat(clip_t[:, part].astype(f32))
            scaled = grad * gain
            dx_out[:, part] = rstd * (
                scaled
                - jnp.mean(scaled, axis=0, keepdims=True)
                - xhat * jnp.mean(scaled * xhat, axis=0, keepdims=True)
            )
            dgain = dgain + jnp.sum(grad * xhat, axis=1, keepdims=True)
            dbeta = dbeta + jnp.sum(grad, axis=1, keepdims=True)
        sums_out[8:9, :width] = as_row(dgain)
        sums_out[9:10, :width] = as_row(dbeta)


def back_ins(saved, parts, w, x):
    qb, qt, do, dot_ = saved
    kt, vt = parts
    rows, keys = qb.shape[1], kt.shape[2]
    flat = (1, WIDE, keys)
    rtall, rflat = (1, rows, WIDE), (1, WIDE, rows)
    return [
        (qb, rtall), (qt, rflat), (do, rtall), (dot_, rflat),
        (kt, flat), (vt, flat), (w, (1,) + w.shape[1:]), (x, None),
    ]


def attend_back_far(saved, parts, w, x, start, count, before=None):
    heads = w.shape[0]
    last = start + count == heads
    rows = saved[0].shape[1]
    keys, width = parts[0].shape[2], w.shape[1]
    ins = back_ins(saved, parts, w, x)
    if before is not None:
        ins += full(before)
    outs = [
        ((count, WIDE, rows), f32, (1, WIDE, rows)),
        ((count, 2, HEAD_DIM, width), f32, (1, 2, HEAD_DIM, width)),
        ((count, 8, WIDE), f32, (1, 8, WIDE)),
        ((keys, width), bf16, None)
        if count == heads
        else ((width, keys), bf16 if last else f32, None),
    ]
    scratch = [pltpu.VMEM((width, keys), f32), pltpu.VMEM((2 * WIDE, keys), bf16)]
    body = functools.partial(bwd_far, before is None, last, count != heads)
    return call(body, (count,), ins, outs, scratch, 14 if count == heads else 1, start)


def attend_back_own(spot, saved, parts, w, x, far):
    dq_far, dw_far, dvs_far = far
    heads = w.shape[0]
    rows = saved[0].shape[1]
    keys, width = parts[0].shape[2], w.shape[1]
    ins = [(spot, SMEM)] + back_ins(saved, parts, w, x)
    ins += [
        (dq_far, (1, WIDE, rows)),
        (dw_far, (1,) + dw_far.shape[1:]),
        (dvs_far, (1,) + dvs_far.shape[1:]),
    ]
    outs = [
        ((2, 3, HEAD_DIM, width), bf16, ("half", 1, 3, HEAD_DIM, width)),
        ((2, 3, HEAD_DIM, width), bf16, ("half", 1, 3, HEAD_DIM, width)),
        ((8, 3 * WIDE), f32, None),
        ((keys, width), f32, None),
    ]
    scratch = [pltpu.VMEM((width, keys), f32), pltpu.VMEM((2 * WIDE, keys), bf16)]
    return call(bwd_own_second, (heads,), ins, outs, scratch, 9 + keys / 105)


def attend_back_side(spot, saved, parts, w, x, far, pooled, start, before):
    dq_far, dw_far, dvs_far = far
    rows = saved[0].shape[1]
    keys, width = parts[0].shape[2], w.shape[1]
    whole = lambda a: (a, ("own", 1) + a.shape[1:])
    ins = [(spot, SMEM)] + back_ins(saved, parts, w, x) + full(*pooled)
    ins += [whole(dq_far), whole(dw_far), whole(dvs_far)]
    first = before is None
    if not first:
        ins += full(*before)
    outs = [
        ((1, 3, HEAD_DIM, width), bf16, None),
        ((1, 3, HEAD_DIM, width), bf16, None),
        ((8 if first else 16, 3 * WIDE), f32, None),
    ]
    scratch = [pltpu.VMEM((2 * WIDE, keys), bf16)]
    totals = [(width, keys), (width, rows)]
    if first:
        outs += [(shape, f32, None) for shape in totals]
    else:
        outs.append(((width, keys), f32, None))
        scratch = [pltpu.VMEM(shape, f32) for shape in totals] + scratch
    body = functools.partial(bwd_own_first, start, first, not first)
    return call(body, (2,), ins, outs, scratch, 20 if first else 0.3, start)


def pieces(spot):
    order = (spot[1], 1 - spot[1])
    return [(2 * side + p, side, p, order[p]) for side in (0, 1) for p in (0, 1)]


def put_row(ref, row, value, width):
    at = lax.broadcasted_iota(jnp.int32, (ref.shape[0], width), 0)
    ref[:, :width] = jnp.where(at == row, value, ref[:, :width])


def get_row(ref, row):
    at = lax.broadcasted_iota(jnp.int32, ref.shape, 0)
    return jnp.sum(jnp.where(at == row, ref[...], 0.0), axis=0, keepdims=True)


def absolute(spot, side, index):
    return 2 * (spot[0] if side == 0 else 1 - spot[0]) + index


def lanes_of(index, size):
    return pl.ds(pl.multiple_of(index * size, size), size)


def pad_heads(spot, wo_own, wo_far, wo_s):
    wo_s[...] = jnp.zeros_like(wo_s)
    for place, side, _, index in pieces(spot):
        wo_s[place, :HEAD_DIM, :] = (wo_own, wo_far)[side][lanes_of(index, HEAD_DIM), :]


def out_branch(attt, wo_s):
    total = None
    for head in range(attt.shape[0]):
        part = dot_tn(attt[head], wo_s[head])
        total = part if total is None else total + part
    return total


def sort_far(spot, mine, other, far_s):
    far_s[spot[1]] = mine[...]
    far_s[1 - spot[1]] = other[...]


def mid_first(
    spot, attt, wo_own, wo_far, xpt, widen, vec, up_own, down_own, up_far, down_far, pack_own, pack_far,
    mid_out, yt_out, act_out, slope_out, layer_out, x2_out, wo_s,
):
    pad_heads(spot, wo_own, wo_far, wo_s)
    size = up_own.shape[1] // 2
    branch = out_branch(attt, wo_s) + vec[OUT_B1 : OUT_B1 + 1]
    mid = (dot_tn(xpt[...], widen[...]) + vec[WIDEN_B : WIDEN_B + 1]) + branch
    mid_out[...] = mid
    xhat, _ = norm_stats(mid)
    y = (xhat * vec[MLP1 : MLP1 + 1] + vec[MLP1 + 1 : MLP1 + 2]).astype(bf16)
    yt_out[...] = flip(y)
    feed = None
    for place, side, _, index in pieces(spot):
        lanes = lanes_of(index, size)
        up = (up_own, up_far)[side][:, lanes]
        down = (down_own, down_far)[side][lanes, :]
        hidden = dot(y, up) + (pack_own, pack_far)[side][0:1, lanes]
        act, slope = gelu_both(hidden)
        act = act.astype(bf16)
        act_out[:, place * size : (place + 1) * size] = act
        slope_out[:, place * size : (place + 1) * size] = slope.astype(bf16)
        part = dot(act, down)
        feed = part if feed is None else feed + part
    layer = mid + feed + vec[DOWN_B1 : DOWN_B1 + 1]
    layer_out[...] = layer
    xhat, _ = norm_stats(layer)
    x2_out[...] = (xhat * vec[NORM2 : NORM2 + 1] + vec[NORM2 + 1 : NORM2 + 2]).astype(bf16)


def branch_back(gatt, attt, inv, wo_s, do_out, dot_out, g_outs, at):
    gatt_t = flip(gatt)
    for head in range(attt.shape[0]):
        do_t = dot(wo_s[head], gatt_t).astype(bf16).astype(f32)
        inner = jnp.sum(do_t * attt[head].astype(f32), axis=0, keepdims=True)
        scale = inv[head]
        do_t = do_t * scale
        row = lax.broadcasted_iota(jnp.int32, do_t.shape, 0)
        for offset, part in enumerate(three_parts(-inner * scale)):
            do_t = jnp.where(row == HEAD_DIM + offset, part, do_t)
        dot_out[head] = do_t.astype(bf16)
        do_out[head] = do_t.T.astype(bf16)
        grad = dot(attt[head, :HEAD_DIM, :], gatt).astype(bf16)
        g_outs[head % 2][head // 2, at : at + HEAD_DIM, :] = grad


def mid_second(
    spot, attt, inv, wo_own, wo_far, layer1, vec, up_own, down_own, mine, other,
    pack_own, pack_far, cot,
    y_out, dmid_out, do_out, dot_out, gmy_out, goth_out, small_out, wo_s, far_s,
):
    pad_heads(spot, wo_own, wo_far, wo_s)
    sort_far(spot, mine, other, far_s)
    size = up_own.shape[1] // 2
    width = cot.shape[1]
    g_outs = (gmy_out, goth_out)
    small_out[...] = jnp.zeros_like(small_out)
    mid = layer1[...] + (out_branch(attt, wo_s) + vec[OUT_B2 : OUT_B2 + 1])
    xhat, rstd = norm_stats(mid)
    gain = vec[MLP2 : MLP2 + 1]
    y = (xhat * gain + vec[MLP2 + 1 : MLP2 + 2]).astype(bf16)
    yt = flip(y)
    g_low = cot[...]
    g = g_low.astype(f32)
    gt = flip(g_low)
    feed = None
    dy = None
    for place, side, p, index in pieces(spot):
        lanes = lanes_of(index, size)
        up = (up_own, far_s.at[0])[side][:, lanes]
        down = (down_own, far_s.at[1])[side][:, lanes]
        hidden = dot(y, up) + (pack_own, pack_far)[side][1:2, lanes]
        act, slope = gelu_both(hidden)
        act = act.astype(bf16)
        dhid = (dot(g_low, down) * slope).astype(bf16)
        part = dot_nt(act, down)
        feed = part if feed is None else feed + part
        part = dot_nt(dhid, up)
        dy = part if dy is None else dy + part
        g_outs[p][side, :width, :] = dot(yt, dhid).astype(bf16)
        g_outs[p][side, width : 2 * width, :] = dot(gt, act).astype(bf16)
        row = 4 + absolute(spot, side, index)
        put_row(small_out, row, jnp.sum(dhid.astype(f32), axis=0, keepdims=True), size)
    y_out[...] = (mid + feed + vec[DOWN_B2 : DOWN_B2 + 1]).astype(bf16)
    back, dgain, dbeta = norm_back(xhat, rstd, gain, dy)
    dmid = g + back
    dmid_out[...] = dmid
    small_out[0:1] = jnp.sum(g, axis=0, keepdims=True)
    small_out[1:2] = dgain
    small_out[2:3] = dbeta
    small_out[3:4] = jnp.sum(dmid, axis=0, keepdims=True)
    branch_back(dmid.astype(bf16), attt, inv, wo_s, do_out, dot_out, g_outs, 2 * width)


def mid_back(
    spot, dx_own, dx_far, layer1, vec, dmid2, act, slope, yt, mid,
    up_own, down_own, up_far, down_far, wo_own, wo_far, attt, inv, xpt, widen,
    do_out, dot_out, gmy_out, goth_out, wgrad_out, small_out, wo_s, widen_s,
):
    pad_heads(spot, wo_own, wo_far, wo_s)
    size = up_own.shape[1] // 2
    width = layer1.shape[1]
    g_outs = (gmy_out, goth_out)
    small_out[...] = jnp.zeros_like(small_out)
    xhat, rstd = norm_stats(layer1[...])
    back, dgain2, dbeta2 = norm_back(
        xhat, rstd, vec[NORM2 : NORM2 + 1], dx_own[...] + dx_far[...].astype(f32)
    )
    g = dmid2[...] + back
    g_low = g.astype(bf16)
    gt = flip(g_low)
    dy = None
    for place, side, p, index in pieces(spot):
        lanes = lanes_of(index, size)
        here = slice(place * size, (place + 1) * size)
        up = (up_own, up_far)[side][:, lanes]
        down = (down_own, down_far)[side][lanes, :]
        dhid = (dot_nt(g_low, down) * slope[:, here].astype(f32)).astype(bf16)
        part = dot_nt(dhid, up)
        dy = part if dy is None else dy + part
        g_outs[p][side, :width, :] = dot(yt[...], dhid).astype(bf16)
        g_outs[p][side, width : 2 * width, :] = dot(gt, act[:, here]).astype(bf16)
        row = 4 + absolute(spot, side, index)
        put_row(small_out, row, jnp.sum(dhid.astype(f32), axis=0, keepdims=True), size)
    xhat, rstd = norm_stats(mid[...])
    back, dgain, dbeta = norm_back(xhat, rstd, vec[MLP1 : MLP1 + 1], dy)
    dmid = g + back
    small_out[0:1] = jnp.sum(g, axis=0, keepdims=True)
    small_out[1:2] = dgain
    small_out[2:3] = dbeta
    small_out[3:4] = jnp.sum(dmid, axis=0, keepdims=True)
    small_out[8:9] = dgain2
    small_out[9:10] = dbeta2
    gatt = dmid.astype(bf16)
    branch_back(gatt, attt, inv, wo_s, do_out, dot_out, g_outs, 2 * width)
    widen_s[...] = dot(xpt[...], gatt)
    rows = widen_s.shape[0] // 4
    at = 2 * width + HEAD_DIM
    for place, side, p, index in pieces(spot):
        quarter = widen_s[lanes_of(absolute(spot, side, index), rows), :]
        g_outs[p][side, at : at + rows, :] = quarter.astype(bf16)
    wgrad_out[...] = dot_nt(gatt, widen[...])


def finish_mlp(spot, mine, other, *refs):
    if len(refs) == 3:
        widen_far, widen_out = None, None
        up_out, down_out, out_out = refs
    else:
        widen_far, up_out, down_out, out_out, widen_out = refs
    width = up_out.shape[0]
    size = up_out.shape[1] // 2
    for part, index in ((mine, spot[1]), (other, 1 - spot[1])):
        lanes = lanes_of(index, size)
        up_out[:, lanes] = part[:width, :].astype(f32)
        down_out[lanes, :] = part[width : 2 * width, :].astype(f32).T
        out_out[lanes_of(index, HEAD_DIM), :] = part[2 * width : 2 * width + HEAD_DIM, :].astype(f32)
    if widen_out is not None:
        rows = widen_out.shape[0] // 4
        at = 2 * width + HEAD_DIM
        for side in (0, 1):
            for p, index in ((0, spot[1]), (1, 1 - spot[1])):
                if side == 0:
                    value = (mine, other)[p][at : at + rows, :]
                else:
                    value = widen_far[p]
                widen_out[lanes_of(absolute(spot, side, index), rows), :] = value.astype(f32)


def finish_qkv(turned, spot, mine, other, out, both_s):
    for j in range(3):
        for part, index in ((mine, spot[1]), (other, 1 - spot[1])):
            both_s[lanes_of(index, HEAD_DIM), :] = part[j].astype(f32)
        out[j] = both_s[...].T if turned else both_s[...]


def finish_small(spot, small, *outs):
    (n1g, n1b, wb, qvb1, ob1, m1g, m1b, ub1, db1, n2g, n2b, qvb2, ob2, m2g, m2b, ub2, db2) = outs
    first = 2 * spot[0]

    def put(out, row):
        out[...] = small[row, : out.shape[0]]

    def put_layer(base, sums, ub, qvb):
        size = ub.shape[0] // 2
        for p in (0, 1):
            ub[p * size : (p + 1) * size] = get_row(small, base + 4 + first + p)[0]
            for j in (0, 1):
                row = get_row(small, sums + 4 * j + first + p)
                qvb[j : j + 1, p * HEAD_DIM : (p + 1) * HEAD_DIM] = row[:, :HEAD_DIM]

    put(db2, 0)
    put(m2g, 1)
    put(m2b, 2)
    put(ob2, 3)
    put(db1, 16)
    put(m1g, 17)
    put(m1b, 18)
    put(ob1, 19)
    put(wb, 19)
    put(n2g, 24)
    put(n2b, 25)
    put(n1g, 48)
    put(n1b, 49)
    put_layer(0, 32, ub2, qvb2)
    put_layer(16, 40, ub1, qvb1)


def swap(x):
    return lax.ppermute(x, "head", [(0, 1), (1, 0)])


def core_swap(x):
    return lax.ppermute(x, "core", [(0, 1), (1, 0)])


def add_low(a, b):
    return (a.astype(f32) + b.astype(f32)).astype(bf16)


def tie(later, dep):
    return lax.optimization_barrier((later, dep))


def exchange(x, axis, bit):
    other = lax.ppermute(x, axis, [(i, i ^ bit) for i in range(lax.axis_size(axis))])
    return (x.astype(f32) + other.astype(f32)).astype(x.dtype)


def exchange_bits(axis):
    bits = [1 << k for k in range((lax.axis_size(axis) - 1).bit_length())]
    return bits[1:] + bits[:1]


def shards(
    clip_in,
    frame_count,
    frame_mask,
    pool_index,
    first_norm_gain,
    first_norm_bias,
    first_widen_weight,
    first_widen_bias,
    first_qkv_weight,
    first_qv_bias,
    first_out_weight,
    first_out_bias,
    first_mlp_gain,
    first_mlp_bias,
    first_up_weight,
    first_up_bias,
    first_down_weight,
    first_down_bias,
    second_norm_gain,
    second_norm_bias,
    second_qkv_weight,
    second_qv_bias,
    second_out_weight,
    second_out_bias,
    second_mlp_gain,
    second_mlp_bias,
    second_up_weight,
    second_up_bias,
    second_down_weight,
    second_down_bias,
    cotangent,
):
    clip_t = clip_in[0].T
    cot = cotangent[0]
    side = lax.axis_index("head")
    spot = jnp.stack([side, lax.axis_index("core")]).astype(jnp.int32)
    scalars = [(spot, SMEM), (frame_count, SMEM), (frame_mask, SMEM)]
    place = (spot, SMEM)
    width1, keys1 = clip_t.shape
    rows, dim = cot.shape
    n_up = first_up_bias.shape[0]
    hidden = 2 * n_up
    heads = 4
    out_rows = 2 * dim + HEAD_DIM
    half_up = n_up // 2

    qkv1 = jnp.swapaxes(first_qkv_weight, 0, 1)
    qkv2 = jnp.transpose(second_qkv_weight, (1, 2, 0))
    qv_row = jnp.concatenate([first_qv_bias.reshape(-1), second_qv_bias.reshape(-1)])
    pack = jnp.stack([first_up_bias, second_up_bias, qv_row])
    far_qkv1 = swap(qkv1)
    far_pack = swap(pack)
    clip_send, (far_qkv1, far_pack) = tie(clip_t, (far_qkv1, far_pack))
    far_clip = swap(clip_send)
    down2 = second_down_weight.T
    first_core = lax.axis_index("core") == 0
    send2 = jnp.where(first_core, second_up_weight, down2)

    def wide(v):
        return jnp.pad(v, (0, dim - v.shape[0]))

    vec = jnp.stack(
        [
            wide(first_norm_gain), wide(first_norm_bias), first_widen_bias, first_out_bias,
            first_mlp_gain, first_mlp_bias, first_down_bias, second_norm_gain, second_norm_bias,
            second_out_bias, second_mlp_gain, second_mlp_bias, second_down_bias,
        ]
    )

    picks = lax.dynamic_slice_in_dim(pool_index[0], side * rows, rows, 0)
    token = jnp.arange(rows, dtype=jnp.int32)
    frame, cell = token // (SIDE * SIDE), token % (SIDE * SIDE)
    line = 2 * (cell // SIDE) + picks // 2
    column = 2 * (cell % SIDE) + picks % 2
    target = (frame * (4 * SIDE * SIDE) + line * (2 * SIDE) + column)[:, None]

    x1t, x1pt, w1, w1t, b1, kt1, vt1, q1, qt1, o1, m1 = attend_own(
        scalars, clip_t, (qkv1, far_qkv1), (pack, far_pack), vec, target
    )
    mlp1, m1 = tie((first_out_weight, first_up_weight, first_down_weight), m1)
    far_out1, far_up1, far_down1 = [swap(w) for w in mlp1]
    x1ft, kt1f, vt1f, attt1, inv1, qb1 = attend_far(
        scalars, far_clip, w1t, b1, q1, qt1, o1, m1, vec
    )
    late, attt1 = tie((qkv2, second_out_weight), attt1)
    far_qkv2, far_out2 = [swap(w) for w in late]
    send2, far_qkv2 = tie(send2, far_qkv2)
    mine2 = swap(send2)
    mid1, yt1, act1, slope1, layer1, x2 = call(
        mid_first,
        (),
        [place]
        + full(
            attt1, first_out_weight, far_out1, x1pt, first_widen_weight, vec,
            first_up_weight, first_down_weight, far_up1, far_down1, pack, far_pack,
        ),
        [
            ((rows, dim), f32, None),
            ((dim, rows), bf16, None),
            ((rows, hidden), bf16, None),
            ((rows, hidden), bf16, None),
            ((rows, dim), f32, None),
            ((rows, dim), bf16, None),
        ],
        [pltpu.VMEM((heads, WIDE, dim), bf16)],
        11,
    )

    x2f = swap(x2)
    w2, w2t, b2, kt2, vt2, q2, qt2, o2, m2 = attend_own(scalars, x2, (qkv2, far_qkv2), (pack, far_pack))
    far_out2, m2 = tie(far_out2, m2)
    kt2f, vt2f, attt2, inv2, qb2 = attend_far(scalars, x2f, w2t, b2, q2, qt2, o2, m2)
    mine2, attt2 = tie(mine2, attt2)
    other2 = core_swap(mine2)
    out, dmid2, do2, dot2, gmy2, goth2, small2 = call(
        mid_second,
        (),
        [place]
        + full(
            attt2, inv2, second_out_weight, far_out2, layer1, vec, second_up_weight, down2,
            mine2, other2, pack, far_pack, cot,
        ),
        [
            ((rows, dim), bf16, None),
            ((rows, dim), f32, None),
            ((heads, rows, WIDE), bf16, None),
            ((heads, WIDE, rows), bf16, None),
            ((2, out_rows, half_up), bf16, None),
            ((2, out_rows, half_up), bf16, None),
            ((16, dim), f32, None),
        ],
        [pltpu.VMEM((heads, WIDE, dim), bf16), pltpu.VMEM((2, dim, n_up), bf16)],
        18,
    )

    got_a = core_swap(goth2)
    saved2 = (qb2, qt2, do2, dot2)
    dq2f, dw2f, dvs2f, dx2_send = attend_back_far(saved2, (kt2f, vt2f), w2, x2f, 0, heads)
    dx2_far = swap(dx2_send)
    near_a, away_a = add_low(gmy2[0], got_a[0]), add_low(gmy2[1], got_a[1])
    (near_a, away_a), dq2f = tie((near_a, away_a), dq2f)
    hmy2, hoth2, sums2, dx2 = attend_back_own(
        spot, saved2, (kt2, vt2), w2, x2, (dq2f, dw2f, dvs2f)
    )
    (away_a, hoth2), dx2 = tie((away_a, hoth2), dx2)
    got_a2 = swap(away_a)
    got_h2 = core_swap(hoth2)

    widen_rows = width1 // 4
    do1, dot1, gmy1, goth1, wgrad, small1 = call(
        mid_back,
        (),
        [place]
        + full(
            dx2, dx2_far, layer1, vec, dmid2, act1, slope1, yt1, mid1,
            first_up_weight, first_down_weight, far_up1, far_down1,
            first_out_weight, far_out1, attt1, inv1, x1pt, first_widen_weight,
        ),
        [
            ((heads, rows, WIDE), bf16, None),
            ((heads, WIDE, rows), bf16, None),
            ((2, out_rows + widen_rows, half_up), bf16, None),
            ((2, out_rows + widen_rows, half_up), bf16, None),
            ((rows, width1), f32, None),
            ((16, dim), f32, None),
        ],
        [
            pltpu.VMEM((heads, WIDE, dim), bf16),
            pltpu.VMEM((width1, dim), f32),
        ],
        17,
    )
    near_h, away_h = add_low(hmy2[0], got_h2[0]), add_low(hmy2[1], got_h2[1])
    total_a = add_low(near_a, got_a2)
    (total_a, near_h, away_h, goth1), do1 = tie((total_a, near_h, away_h, goth1), do1)
    bits = exchange_bits("outer")
    next_a = exchange(total_a, "outer", bits[0])
    got_b = core_swap(goth1)
    got_h = swap(away_h)

    saved1 = (qb1, qt1, do1, dot1)
    two = heads // 2
    *own_far, dx1_part = attend_back_far(saved1, (kt1f, vt1f), w1, x1ft, 0, two)
    near_b, away_b = add_low(gmy1[0], got_b[0]), add_low(gmy1[1], got_b[1])
    total_h = add_low(near_h, got_h)
    (near_b, away_b, total_h, next_a), dx1_part = tie((near_b, away_b, total_h, next_a), dx1_part)
    got_b2 = swap(away_b)
    for bit in bits[2:]:
        next_a = exchange(next_a, "outer", bit)
    next_h = exchange(total_h, "outer", bits[1])
    *far_far, dx1_send = attend_back_far(saved1, (kt1f, vt1f), w1, x1ft, two, two, dx1_part)
    dx1_far = swap(dx1_send)
    total_b = add_low(near_b, got_b2)
    (next_a, total_b, next_h), far_far = tie((next_a, total_b, next_h), far_far)
    next_b = exchange(total_b, "outer", bits[0])
    for bit in bits[2:]:
        next_h = exchange(next_h, "outer", bit)
    next_a = exchange(next_a, "outer", bits[1])
    pooled = (x1pt, target, wgrad)
    gmy_f, goth_f, sums1f, *totals = attend_back_side(
        spot, saved1, (kt1, vt1), w1, x1t, far_far, pooled, two, None
    )
    (dx1_far, goth_f, total_a, next_b, next_h), own_far = tie(
        (dx1_far, goth_f, next_a, next_b, next_h), own_far
    )
    next_b = exchange(next_b, "outer", bits[1])
    next_h = exchange(next_h, "outer", bits[0])
    other_a = core_swap(total_a)
    got_cf = core_swap(goth_f)
    gmy_o, goth_o, sums1, grad_in = attend_back_side(
        spot, saved1, (kt1, vt1), w1, x1t, own_far, pooled, 0, (*totals, sums1f, dx1_far, clip_t, vec)
    )

    (total_b, total_h), goth_o = tie((next_b, next_h), goth_o)
    for bit in bits[2:]:
        total_b = exchange(total_b, "outer", bit)
    small = jnp.concatenate([small2, small1, sums2, sums1])
    got_co = core_swap(goth_o)
    got_c2 = swap(add_low(gmy_f[0], got_cf[0]))
    total_c = add_low(gmy_o[0], got_co[0])
    total_c, small = tie(add_low(total_c, got_c2), exchange(small, "core", 1))
    total_c, small = tie(exchange(total_c, "outer", bits[0]), exchange(small, "head", 1))
    other_h = core_swap(total_h)
    total_c = exchange(total_c, "outer", bits[1])
    small = exchange(small, "outer", bits[0])
    (total_c, small), (total_b, other_h) = tie((total_c, small), (total_b, other_h))
    other_b = core_swap(total_b)
    widen_far = swap(jnp.stack([total_b[out_rows:], other_b[out_rows:]]))
    for bit in bits[2:]:
        total_c = exchange(total_c, "outer", bit)
    small = exchange(small, "outer", bits[1])
    (total_c, small), widen_far = tie((total_c, small), widen_far)
    other_c = core_swap(total_c)
    for bit in bits[2:]:
        small = exchange(small, "outer", bit)

    def qkv_form(mine, other, turned):
        width = mine.shape[2]
        shape = (2 * HEAD_DIM, width)
        (grad,) = call(
            functools.partial(finish_qkv, turned),
            (),
            [place] + full(mine, other),
            [((3,) + (shape[::-1] if turned else shape), f32, None)],
            [pltpu.VMEM(shape, f32)],
            2,
        )
        return jnp.transpose(grad, (1, 0, 2) if turned else (2, 0, 1))

    mlp_outs = [
        ((dim, n_up), f32, None),
        ((n_up, dim), f32, None),
        ((2 * HEAD_DIM, dim), f32, None),
    ]
    gup2, gdn2, gout2 = call(
        finish_mlp, (), [place] + full(total_a, other_a), mlp_outs, [], 3
    )
    gup1, gdn1, gout1, gwiden = call(
        finish_mlp,
        (),
        [place] + full(total_b, other_b, widen_far),
        mlp_outs + [((width1, dim), f32, None)],
        [],
        3,
    )
    gqkv2 = qkv_form(total_h, other_h, False)
    gqkv1 = qkv_form(total_c, other_c, True)
    vector = ((dim,), f32, None)
    thin = ((width1,), f32, None)
    layer_vectors = [((2, 2 * HEAD_DIM), f32, None)] + [vector] * 3 + [((n_up,), f32, None), vector]
    (n1g, n1b, wb, qvb1, ob1, m1g, m1b, ub1, db1, n2g, n2b, qvb2, ob2, m2g, m2b, ub2, db2) = call(
        finish_small,
        (),
        [place] + full(small),
        [thin, thin, vector] + layer_vectors + [vector, vector] + layer_vectors,
        [],
        2,
    )
    return (
        out[None], grad_in.T[None],
        n1g, n1b, gwiden, wb, gqkv1, qvb1, gout1, ob1, m1g, m1b, gup1, ub1, gdn1, db1,
        n2g, n2b, gqkv2, qvb2, gout2, ob2, m2g, m2b, gup2, ub2, gdn2, db2,
    )


def solution(mesh):
    in_specs = (
        P(BATCH, "head", None),
        P(BATCH),
        P(BATCH, None),
        P(BATCH, None),
        P(),
        P(),
        P(),
        P(),
        P(None, None, "head"),
        P(None, "head"),
        P("head", None),
        P(),
        P(),
        P(),
        P(None, "head"),
        P("head"),
        P("head", None),
        P(),
        P(),
        P(),
        P(None, None, "head"),
        P(None, "head"),
        P("head", None),
        P(),
        P(),
        P(),
        P(None, "head"),
        P("head"),
        P("head", None),
        P(),
        P(BATCH, "head", None),
    )
    out_specs = (
        P(BATCH, "head", None),
        P(BATCH, "head", None),
        P(),
        P(),
        P(),
        P(),
        P(None, None, "head"),
        P(None, "head"),
        P("head", None),
        P(),
        P(),
        P(),
        P(None, "head"),
        P("head"),
        P("head", None),
        P(),
        P(),
        P(),
        P(None, None, "head"),
        P(None, "head"),
        P("head", None),
        P(),
        P(),
        P(),
        P(None, "head"),
        P("head"),
        P("head", None),
        P(),
    )
    outer = mesh.shape["batch"] // 2
    split = Mesh(
        mesh.devices.reshape(outer, 2, mesh.shape["head"]), ("outer", "core", "head")
    )
    return jax.shard_map(shards, mesh=split, in_specs=in_specs, out_specs=out_specs, check_vma=False)
```

```python
import functools

import jax
import jax.numpy as jnp
from jax import lax
from jax.experimental import pallas as pl
from jax.experimental.pallas import tpu as pltpu
from jax.sharding import Mesh, PartitionSpec as P

HEAD_DIM = 96
WIDE = 128
SIDE = 14
DEAD = -1e30
LOG2E = 1.4426950408889634
LN2 = 0.6931471805599453
SCALE = HEAD_DIM ** (-0.5)
EPS = 1e-06
CHUNK = 256
SAFE = 60.0
BATCH = ("outer", "core")

bf16 = jnp.bfloat16
f32 = jnp.float32


def dot(a, b):
    return jnp.dot(a, b, preferred_element_type=f32)


def dot_nt(a, b):
    return lax.dot_general(a, b, (((1,), (1,)), ((), ())), preferred_element_type=f32)


def eye(size):
    row = lax.broadcasted_iota(jnp.int32, (size, size), 0)
    return jnp.where(row == lax.broadcasted_iota(jnp.int32, (size, size), 1), 1.0, 0.0).astype(bf16)


def flip(a):
    return dot_nt(eye(a.shape[1]), a).astype(bf16)


def dot_tn(a, b):
    return lax.dot_general(a, b, (((0,), (0,)), ((), ())), preferred_element_type=f32)


def chunks(total, step=CHUNK):
    return [(start, min(step, total - start)) for start in range(0, total, step)]


def norm_stats(v):
    centered = v - jnp.mean(v, axis=-1, keepdims=True)
    rstd = lax.rsqrt(jnp.mean(centered * centered, axis=-1, keepdims=True) + EPS)
    return centered * rstd, rstd


def norm_back(xhat, rstd, gain, grad):
    scaled = grad * gain
    back = rstd * (
        scaled
        - jnp.mean(scaled, axis=-1, keepdims=True)
        - xhat * jnp.mean(scaled * xhat, axis=-1, keepdims=True)
    )
    return (
        back,
        jnp.sum(grad * xhat, axis=0, keepdims=True),
        jnp.sum(grad, axis=0, keepdims=True),
    )


def norm_flat(v):
    centered = v - jnp.mean(v, axis=0, keepdims=True)
    rstd = lax.rsqrt(jnp.mean(centered * centered, axis=0, keepdims=True) + EPS)
    return centered * rstd, rstd


def as_column(row):
    return jnp.broadcast_to(row, (WIDE, row.shape[1])).T[:, :1]


def as_row(column):
    return jnp.broadcast_to(column, (column.shape[0], WIDE)).T[:1]


def three_parts(v):
    high = v.astype(bf16).astype(f32)
    rest = v - high
    middle = rest.astype(bf16).astype(f32)
    return high, middle, rest - middle


def with_columns(block, first, column):
    lane = lax.broadcasted_iota(jnp.int32, block.shape, 1)
    for offset, part in enumerate(three_parts(column)):
        block = jnp.where(lane == first + offset, part, block)
    return block


def gelu_both(u):
    cdf = 0.5 + 0.5 * lax.erf(u * 0.7071067811865476)
    return u * cdf, cdf + u * (jnp.exp(-0.5 * u * u) * 0.3989422804014327)


NORM1, WIDEN_B, OUT_B1, MLP1, DOWN_B1, NORM2, OUT_B2, MLP2, DOWN_B2 = 0, 2, 3, 4, 6, 7, 9, 10, 12
SMEM = "smem"


def call(body, grid, ins, outs, scratch, micros, offset=0, megabytes=56):
    def spec(shape, block):
        if block == SMEM:
            return pl.BlockSpec(memory_space=pltpu.SMEM)
        if block is None:
            zeros = (0,) * len(shape)
            return pl.BlockSpec(tuple(shape), lambda *_: zeros)
        if block[0] == "own":
            rest = (0,) * (len(shape) - 1)
            return pl.BlockSpec(tuple(block[1:]), lambda i, *_: (i,) + rest)
        if block[0] == "half":
            rest = (0,) * (len(shape) - 1)
            return pl.BlockSpec(tuple(block[1:]), lambda i, *_: ((i + offset) // 2,) + rest)
        rest = (0,) * (len(shape) - 1)
        return pl.BlockSpec(tuple(block), lambda i, *_: (i + offset,) + rest)

    def out_spec(shape, block):
        if block is None or block[0] == "half":
            return spec(shape, block)
        rest = (0,) * (len(shape) - 1)
        return pl.BlockSpec(tuple(block), lambda i, *_: (i,) + rest)

    return pl.pallas_call(
        body,
        grid=grid,
        in_specs=[spec(a.shape, b) for a, b in ins],
        out_specs=[out_spec(s, b) for s, _, b in outs],
        out_shape=[jax.ShapeDtypeStruct(s, d) for s, d, _ in outs],
        scratch_shapes=scratch,
        cost_estimate=pl.CostEstimate(
            flops=int(micros * 1.15e9), transcendentals=0, bytes_accessed=int(micros * 3.69e6)
        ),
        compiler_params=pltpu.CompilerParams(
            dimension_semantics=("arbitrary",) * len(grid),
            vmem_limit_bytes=megabytes << 20,
        ),
    )(*[a for a, _ in ins])


def full(*arrays):
    return [(a, None) for a in arrays]


def dead_keys(spot, count, marks, keys, far):
    half = marks.shape[1] // 2
    each = keys // half
    first = (1 - spot[0] if far else spot[0]) * half
    lane = lax.broadcasted_iota(jnp.int32, (1, keys), 1)
    row = jnp.zeros((1, keys), f32)
    for f in range(half):
        dead = (first + f >= count[0]) | (marks[0, first + f] != 1)
        row = jnp.where((lane >= f * each) & (lane < (f + 1) * each), jnp.where(dead, DEAD, 0.0), row)
    return row


def head_forms(spot, w_own, w_far, pack_own, pack_far, layer, w_out, wt_out, b_out):
    first = spot[1] == 0
    filled = wt_out if layer else w_out
    filled[...] = jnp.zeros_like(filled)
    b_out[...] = jnp.zeros_like(b_out)
    for side, (w, pack) in enumerate(((w_own, pack_own), (w_far, pack_far))):
        for j in range(3):
            place = slice(j * WIDE, j * WIDE + HEAD_DIM)
            if layer:
                low, high = w[j, :HEAD_DIM].astype(f32), w[j, HEAD_DIM:].astype(f32)
                wt_out[2 * side, place] = jnp.where(first, low, high).astype(bf16)
                wt_out[2 * side + 1, place] = jnp.where(first, high, low).astype(bf16)
            else:
                low, high = w[j, :, :HEAD_DIM].astype(f32), w[j, :, HEAD_DIM:].astype(f32)
                w_out[2 * side, :, place] = jnp.where(first, low, high).astype(bf16)
                w_out[2 * side + 1, :, place] = jnp.where(first, high, low).astype(bf16)
        for j in range(2):
            start = (2 * layer + j) * 2 * HEAD_DIM
            low = pack[2:3, start : start + HEAD_DIM]
            high = pack[2:3, start + HEAD_DIM : start + 2 * HEAD_DIM]
            b_out[2 * side, j : j + 1, :HEAD_DIM] = jnp.where(first, low, high)
            b_out[2 * side + 1, j : j + 1, :HEAD_DIM] = jnp.where(first, high, low)
    for head in range(w_out.shape[0]):
        if layer:
            w_out[head] = flip(wt_out[head])
        else:
            wt_out[head] = flip(w_out[head])


def project_keys(x_t, w_t, b, mask, kt_out, vt_out):
    both = dot(w_t[WIDE:], x_t)
    k_t, v_t = both[:WIDE], both[WIDE:]
    key_bound = jnp.max(jnp.sum(k_t * k_t, axis=0, keepdims=True))
    row = lax.broadcasted_iota(jnp.int32, k_t.shape, 0)
    k_t = jnp.where(row == HEAD_DIM, mask, k_t)
    k_t = jnp.where((row > HEAD_DIM) & (row < HEAD_DIM + 4), 1.0, k_t)
    kt_out[0] = k_t.astype(bf16)
    column = as_column(b[1:2])
    row = lax.broadcasted_iota(jnp.int32, column.shape, 0)
    column = jnp.where((row >= HEAD_DIM) & (row < HEAD_DIM + 3), 1.0, column)
    vt_out[0] = (v_t + column).astype(bf16)
    return key_bound


def soft_part(q_t_ref, q, key_bound, kt_ref, vt_ref, s_ref, o_ref, m_ref):
    total = kt_ref.shape[2]
    q_wide = q_t_ref[0, :HEAD_DIM, :].astype(f32)
    bound = jnp.max(jnp.sum(q_wide * q_wide, axis=0, keepdims=True)) * key_bound
    safe = bound < SAFE * SAFE

    @pl.when(safe)
    def _():
        parts = [slice(start, start + size) for start, size in chunks(total)]
        out = s = p = None
        for i in range(len(parts) + 2):
            s_next = dot(q, kt_ref[0, :, parts[i]]) if i < len(parts) else None
            p_next = None if s is None else jnp.exp2(s).astype(bf16)
            if p is not None:
                o = dot_nt(vt_ref[0, :, parts[i - 2]], p)
                out = o if out is None else out + o
            s, p = s_next, p_next
        o_ref[0] = out
        m_ref[0] = jnp.zeros_like(m_ref[0])

    @pl.when(jnp.logical_not(safe))
    def _():
        peak = None
        for start, size in chunks(total):
            s = dot(q, kt_ref[0, :, start : start + size])
            s_ref[:, start : start + size] = s
            top = jnp.max(s, axis=1, keepdims=True)
            peak = top if peak is None else jnp.maximum(peak, top)
        out = None
        for start, size in chunks(total):
            part = slice(start, start + size)
            p = jnp.exp2(s_ref[:, part] - peak).astype(bf16)
            o = dot_nt(vt_ref[0, :, part], p)
            out = o if out is None else out + o
        o_ref[0] = out
        m_ref[0] = as_row(peak)


def queries(q, rows_t, w_t, b, q_out, qt_out):
    q = (q + b[0:1]) * (SCALE * LOG2E)
    lane = lax.broadcasted_iota(jnp.int32, q.shape, 1)
    q = jnp.where(lane == HEAD_DIM, 1.0, q).astype(bf16)
    q_out[0] = q
    qt_out[0] = ((dot(w_t[:WIDE], rows_t) + as_column(b[0:1])) * (SCALE * LOG2E)).astype(bf16)
    return q


def input_norm(clip_t, vec):
    width = clip_t.shape[0]
    xhat, _ = norm_flat(clip_t[...].astype(f32))
    gain, beta = vec[NORM1 : NORM1 + 1, :width], vec[NORM1 + 1 : NORM1 + 2, :width]
    return (xhat * as_column(gain) + as_column(beta)).astype(bf16)


def fwd_own_first(
    spot, count, marks, clip_t, vec, target, w_own, w_far, pack_own, pack_far,
    xt_out, xpt_out, w_out, wt_out, b_out, kt_out, vt_out, q_out, qt_out, o_out, m_out,
    s_s,
):
    head = pl.program_id(0)

    @pl.when(head == 0)
    def _():
        head_forms(spot, w_own, w_far, pack_own, pack_far, 0, w_out, wt_out, b_out)
        xt_out[...] = input_norm(clip_t, vec)
        picked = None
        for start, size in chunks(clip_t.shape[1], 2 * CHUNK):
            lane = lax.broadcasted_iota(jnp.int32, (target.shape[0], size), 1) + start
            hot = jnp.where(lane == target[...], 1.0, 0.0).astype(bf16)
            part = dot_nt(xt_out[:, start : start + size], hot)
            picked = part if picked is None else picked + part
        xpt_out[...] = picked.astype(bf16)

    mask = dead_keys(spot, count, marks, clip_t.shape[1], False)
    w_t, b = wt_out[head], b_out[head]
    bound = project_keys(xt_out[...], w_t, b, mask, kt_out, vt_out)
    q = dot_tn(xpt_out[...], w_out[head, :, :WIDE])
    q = queries(q, xpt_out[...], w_t, b, q_out, qt_out)
    soft_part(qt_out, q, bound, kt_out, vt_out, s_s, o_out, m_out)


def fwd_own_second(
    spot, count, marks, x, w_own, w_far, pack_own, pack_far,
    w_out, wt_out, b_out, kt_out, vt_out, q_out, qt_out, o_out, m_out,
    xt_s, s_s,
):
    head = pl.program_id(0)

    @pl.when(head == 0)
    def _():
        head_forms(spot, w_own, w_far, pack_own, pack_far, 1, w_out, wt_out, b_out)
        xt_s[...] = flip(x[...])

    mask = dead_keys(spot, count, marks, x.shape[0], False)
    w_t, b = wt_out[head], b_out[head]
    bound = project_keys(xt_s[...], w_t, b, mask, kt_out, vt_out)
    q = queries(dot(x[...], w_out[head, :, :WIDE]), xt_s[...], w_t, b, q_out, qt_out)
    soft_part(qt_out, q, bound, kt_out, vt_out, s_s, o_out, m_out)


def finish_head(q, o1, m1, o2, m2, attt_out, inv_out, qb_out):
    peak = jnp.maximum(m1, m2)
    o = o1 * jnp.exp2(m1 - peak) + o2 * jnp.exp2(m2 - peak)
    inv = 1.0 / o[HEAD_DIM : HEAD_DIM + 1]
    attt_out[0] = (o * inv).astype(bf16)
    inv_out[0] = inv
    qb_out[0] = q

    @pl.when(jnp.max(jnp.abs(peak)) > 0.0)
    def _():
        qb_out[0] = with_columns(q.astype(f32), HEAD_DIM + 1, -as_column(peak)).astype(bf16)


def fwd_far_first(
    spot, count, marks, clip_t, vec, w_t, b, q, qt, o1, m1,
    xt_out, kt_out, vt_out, attt_out, inv_out, qb_out,
    s_s, o_s, m_s,
):
    @pl.when(pl.program_id(0) == 0)
    def _():
        xt_out[...] = input_norm(clip_t, vec)

    mask = dead_keys(spot, count, marks, clip_t.shape[1], True)
    bound = project_keys(xt_out[...], w_t[0], b[0], mask, kt_out, vt_out)
    soft_part(qt, q[0], bound, kt_out, vt_out, s_s, o_s, m_s)
    finish_head(q[0], o1[0], m1[0], o_s[0], m_s[0], attt_out, inv_out, qb_out)


def fwd_far_second(
    spot, count, marks, x, w_t, b, q, qt, o1, m1,
    kt_out, vt_out, attt_out, inv_out, qb_out,
    s_s, o_s, m_s, xt_s,
):
    @pl.when(pl.program_id(0) == 0)
    def _():
        xt_s[...] = flip(x[...])

    mask = dead_keys(spot, count, marks, x.shape[0], True)
    bound = project_keys(xt_s[...], w_t[0], b[0], mask, kt_out, vt_out)
    soft_part(qt, q[0], bound, kt_out, vt_out, s_s, o_s, m_s)
    finish_head(q[0], o1[0], m1[0], o_s[0], m_s[0], attt_out, inv_out, qb_out)


def attend_own(scalars, x, weights, packs, vec=None, target=None):
    heads = 4
    width, keys = x.shape if target is not None else x.shape[::-1]
    rows = keys if target is None else target.shape[0]
    flat = (1, WIDE, keys)
    head_outs = [
        ((heads, width, 3 * WIDE), bf16, None),
        ((heads, 3 * WIDE, width), bf16, None),
        ((heads, 8, WIDE), f32, None),
        ((heads,) + flat[1:], bf16, flat),
        ((heads,) + flat[1:], bf16, flat),
        ((heads, rows, WIDE), bf16, (1, rows, WIDE)),
        ((heads, WIDE, rows), bf16, (1, WIDE, rows)),
        ((heads, WIDE, rows), f32, (1, WIDE, rows)),
        ((heads, 1, rows), f32, (1, 1, rows)),
    ]
    scratch = [pltpu.VMEM((rows, keys), f32)]
    micros = 5 + keys / 210
    if target is not None:
        ins = scalars + full(x, vec, target, *weights, *packs)
        outs = [((width, keys), bf16, None), ((width, rows), bf16, None)] + head_outs
        return call(fwd_own_first, (heads,), ins, outs, scratch, micros)
    ins = scalars + full(x, *weights, *packs)
    scratch = [pltpu.VMEM((width, keys), bf16)] + scratch
    return call(fwd_own_second, (heads,), ins, head_outs, scratch, micros)


def attend_far(scalars, x, w_t, b, q, qt, o1, m1, vec=None):
    heads = w_t.shape[0]
    width, keys = x.shape if vec is not None else x.shape[::-1]
    rows = q.shape[1]
    flat = (1, WIDE, keys)
    head_ins = [
        (w_t, (1,) + w_t.shape[1:]),
        (b, (1,) + b.shape[1:]),
        (q, (1, rows, WIDE)),
        (qt, (1, WIDE, rows)),
        (o1, (1, WIDE, rows)),
        (m1, (1, 1, rows)),
    ]
    head_outs = [
        ((heads,) + flat[1:], bf16, flat),
        ((heads,) + flat[1:], bf16, flat),
        ((heads, WIDE, rows), bf16, (1, WIDE, rows)),
        ((heads, 1, rows), f32, (1, 1, rows)),
        ((heads, rows, WIDE), bf16, (1, rows, WIDE)),
    ]
    scratch = [
        pltpu.VMEM((rows, keys), f32),
        pltpu.VMEM((1, WIDE, rows), f32),
        pltpu.VMEM((1, 1, rows), f32),
    ]
    micros = 6 + keys / 210
    if vec is not None:
        ins = scalars + full(x, vec) + head_ins
        outs = [((width, keys), bf16, None)] + head_outs
        return call(fwd_far_first, (heads,), ins, outs, scratch, micros)
    scratch.append(pltpu.VMEM((width, keys), bf16))
    return call(fwd_far_second, (heads,), scalars + full(x) + head_ins, head_outs, scratch, micros)


def score_grads(qb, qt, do, dot_, kt, vt, dkv_s):
    q_all, qt_all, do_all, dot_all = qb[0], qt[0], do[0], dot_[0]
    parts = [slice(start, start + size) for start, size in chunks(kt.shape[2])]
    dq = scores = probs = None
    for i in range(len(parts) + 2):
        ahead = behind = None
        if i < len(parts):
            ahead = dot(q_all, kt[0, :, parts[i]]), dot(do_all, vt[0, :, parts[i]])
        if scores is not None:
            p = jnp.exp2(scores[0])
            behind = p.astype(bf16), (p * scores[1]).astype(bf16)
        if probs is not None:
            part = parts[i - 2]
            dkv_s[WIDE:, part] = dot(dot_all, probs[0]).astype(bf16)
            dkv_s[:WIDE, part] = (dot(qt_all, probs[1]) * LN2).astype(bf16)
            dq_part = dot_nt(kt[0, :, part], probs[1])
            dq = dq_part if dq is None else dq + dq_part
        scores, probs = ahead, behind
    return dq


def add_up(head, total, value):
    @pl.when(head == 0)
    def _():
        total[...] = value

    @pl.when(head > 0)
    def _():
        total[...] += value


def row_sums(columns):
    ones = jnp.ones((8, columns.shape[1]), bf16)
    return dot_nt(ones, columns)[0:1]


def times(a, x, flat):
    return dot_nt(a, x) if flat else dot(a, x)


def bwd_far(first, last, flat, qb, qt, do, dot_, kt, vt, w, x, *refs):
    if first:
        dxt_in = None
    else:
        dxt_in, refs = refs[0], refs[1:]
    dq_out, dw_out, dvs_out, dx_out, dxt_s, dkv_s = refs
    head = pl.program_id(0)
    dq_out[0] = score_grads(qb, qt, do, dot_, kt, vt, dkv_s)
    dxt = dot(w[0, :, WIDE:], dkv_s[...])
    dw_out[0, 0] = times(dkv_s[:HEAD_DIM, :], x[...], flat)
    dw_out[0, 1] = times(dkv_s[WIDE : WIDE + HEAD_DIM, :], x[...], flat)
    dvs_out[0] = jnp.broadcast_to(row_sums(dkv_s[WIDE:, :]), (8, WIDE))
    add_up(head, dxt_s, dxt if first else dxt + jnp.where(head == 0, 1.0, 0.0) * dxt_in[...])

    @pl.when(head == pl.num_programs(0) - 1)
    def _():
        if first and last:
            dx_out[...] = dxt_s[...].T.astype(bf16)
        else:
            dx_out[...] = dxt_s[...].astype(dx_out.dtype)


def near_head(
    flat, spot, head, step, qb, qt, do, dot_, kt, vt, w, x, xq, dq_far, dw_far, dvs_far,
    gmy_out, goth_out, sums_out, dkv_s,
):
    dqt = score_grads(qb, qt, do, dot_, kt, vt, dkv_s) + dq_far[0]
    dqt = (dqt * SCALE).astype(bf16)
    grads = (
        times(dqt[:HEAD_DIM, :], xq[...], flat),
        times(dkv_s[:HEAD_DIM, :], x[...], flat) + dw_far[0, 0],
        times(dkv_s[WIDE : WIDE + HEAD_DIM, :], x[...], flat) + dw_far[0, 1],
    )

    @pl.when(head % 2 == 0)
    def _():
        for j in range(3):
            gmy_out[0, j] = grads[j].astype(bf16)

    @pl.when(head % 2 == 1)
    def _():
        for j in range(3):
            goth_out[0, j] = grads[j].astype(bf16)

    @pl.when(step == 0)
    def _():
        sums_out[...] = jnp.zeros_like(sums_out)

    side = jnp.where(head < 2, spot[0], 1 - spot[0])
    piece = jnp.where(head % 2 == 0, spot[1], 1 - spot[1])
    quarter = 2 * side + piece
    put_row(sums_out, quarter, row_sums(dqt), WIDE)
    put_row(sums_out, 4 + quarter, row_sums(dkv_s[WIDE:, :]) + dvs_far[0, 0:1], WIDE)
    return dot(w[0, :, :WIDE], dqt), dot(w[0, :, WIDE:], dkv_s[...])


def bwd_own_second(
    spot, qb, qt, do, dot_, kt, vt, w, x, dq_far, dw_far, dvs_far,
    gmy_out, goth_out, sums_out, dx_out,
    dxt_s, dkv_s,
):
    head = pl.program_id(0)
    from_q, from_kv = near_head(
        False, spot, head, head, qb, qt, do, dot_, kt, vt, w, x, x, dq_far, dw_far, dvs_far,
        gmy_out, goth_out, sums_out, dkv_s,
    )
    add_up(head, dxt_s, from_q + from_kv)

    @pl.when(head == pl.num_programs(0) - 1)
    def _():
        dx_out[...] = dxt_s[...].T


def bwd_own_first(
    start, first, last, spot, qb, qt, do, dot_, kt, vt, w, x, xq, target, widen_grad,
    dq_far, dw_far, dvs_far, *refs,
):
    if not first:
        dxt_in, dxpt_in, sums_in, dxt_far, clip_t, vec = refs[:6]
        refs = refs[6:]
    gmy_out, goth_out, sums_out, refs = refs[0], refs[1], refs[2], refs[3:]
    if last:
        dx_out, dxt_s, dxpt_s, dkv_s = refs
    else:
        dxt_s, dxpt_s, dkv_s = refs
    step = pl.program_id(0)

    @pl.when(step == 0)
    def _():
        sums_out[...] = jnp.zeros_like(sums_out)
        if not first:
            sums_out[0:8] = sums_in[...]

    from_q, from_kv = near_head(
        True, spot, start + step, 1, qb, qt, do, dot_, kt, vt, w, x, xq, dq_far, dw_far, dvs_far,
        gmy_out, goth_out, sums_out, dkv_s,
    )

    @pl.when(step == 0)
    def _():
        dxt_s[...] = from_kv if first else from_kv + dxt_in[...]
        dxpt_s[...] = from_q + (widen_grad[...].T if first else dxpt_in[...])

    @pl.when(step > 0)
    def _():
        dxt_s[...] += from_kv
        dxpt_s[...] += from_q

    if not last:
        return

    @pl.when(step == pl.num_programs(0) - 1)
    def _():
        width = clip_t.shape[0]
        dxpt = dxpt_s[...].astype(bf16)
        gain = as_column(vec[NORM1 : NORM1 + 1, :width])
        dgain = jnp.zeros((width, 1), f32)
        dbeta = jnp.zeros((width, 1), f32)
        for at, size in chunks(clip_t.shape[1], 2 * CHUNK):
            lane = lax.broadcasted_iota(jnp.int32, (target.shape[0], size), 1) + at
            hot = jnp.where(lane == target[...], 1.0, 0.0).astype(bf16)
            part = slice(at, at + size)
            grad = dxt_s[:, part] + dxt_far[:, part].astype(f32) + dot(dxpt, hot)
            xhat, rstd = norm_flat(clip_t[:, part].astype(f32))
            scaled = grad * gain
            dx_out[:, part] = rstd * (
                scaled
                - jnp.mean(scaled, axis=0, keepdims=True)
                - xhat * jnp.mean(scaled * xhat, axis=0, keepdims=True)
            )
            dgain = dgain + jnp.sum(grad * xhat, axis=1, keepdims=True)
            dbeta = dbeta + jnp.sum(grad, axis=1, keepdims=True)
        sums_out[8:9, :width] = as_row(dgain)
        sums_out[9:10, :width] = as_row(dbeta)


def back_ins(saved, parts, w, x):
    qb, qt, do, dot_ = saved
    kt, vt = parts
    rows, keys = qb.shape[1], kt.shape[2]
    flat = (1, WIDE, keys)
    rtall, rflat = (1, rows, WIDE), (1, WIDE, rows)
    return [
        (qb, rtall), (qt, rflat), (do, rtall), (dot_, rflat),
        (kt, flat), (vt, flat), (w, (1,) + w.shape[1:]), (x, None),
    ]


def attend_back_far(saved, parts, w, x, start, count, before=None):
    heads = w.shape[0]
    last = start + count == heads
    rows = saved[0].shape[1]
    keys, width = parts[0].shape[2], w.shape[1]
    ins = back_ins(saved, parts, w, x)
    if before is not None:
        ins += full(before)
    outs = [
        ((count, WIDE, rows), f32, (1, WIDE, rows)),
        ((count, 2, HEAD_DIM, width), f32, (1, 2, HEAD_DIM, width)),
        ((count, 8, WIDE), f32, (1, 8, WIDE)),
        ((keys, width), bf16, None)
        if count == heads
        else ((width, keys), bf16 if last else f32, None),
    ]
    scratch = [pltpu.VMEM((width, keys), f32), pltpu.VMEM((2 * WIDE, keys), bf16)]
    body = functools.partial(bwd_far, before is None, last, count != heads)
    return call(body, (count,), ins, outs, scratch, 14 if count == heads else 1, start)


def attend_back_own(spot, saved, parts, w, x, far):
    dq_far, dw_far, dvs_far = far
    heads = w.shape[0]
    rows = saved[0].shape[1]
    keys, width = parts[0].shape[2], w.shape[1]
    ins = [(spot, SMEM)] + back_ins(saved, parts, w, x)
    ins += [
        (dq_far, (1, WIDE, rows)),
        (dw_far, (1,) + dw_far.shape[1:]),
        (dvs_far, (1,) + dvs_far.shape[1:]),
    ]
    outs = [
        ((2, 3, HEAD_DIM, width), bf16, ("half", 1, 3, HEAD_DIM, width)),
        ((2, 3, HEAD_DIM, width), bf16, ("half", 1, 3, HEAD_DIM, width)),
        ((8, 3 * WIDE), f32, None),
        ((keys, width), f32, None),
    ]
    scratch = [pltpu.VMEM((width, keys), f32), pltpu.VMEM((2 * WIDE, keys), bf16)]
    return call(bwd_own_second, (heads,), ins, outs, scratch, 9 + keys / 105)


def attend_back_side(spot, saved, parts, w, x, far, pooled, start, before):
    dq_far, dw_far, dvs_far = far
    rows = saved[0].shape[1]
    keys, width = parts[0].shape[2], w.shape[1]
    whole = lambda a: (a, ("own", 1) + a.shape[1:])
    ins = [(spot, SMEM)] + back_ins(saved, parts, w, x) + full(*pooled)
    ins += [whole(dq_far), whole(dw_far), whole(dvs_far)]
    first = before is None
    if not first:
        ins += full(*before)
    outs = [
        ((1, 3, HEAD_DIM, width), bf16, None),
        ((1, 3, HEAD_DIM, width), bf16, None),
        ((8 if first else 16, 3 * WIDE), f32, None),
    ]
    scratch = [pltpu.VMEM((2 * WIDE, keys), bf16)]
    totals = [(width, keys), (width, rows)]
    if first:
        outs += [(shape, f32, None) for shape in totals]
    else:
        outs.append(((width, keys), f32, None))
        scratch = [pltpu.VMEM(shape, f32) for shape in totals] + scratch
    body = functools.partial(bwd_own_first, start, first, not first)
    return call(body, (2,), ins, outs, scratch, 20 if first else 0.3, start)


def pieces(spot):
    order = (spot[1], 1 - spot[1])
    return [(2 * side + p, side, p, order[p]) for side in (0, 1) for p in (0, 1)]


def put_row(ref, row, value, width):
    at = lax.broadcasted_iota(jnp.int32, (ref.shape[0], width), 0)
    ref[:, :width] = jnp.where(at == row, value, ref[:, :width])


def get_row(ref, row):
    at = lax.broadcasted_iota(jnp.int32, ref.shape, 0)
    return jnp.sum(jnp.where(at == row, ref[...], 0.0), axis=0, keepdims=True)


def absolute(spot, side, index):
    return 2 * (spot[0] if side == 0 else 1 - spot[0]) + index


def lanes_of(index, size):
    return pl.ds(pl.multiple_of(index * size, size), size)


def pad_heads(spot, wo_own, wo_far, wo_s):
    wo_s[...] = jnp.zeros_like(wo_s)
    for place, side, _, index in pieces(spot):
        wo_s[place, :HEAD_DIM, :] = (wo_own, wo_far)[side][lanes_of(index, HEAD_DIM), :]


def out_branch(attt, wo_s):
    total = None
    for head in range(attt.shape[0]):
        part = dot_tn(attt[head], wo_s[head])
        total = part if total is None else total + part
    return total


def sort_far(spot, mine, other, far_s):
    far_s[spot[1]] = mine[...]
    far_s[1 - spot[1]] = other[...]


def mid_first(
    spot, attt, wo_own, wo_far, xpt, widen, vec, up_own, down_own, up_far, down_far, pack_own, pack_far,
    mid_out, yt_out, act_out, slope_out, layer_out, x2_out, wo_s,
):
    pad_heads(spot, wo_own, wo_far, wo_s)
    size = up_own.shape[1] // 2
    branch = out_branch(attt, wo_s) + vec[OUT_B1 : OUT_B1 + 1]
    mid = (dot_tn(xpt[...], widen[...]) + vec[WIDEN_B : WIDEN_B + 1]) + branch
    mid_out[...] = mid
    xhat, _ = norm_stats(mid)
    y = (xhat * vec[MLP1 : MLP1 + 1] + vec[MLP1 + 1 : MLP1 + 2]).astype(bf16)
    yt_out[...] = flip(y)
    feed = ahead = None
    for step in pieces(spot) + [None]:
        hidden = None
        if step is not None:
            place, side, _, index = step
            lanes = lanes_of(index, size)
            hidden = dot(y, (up_own, up_far)[side][:, lanes])
            hidden = place, side, lanes, hidden + (pack_own, pack_far)[side][0:1, lanes]
        if ahead is not None:
            place, side, lanes, value = ahead
            act, slope = gelu_both(value)
            act = act.astype(bf16)
            act_out[:, place * size : (place + 1) * size] = act
            slope_out[:, place * size : (place + 1) * size] = slope.astype(bf16)
            part = dot(act, (down_own, down_far)[side][lanes, :])
            feed = part if feed is None else feed + part
        ahead = hidden
    layer = mid + feed + vec[DOWN_B1 : DOWN_B1 + 1]
    layer_out[...] = layer
    xhat, _ = norm_stats(layer)
    x2_out[...] = (xhat * vec[NORM2 : NORM2 + 1] + vec[NORM2 + 1 : NORM2 + 2]).astype(bf16)


def branch_back(gatt, attt, inv, wo_s, do_out, dot_out, g_outs, at):
    gatt_t = flip(gatt)
    for head in range(attt.shape[0]):
        do_t = dot(wo_s[head], gatt_t).astype(bf16).astype(f32)
        inner = jnp.sum(do_t * attt[head].astype(f32), axis=0, keepdims=True)
        scale = inv[head]
        do_t = do_t * scale
        row = lax.broadcasted_iota(jnp.int32, do_t.shape, 0)
        for offset, part in enumerate(three_parts(-inner * scale)):
            do_t = jnp.where(row == HEAD_DIM + offset, part, do_t)
        dot_out[head] = do_t.astype(bf16)
        do_out[head] = do_t.T.astype(bf16)
        grad = dot(attt[head, :HEAD_DIM, :], gatt).astype(bf16)
        g_outs[head % 2][head // 2, at : at + HEAD_DIM, :] = grad


def mid_second(
    spot, attt, inv, wo_own, wo_far, layer1, vec, up_own, down_own, mine, other,
    pack_own, pack_far, cot,
    y_out, dmid_out, do_out, dot_out, gmy_out, goth_out, small_out, wo_s, far_s,
):
    pad_heads(spot, wo_own, wo_far, wo_s)
    sort_far(spot, mine, other, far_s)
    size = up_own.shape[1] // 2
    width = cot.shape[1]
    g_outs = (gmy_out, goth_out)
    small_out[...] = jnp.zeros_like(small_out)
    mid = layer1[...] + (out_branch(attt, wo_s) + vec[OUT_B2 : OUT_B2 + 1])
    xhat, rstd = norm_stats(mid)
    gain = vec[MLP2 : MLP2 + 1]
    y = (xhat * gain + vec[MLP2 + 1 : MLP2 + 2]).astype(bf16)
    yt = flip(y)
    g_low = cot[...]
    g = g_low.astype(f32)
    gt = flip(g_low)
    feed = dy = ahead = None
    for step in pieces(spot) + [None]:
        values = None
        if step is not None:
            _, side, p, index = step
            lanes = lanes_of(index, size)
            hidden = dot(y, (up_own, far_s.at[0])[side][:, lanes])
            hidden = hidden + (pack_own, pack_far)[side][1:2, lanes]
            dact = dot(g_low, (down_own, far_s.at[1])[side][:, lanes])
            values = side, p, index, lanes, hidden, dact
        if ahead is not None:
            side, p, index, lanes, hidden, dact = ahead
            act, slope = gelu_both(hidden)
            act = act.astype(bf16)
            dhid = (dact * slope).astype(bf16)
            part = dot_nt(act, (down_own, far_s.at[1])[side][:, lanes])
            feed = part if feed is None else feed + part
            part = dot_nt(dhid, (up_own, far_s.at[0])[side][:, lanes])
            dy = part if dy is None else dy + part
            g_outs[p][side, :width, :] = dot(yt, dhid).astype(bf16)
            g_outs[p][side, width : 2 * width, :] = dot(gt, act).astype(bf16)
            row = 4 + absolute(spot, side, index)
            put_row(small_out, row, jnp.sum(dhid.astype(f32), axis=0, keepdims=True), size)
        ahead = values
    y_out[...] = (mid + feed + vec[DOWN_B2 : DOWN_B2 + 1]).astype(bf16)
    back, dgain, dbeta = norm_back(xhat, rstd, gain, dy)
    dmid = g + back
    dmid_out[...] = dmid
    small_out[0:1] = jnp.sum(g, axis=0, keepdims=True)
    small_out[1:2] = dgain
    small_out[2:3] = dbeta
    small_out[3:4] = jnp.sum(dmid, axis=0, keepdims=True)
    branch_back(dmid.astype(bf16), attt, inv, wo_s, do_out, dot_out, g_outs, 2 * width)


def mid_back(
    spot, dx_own, dx_far, layer1, vec, dmid2, act, slope, yt, mid,
    up_own, down_own, up_far, down_far, wo_own, wo_far, attt, inv, xpt, widen,
    do_out, dot_out, gmy_out, goth_out, wgrad_out, small_out, wo_s,
):
    pad_heads(spot, wo_own, wo_far, wo_s)
    size = up_own.shape[1] // 2
    width = layer1.shape[1]
    g_outs = (gmy_out, goth_out)
    small_out[...] = jnp.zeros_like(small_out)
    xhat, rstd = norm_stats(layer1[...])
    back, dgain2, dbeta2 = norm_back(
        xhat, rstd, vec[NORM2 : NORM2 + 1], dx_own[...] + dx_far[...].astype(f32)
    )
    g = dmid2[...] + back
    g_low = g.astype(bf16)
    gt = flip(g_low)
    dy = None
    for place, side, p, index in pieces(spot):
        lanes = lanes_of(index, size)
        here = slice(place * size, (place + 1) * size)
        up = (up_own, up_far)[side][:, lanes]
        down = (down_own, down_far)[side][lanes, :]
        dhid = (dot_nt(g_low, down) * slope[:, here].astype(f32)).astype(bf16)
        part = dot_nt(dhid, up)
        dy = part if dy is None else dy + part
        g_outs[p][side, :width, :] = dot(yt[...], dhid).astype(bf16)
        g_outs[p][side, width : 2 * width, :] = dot(gt, act[:, here]).astype(bf16)
        row = 4 + absolute(spot, side, index)
        put_row(small_out, row, jnp.sum(dhid.astype(f32), axis=0, keepdims=True), size)
    xhat, rstd = norm_stats(mid[...])
    back, dgain, dbeta = norm_back(xhat, rstd, vec[MLP1 : MLP1 + 1], dy)
    dmid = g + back
    small_out[0:1] = jnp.sum(g, axis=0, keepdims=True)
    small_out[1:2] = dgain
    small_out[2:3] = dbeta
    small_out[3:4] = jnp.sum(dmid, axis=0, keepdims=True)
    small_out[8:9] = dgain2
    small_out[9:10] = dbeta2
    gatt = dmid.astype(bf16)
    branch_back(gatt, attt, inv, wo_s, do_out, dot_out, g_outs, 2 * width)
    whole = dot(xpt[...], gatt).astype(bf16)
    for g_out in g_outs:
        for side in (0, 1):
            g_out[side, 2 * width + HEAD_DIM :, :] = whole
    wgrad_out[...] = dot_nt(gatt, widen[...])


def finish_mlp(spot, mine, other, up_out, down_out, out_out, *widen_out):
    width = up_out.shape[0]
    size = up_out.shape[1] // 2
    at = 2 * width + HEAD_DIM
    for part, index in ((mine, spot[1]), (other, 1 - spot[1])):
        lanes = lanes_of(index, size)
        up_out[:, lanes] = part[:width, :].astype(f32)
        down_out[lanes, :] = part[width : 2 * width, :].astype(f32).T
        out_out[lanes_of(index, HEAD_DIM), :] = part[2 * width : at, :].astype(f32)
    for out in widen_out:
        out[...] = mine[at:, :].astype(f32)


def finish_qkv(turned, spot, mine, other, out, both_s):
    for j in range(3):
        for part, index in ((mine, spot[1]), (other, 1 - spot[1])):
            both_s[lanes_of(index, HEAD_DIM), :] = part[j].astype(f32)
        out[j] = both_s[...].T if turned else both_s[...]


def finish_small(spot, small, *outs):
    (n1g, n1b, wb, qvb1, ob1, m1g, m1b, ub1, db1, n2g, n2b, qvb2, ob2, m2g, m2b, ub2, db2) = outs
    first = 2 * spot[0]

    def put(out, row):
        out[...] = small[row, : out.shape[0]]

    def put_layer(base, sums, ub, qvb):
        size = ub.shape[0] // 2
        for p in (0, 1):
            ub[p * size : (p + 1) * size] = get_row(small, base + 4 + first + p)[0]
            for j in (0, 1):
                row = get_row(small, sums + 4 * j + first + p)
                qvb[j : j + 1, p * HEAD_DIM : (p + 1) * HEAD_DIM] = row[:, :HEAD_DIM]

    put(db2, 0)
    put(m2g, 1)
    put(m2b, 2)
    put(ob2, 3)
    put(db1, 16)
    put(m1g, 17)
    put(m1b, 18)
    put(ob1, 19)
    put(wb, 19)
    put(n2g, 24)
    put(n2b, 25)
    put(n1g, 48)
    put(n1b, 49)
    put_layer(0, 32, ub2, qvb2)
    put_layer(16, 40, ub1, qvb1)


def swap(x):
    return lax.ppermute(x, "head", [(0, 1), (1, 0)])


def core_swap(x):
    return lax.ppermute(x, "core", [(0, 1), (1, 0)])


def add_low(a, b):
    return (a.astype(f32) + b.astype(f32)).astype(bf16)


def tie(later, dep):
    return lax.optimization_barrier((later, dep))


def exchange(x, axis, bit):
    other = lax.ppermute(x, axis, [(i, i ^ bit) for i in range(lax.axis_size(axis))])
    return (x.astype(f32) + other.astype(f32)).astype(x.dtype)


def exchange_bits(axis):
    bits = [1 << k for k in range((lax.axis_size(axis) - 1).bit_length())]
    return bits[1:] + bits[:1]


def shards(
    clip_in,
    frame_count,
    frame_mask,
    pool_index,
    first_norm_gain,
    first_norm_bias,
    first_widen_weight,
    first_widen_bias,
    first_qkv_weight,
    first_qv_bias,
    first_out_weight,
    first_out_bias,
    first_mlp_gain,
    first_mlp_bias,
    first_up_weight,
    first_up_bias,
    first_down_weight,
    first_down_bias,
    second_norm_gain,
    second_norm_bias,
    second_qkv_weight,
    second_qv_bias,
    second_out_weight,
    second_out_bias,
    second_mlp_gain,
    second_mlp_bias,
    second_up_weight,
    second_up_bias,
    second_down_weight,
    second_down_bias,
    cotangent,
):
    clip_t = clip_in[0].T
    cot = cotangent[0]
    side = lax.axis_index("head")
    spot = jnp.stack([side, lax.axis_index("core")]).astype(jnp.int32)
    scalars = [(spot, SMEM), (frame_count, SMEM), (frame_mask, SMEM)]
    place = (spot, SMEM)
    width1, keys1 = clip_t.shape
    rows, dim = cot.shape
    n_up = first_up_bias.shape[0]
    hidden = 2 * n_up
    heads = 4
    out_rows = 2 * dim + HEAD_DIM
    half_up = n_up // 2

    qkv1 = jnp.swapaxes(first_qkv_weight, 0, 1)
    qkv2 = jnp.transpose(second_qkv_weight, (1, 2, 0))
    qv_row = jnp.concatenate([first_qv_bias.reshape(-1), second_qv_bias.reshape(-1)])
    pack = jnp.stack([first_up_bias, second_up_bias, qv_row])
    far_qkv1 = swap(qkv1)
    far_pack = swap(pack)
    clip_send, (far_qkv1, far_pack) = tie(clip_t, (far_qkv1, far_pack))
    far_clip = swap(clip_send)
    first_core = lax.axis_index("core") == 0

    def wide(v):
        return jnp.pad(v, (0, dim - v.shape[0]))

    vec = jnp.stack(
        [
            wide(first_norm_gain), wide(first_norm_bias), first_widen_bias, first_out_bias,
            first_mlp_gain, first_mlp_bias, first_down_bias, second_norm_gain, second_norm_bias,
            second_out_bias, second_mlp_gain, second_mlp_bias, second_down_bias,
        ]
    )

    picks = lax.dynamic_slice_in_dim(pool_index[0], side * rows, rows, 0)
    token = jnp.arange(rows, dtype=jnp.int32)
    frame, cell = token // (SIDE * SIDE), token % (SIDE * SIDE)
    line = 2 * (cell // SIDE) + picks // 2
    column = 2 * (cell % SIDE) + picks % 2
    target = (frame * (4 * SIDE * SIDE) + line * (2 * SIDE) + column)[:, None]

    x1t, x1pt, w1, w1t, b1, kt1, vt1, q1, qt1, o1, m1 = attend_own(
        scalars, clip_t, (qkv1, far_qkv1), (pack, far_pack), vec, target
    )
    mlp1, m1 = tie((first_out_weight, first_up_weight, first_down_weight), m1)
    far_out1, far_up1, far_down1 = [swap(w) for w in mlp1]
    x1ft, kt1f, vt1f, attt1, inv1, qb1 = attend_far(
        scalars, far_clip, w1t, b1, q1, qt1, o1, m1, vec
    )
    (qkv2, out2, up2, down2), attt1 = tie(
        (qkv2, second_out_weight, second_up_weight, second_down_weight), attt1
    )
    far_qkv2, far_out2 = swap(qkv2), swap(out2)
    down2 = down2.T
    send2, (far_qkv2, far_out2) = tie(
        jnp.where(first_core, up2, down2), (far_qkv2, far_out2)
    )
    mine2 = swap(send2)
    mid1, yt1, act1, slope1, layer1, x2 = call(
        mid_first,
        (),
        [place]
        + full(
            attt1, first_out_weight, far_out1, x1pt, first_widen_weight, vec,
            first_up_weight, first_down_weight, far_up1, far_down1, pack, far_pack,
        ),
        [
            ((rows, dim), f32, None),
            ((dim, rows), bf16, None),
            ((rows, hidden), bf16, None),
            ((rows, hidden), bf16, None),
            ((rows, dim), f32, None),
            ((rows, dim), bf16, None),
        ],
        [pltpu.VMEM((heads, WIDE, dim), bf16)],
        11,
    )

    x2f = swap(x2)
    w2, w2t, b2, kt2, vt2, q2, qt2, o2, m2 = attend_own(scalars, x2, (qkv2, far_qkv2), (pack, far_pack))
    kt2f, vt2f, attt2, inv2, qb2 = attend_far(scalars, x2f, w2t, b2, q2, qt2, o2, m2)
    mine2, attt2 = tie(mine2, attt2)
    other2 = core_swap(mine2)
    out, dmid2, do2, dot2, gmy2, goth2, small2 = call(
        mid_second,
        (),
        [place]
        + full(
            attt2, inv2, second_out_weight, far_out2, layer1, vec, second_up_weight, down2,
            mine2, other2, pack, far_pack, cot,
        ),
        [
            ((rows, dim), bf16, None),
            ((rows, dim), f32, None),
            ((heads, rows, WIDE), bf16, None),
            ((heads, WIDE, rows), bf16, None),
            ((2, out_rows, half_up), bf16, None),
            ((2, out_rows, half_up), bf16, None),
            ((16, dim), f32, None),
        ],
        [pltpu.VMEM((heads, WIDE, dim), bf16), pltpu.VMEM((2, dim, n_up), bf16)],
        18,
    )

    got_a = core_swap(goth2)
    saved2 = (qb2, qt2, do2, dot2)
    dq2f, dw2f, dvs2f, dx2_send = attend_back_far(saved2, (kt2f, vt2f), w2, x2f, 0, heads)
    dx2_far = swap(dx2_send)
    near_a, away_a = add_low(gmy2[0], got_a[0]), add_low(gmy2[1], got_a[1])
    (near_a, away_a), dq2f = tie((near_a, away_a), dq2f)
    hmy2, hoth2, sums2, dx2 = attend_back_own(
        spot, saved2, (kt2, vt2), w2, x2, (dq2f, dw2f, dvs2f)
    )
    (away_a, hoth2), dx2 = tie((away_a, hoth2), dx2)
    got_a2 = swap(away_a)
    got_h2 = core_swap(hoth2)

    do1, dot1, gmy1, goth1, wgrad, small1 = call(
        mid_back,
        (),
        [place]
        + full(
            dx2, dx2_far, layer1, vec, dmid2, act1, slope1, yt1, mid1,
            first_up_weight, first_down_weight, far_up1, far_down1,
            first_out_weight, far_out1, attt1, inv1, x1pt, first_widen_weight,
        ),
        [
            ((heads, rows, WIDE), bf16, None),
            ((heads, WIDE, rows), bf16, None),
            ((2, out_rows + width1, half_up), bf16, None),
            ((2, out_rows + width1, half_up), bf16, None),
            ((rows, width1), f32, None),
            ((16, dim), f32, None),
        ],
        [pltpu.VMEM((heads, WIDE, dim), bf16)],
        17,
    )
    near_h, away_h = add_low(hmy2[0], got_h2[0]), add_low(hmy2[1], got_h2[1])
    total_a = add_low(near_a, got_a2)
    (total_a, near_h, away_h, goth1), do1 = tie((total_a, near_h, away_h, goth1), do1)
    bits = exchange_bits("outer")
    next_a = exchange(total_a, "outer", bits[0])
    got_b = core_swap(goth1)
    got_h = swap(away_h)

    saved1 = (qb1, qt1, do1, dot1)
    two = heads // 2
    *own_far, dx1_part = attend_back_far(saved1, (kt1f, vt1f), w1, x1ft, 0, two)
    near_b, away_b = add_low(gmy1[0], got_b[0]), add_low(gmy1[1], got_b[1])
    total_h = add_low(near_h, got_h)
    (near_b, away_b, total_h, next_a), dx1_part = tie((near_b, away_b, total_h, next_a), dx1_part)
    got_b2 = swap(away_b)
    for bit in bits[2:]:
        next_a = exchange(next_a, "outer", bit)
    next_h = exchange(total_h, "outer", bits[1])
    *far_far, dx1_send = attend_back_far(saved1, (kt1f, vt1f), w1, x1ft, two, two, dx1_part)
    dx1_far = swap(dx1_send)
    total_b = add_low(near_b, got_b2)
    (next_a, total_b, next_h), far_far = tie((next_a, total_b, next_h), far_far)
    next_b = exchange(total_b, "outer", bits[0])
    for bit in bits[2:]:
        next_h = exchange(next_h, "outer", bit)
    next_a = exchange(next_a, "outer", bits[1])
    pooled = (x1pt, target, wgrad)
    gmy_f, goth_f, sums1f, *totals = attend_back_side(
        spot, saved1, (kt1, vt1), w1, x1t, far_far, pooled, two, None
    )
    (dx1_far, goth_f, total_a, next_b, next_h), own_far = tie(
        (dx1_far, goth_f, next_a, next_b, next_h), own_far
    )
    next_b = exchange(next_b, "outer", bits[1])
    next_h = exchange(next_h, "outer", bits[0])
    other_a = core_swap(total_a)
    got_cf = core_swap(goth_f)
    gmy_o, goth_o, sums1, grad_in = attend_back_side(
        spot, saved1, (kt1, vt1), w1, x1t, own_far, pooled, 0, (*totals, sums1f, dx1_far, clip_t, vec)
    )

    (total_b, total_h, other_a), goth_o = tie((next_b, next_h, other_a), goth_o)
    for bit in bits[2:]:
        total_b = exchange(total_b, "outer", bit)
    small = jnp.concatenate([small2, small1, sums2, sums1])
    got_co = core_swap(goth_o)
    got_c2 = swap(add_low(gmy_f[0], got_cf[0]))
    total_c = add_low(gmy_o[0], got_co[0])
    total_c, small = tie(add_low(total_c, got_c2), exchange(small, "core", 1))
    total_c, small = tie(exchange(total_c, "outer", bits[0]), exchange(small, "head", 1))
    other_h = core_swap(total_h)
    total_c = exchange(total_c, "outer", bits[1])
    small = exchange(small, "outer", bits[0])
    (total_c, small), (total_b, other_h) = tie((total_c, small), (total_b, other_h))
    other_b = core_swap(total_b)
    for bit in bits[2:]:
        total_c = exchange(total_c, "outer", bit)
    small = exchange(small, "outer", bits[1])
    total_c, small = tie(total_c, small)
    other_c = core_swap(total_c)
    for bit in bits[2:]:
        small = exchange(small, "outer", bit)

    def qkv_form(mine, other, turned):
        width = mine.shape[2]
        shape = (2 * HEAD_DIM, width)
        (grad,) = call(
            functools.partial(finish_qkv, turned),
            (),
            [place] + full(mine, other),
            [((3,) + (shape[::-1] if turned else shape), f32, None)],
            [pltpu.VMEM(shape, f32)],
            2,
        )
        return jnp.transpose(grad, (1, 0, 2) if turned else (2, 0, 1))

    mlp_outs = [
        ((dim, n_up), f32, None),
        ((n_up, dim), f32, None),
        ((2 * HEAD_DIM, dim), f32, None),
    ]
    gup2, gdn2, gout2 = call(
        finish_mlp, (), [place] + full(total_a, other_a), mlp_outs, [], 3
    )
    gup1, gdn1, gout1, gwiden = call(
        finish_mlp,
        (),
        [place] + full(total_b, other_b),
        mlp_outs + [((width1, dim), f32, None)],
        [],
        3,
    )
    gqkv2 = qkv_form(total_h, other_h, False)
    gqkv1 = qkv_form(total_c, other_c, True)
    vector = ((dim,), f32, None)
    thin = ((width1,), f32, None)
    layer_vectors = [((2, 2 * HEAD_DIM), f32, None)] + [vector] * 3 + [((n_up,), f32, None), vector]
    (n1g, n1b, wb, qvb1, ob1, m1g, m1b, ub1, db1, n2g, n2b, qvb2, ob2, m2g, m2b, ub2, db2) = call(
        finish_small,
        (),
        [place] + full(small),
        [thin, thin, vector] + layer_vectors + [vector, vector] + layer_vectors,
        [],
        2,
    )
    return (
        out[None], grad_in.T[None],
        n1g, n1b, gwiden, wb, gqkv1, qvb1, gout1, ob1, m1g, m1b, gup1, ub1, gdn1, db1,
        n2g, n2b, gqkv2, qvb2, gout2, ob2, m2g, m2b, gup2, ub2, gdn2, db2,
    )


def solution(mesh):
    in_specs = (
        P(BATCH, "head", None),
        P(BATCH),
        P(BATCH, None),
        P(BATCH, None),
        P(),
        P(),
        P(),
        P(),
        P(None, None, "head"),
        P(None, "head"),
        P("head", None),
        P(),
        P(),
        P(),
        P(None, "head"),
        P("head"),
        P("head", None),
        P(),
        P(),
        P(),
        P(None, None, "head"),
        P(None, "head"),
        P("head", None),
        P(),
        P(),
        P(),
        P(None, "head"),
        P("head"),
        P("head", None),
        P(),
        P(BATCH, "head", None),
    )
    out_specs = (
        P(BATCH, "head", None),
        P(BATCH, "head", None),
        P(),
        P(),
        P(),
        P(),
        P(None, None, "head"),
        P(None, "head"),
        P("head", None),
        P(),
        P(),
        P(),
        P(None, "head"),
        P("head"),
        P("head", None),
        P(),
        P(),
        P(),
        P(None, None, "head"),
        P(None, "head"),
        P("head", None),
        P(),
        P(),
        P(),
        P(None, "head"),
        P("head"),
        P("head", None),
        P(),
    )
    outer = mesh.shape["batch"] // 2
    split = Mesh(
        mesh.devices.reshape(outer, 2, mesh.shape["head"]), ("outer", "core", "head")
    )
    return jax.shard_map(shards, mesh=split, in_specs=in_specs, out_specs=out_specs, check_vma=False)
```
